128 devices in a mesh: dp: 16 (over x, z_lo, core), tensor: 8 (over y, z_hi).
Axes of the slice: x: 4, y: 4, z: 4 (z_hi: 2, z_lo: 2; z = z_hi * 2 + z_lo), core: 2. Of those that a mesh axis runs over, the one named last changes fastest.
Arguments:
- tokens: bfloat16 [8192, 1024], P('dp'), may hold values from -6 to 6
- cotangent: bfloat16 [8192, 1024], P('dp'), may hold values from -6 to 6
- ln_gain: float32 [2, 2, 1024], replicated, may hold values from 0.5 to 1.5
- ln_bias: float32 [2, 2, 1024], replicated, may hold values from -2 to 2
- w_qkv: bfloat16 [2, 1024, 3, 1024], P(None, None, None, 'tensor'), may hold values from -0.1875 to 0.1875
- b_qkv: float32 [2, 3, 1024], P(None, None, 'tensor'), may hold values from -3 to 3
- w_out: bfloat16 [2, 1024, 1024], P(None, 'tensor'), may hold values from -1.5 to 1.5
- b_out: float32 [2, 1024], replicated, may hold values from -3 to 3
- w_in: bfloat16 [2, 1024, 4096], P(None, None, 'tensor'), may hold values from -0.1875 to 0.1875
- b_in: float32 [2, 4096], P(None, 'tensor'), may hold values from -3 to 3
- w_down: bfloat16 [2, 4096, 1024], P(None, 'tensor'), may hold values from -0.09375 to 0.09375
- b_down: float32 [2, 1024], replicated, may hold values from -3 to 3
Outputs:
- output: float32 [8192, 1024], P('dp')
- input_grad: float32 [8192, 1024], P('dp')
- grad_ln_gain: float32 [2, 2, 1024], replicated
- grad_ln_bias: float32 [2, 2, 1024], replicated
- grad_w_qkv: float32 [2, 1024, 3, 1024], P(None, 'dp', None, 'tensor')
- grad_b_qkv: float32 [2, 3, 1024], P(None, None, 'tensor')
- grad_w_out: float32 [2, 1024, 1024], P(None, 'tensor', 'dp')
- grad_b_out: float32 [2, 1024], replicated
- grad_w_in: float32 [2, 1024, 4096], P(None, 'dp', 'tensor')
- grad_b_in: float32 [2, 4096], P(None, 'tensor')
- grad_w_down: float32 [2, 4096, 1024], P(None, 'tensor', 'dp')
- grad_b_down: float32 [2, 1024], replicated
The draws below stay inside these ranges and needn't reach their ends.
All inputs are finite; a program needn't handle non-finite values.
Results may differ from the reference program's by a relative error of at most 0.015.
The reference program's roundings to bfloat16 on the way count: a program that leaves them out, or rounds other values in their place, can miss the bound.
Values may be sent and summed in bfloat16 or wider, within the bound.
A program may use at most 128 MiB of HBM per device.

```python
import jax
import jax.numpy as jnp
from jax import lax

D = 1024
HEADS = 16
HEAD_DIM = 64
ROT = 16
FF = 4096
SEQ = 2048
LAYERS = 2
TOKENS = 8192


def levels(stream_key, dims, cuts, least, largest):
    def one(axis_at, parts):
        steps = jax.random.uniform(jax.random.fold_in(jax.random.fold_in(stream_key, 6), axis_at), (parts,), jnp.float32, least / len(cuts), largest / len(cuts))
        return jnp.repeat(jnp.exp(steps), dims[axis_at] // parts).reshape((-1,) + (1,) * (len(dims) - axis_at - 1))

    factor_of = one(*cuts[0])
    for cut in cuts[1:]:
        factor_of = factor_of * one(*cut)
    return factor_of


def noise(rng, shape, width, limit, split=(), held_as=jnp.bfloat16):
    level = levels(rng, shape, split, -0.22, 0.18) if split else 1.0
    values = jax.random.normal(rng, shape, jnp.float32) * width * level
    return jnp.minimum(jnp.maximum(values, -limit), limit).astype(held_as)


def setup_inputs(seed: int = 0) -> dict:
    seeds = jax.random.split(jax.random.key(seed), 13)
    tokens = noise(seeds[0], (TOKENS, D), 1.0, 6.0, ((0, 16),))
    cotangent = noise(seeds[1], (TOKENS, D), 1.0, 6.0, ((0, 16),))
    ln_gain = jnp.clip(1.0 + 0.1 * jax.random.normal(seeds[2], (LAYERS, 2, D), jnp.float32), 0.5, 1.5)
    ln_bias = noise(seeds[3], (LAYERS, 2, D), 0.3, 2.0, (), jnp.float32)
    w_qkv = noise(seeds[4], (LAYERS, D, 3, D), D ** -0.5, 0.1875, ((3, 8),))
    b_qkv = noise(seeds[5], (LAYERS, 3, D), 0.5, 3.0, ((2, 8),), jnp.float32)
    w_out = noise(seeds[6], (LAYERS, D, D), (D // 64) ** -0.5, 1.5, ((1, 8),))
    b_out = noise(seeds[7], (LAYERS, D), 0.5, 3.0, (), jnp.float32)
    w_in = noise(seeds[8], (LAYERS, D, FF), D ** -0.5, 0.1875, ((2, 8),))
    b_in = noise(seeds[9], (LAYERS, FF), 0.5, 3.0, ((1, 8),), jnp.float32)
    w_down = noise(seeds[10], (LAYERS, FF, D), FF ** -0.5, 0.09375, ((1, 8),))
    b_down = noise(seeds[11], (LAYERS, D), 0.5, 3.0, (), jnp.float32)
    return dict(tokens=tokens, cotangent=cotangent, ln_gain=ln_gain, ln_bias=ln_bias, w_qkv=w_qkv, b_qkv=b_qkv, w_out=w_out, b_out=b_out, w_in=w_in, b_in=b_in, w_down=w_down, b_down=b_down)


@jax.custom_vjp
def low(v):
    return lax.optimization_barrier(v.astype(jnp.bfloat16)).astype(jnp.float32)

@jax.custom_vjp
def low_back(v):
    return v

def low_keep(v):
    return (low(v), None)

def low_pass(kept, grad):
    return (grad,)

def back_keep(v):
    return (v, None)

def back_low(kept, grad):
    return (low(grad),)
low.defvjp(low_keep, low_pass)
low_back.defvjp(back_keep, back_low)
highest = lax.Precision.HIGHEST

def layer_norms(stream, gains, biases):
    center = stream - lax.optimization_barrier(jnp.mean(stream, axis=-1, keepdims=True))
    spread = lax.optimization_barrier(jnp.mean(center * center, axis=-1, keepdims=True))
    normed = center * lax.rsqrt(spread + 1e-05)
    return normed[None] * gains[:, None, :] + biases[:, None, :]

def rope_tables(positions):
    exponent = jnp.arange(0, ROT, 2).astype(jnp.float32) / ROT
    inverse = 1.0 / 10000.0 ** exponent
    angles = positions[:, None] * inverse[None, :]
    return (jnp.cos(angles), jnp.sin(angles))

def rotate(values, cosine, sine):
    halfway = cosine.shape[-1]
    leading = values[..., :halfway]
    trailing = values[..., halfway:2 * halfway]
    cos_part = cosine[:, None, :]
    sin_part = sine[:, None, :]
    return jnp.concatenate([leading * cos_part - trailing * sin_part, trailing * cos_part + leading * sin_part, values[..., 2 * halfway:]], axis=-1)

def head_attention(queries, keys, values):
    length = queries.shape[0]
    block = min(512, length)
    count = length // block
    key_pos = jnp.arange(length).astype(jnp.int32)

    def one_block(pair):
        query_block, start = pair
        query_pos = start + jnp.arange(block).astype(jnp.int32)
        scores = low_back(jnp.einsum('qd,kd->qk', query_block, keys, precision=highest) * 0.125)
        scores = jnp.where(key_pos[None, :] <= query_pos[:, None], scores, -1e+30)
        probs = low(jax.nn.softmax(scores, axis=-1))
        return jnp.einsum('qk,kd->qd', probs, values, precision=highest)
    starts = jnp.arange(count).astype(jnp.int32) * block
    result = lax.map(jax.checkpoint(one_block), (queries.reshape(count, block, queries.shape[1]), starts))
    return result.reshape(length, queries.shape[1])

def head_task(triple):
    return head_attention(triple[0], triple[1], triple[2])

def split_sequences(values, count):
    return values.reshape(count, SEQ, HEADS, HEAD_DIM).transpose(0, 2, 1, 3).reshape(count * HEADS, SEQ, HEAD_DIM)

def forward(stream, ln_gain, ln_bias, w_qkv, b_qkv, w_out, b_out, w_in, b_in, w_down, b_down):
    length = stream.shape[0]
    seq_count = length // SEQ
    positions = (jnp.arange(length).astype(jnp.int32) % SEQ).astype(jnp.float32)
    cosine, sine = rope_tables(positions)
    for layer_index in range(LAYERS):
        normed = low(layer_norms(stream, ln_gain[layer_index], ln_bias[layer_index]))
        mixed = jnp.einsum('td,dcf->tcf', normed[0], w_qkv[layer_index], precision=highest) + b_qkv[layer_index][None]
        mixed = low_back(mixed)
        heads_q = low(rotate(mixed[:, 0].reshape(length, HEADS, HEAD_DIM), cosine, sine))
        heads_k = low(rotate(mixed[:, 1].reshape(length, HEADS, HEAD_DIM), cosine, sine))
        heads_v = low(mixed[:, 2].reshape(length, HEADS, HEAD_DIM))
        attended = lax.map(head_task, (split_sequences(heads_q, seq_count), split_sequences(heads_k, seq_count), split_sequences(heads_v, seq_count)))
        attended = attended.reshape(seq_count, HEADS, SEQ, HEAD_DIM).transpose(0, 2, 1, 3).reshape(length, D)
        attended = low(low_back(attended))
        hidden = low_back(jnp.dot(normed[1], w_in[layer_index], precision=highest) + b_in[layer_index])
        active = low(jax.nn.gelu(hidden, approximate=False))
        branch = jnp.dot(attended, w_out[layer_index], precision=highest) + b_out[layer_index]
        branch = branch + jnp.dot(active, w_down[layer_index], precision=highest) + b_down[layer_index]
        stream = stream + low_back(branch)
    return stream

def reference(tokens, cotangent, ln_gain, ln_bias, w_qkv, b_qkv, w_out, b_out, w_in, b_in, w_down, b_down):
    inputs = [tokens.astype(jnp.float32), ln_gain.astype(jnp.float32), ln_bias.astype(jnp.float32), w_qkv.astype(jnp.float32), b_qkv.astype(jnp.float32), w_out.astype(jnp.float32), b_out.astype(jnp.float32), w_in.astype(jnp.float32), b_in.astype(jnp.float32), w_down.astype(jnp.float32), b_down.astype(jnp.float32)]
    result, pullback = jax.vjp(forward, *inputs)
    grads = pullback(cotangent.astype(jnp.float32))
    return (result, grads[0], grads[1], grads[2], grads[3], grads[4], grads[5], grads[6], grads[7], grads[8], grads[9], grads[10])
```

```python
import functools

import jax
import jax.numpy as jnp
import numpy as np
from jax import lax
from jax.experimental import pallas as pl
from jax.experimental.pallas import tpu as pltpu
from jax.sharding import PartitionSpec as P

HEAD_DIM = 64
ROT = 16
SEQ = 2048
LAYERS = 2
EPS = 1e-05
F32 = jnp.float32
BF16 = jnp.bfloat16
MESH = pl.DeviceIdType.MESH
LANES = 128
QT = 256
KT = 256
MT = 256
ST = 32


def nn(a, b):
    return jnp.dot(a, b, preferred_element_type=F32)


def nt(a, b):
    return lax.dot_general(a, b, (((1,), (1,)), ((), ())), preferred_element_type=F32)


def rope_constants():
    half = ROT // 2
    exponent = np.arange(0, ROT, 2).astype(np.float32) / np.float32(ROT)
    inverse = (np.float32(1.0) / np.float32(10000.0) ** exponent).astype(np.float32)
    angles = np.arange(SEQ).astype(np.float32)[:, None] * inverse[None, :]
    cosine = np.ones((SEQ, LANES), np.float32)
    sine = np.zeros((SEQ, LANES), np.float32)
    for start in range(0, LANES, HEAD_DIM):
        cosine[:, start : start + half] = np.cos(angles)
        cosine[:, start + half : start + ROT] = np.cos(angles)
        sine[:, start : start + half] = -np.sin(angles)
        sine[:, start + half : start + ROT] = np.sin(angles)
    return cosine, sine


def rotate(values, cosine, sine):
    half = ROT // 2
    lane = lax.broadcasted_iota(jnp.int32, values.shape, 1)
    partner = jnp.where(
        lane % HEAD_DIM < half,
        pltpu.roll(values, LANES - half, 1),
        pltpu.roll(values, half, 1),
    )
    return values * cosine + partner * sine


def head_only(values, head):
    lane = lax.broadcasted_iota(jnp.int32, values.shape, 1)
    return jnp.where(lane // HEAD_DIM == head, values, jnp.zeros_like(values))


def rows_at(step, size):
    return pl.ds(pl.multiple_of(step * size, size), size)


def remote(src, dst, send_sem, recv_sem, **device):
    return pltpu.make_async_remote_copy(
        src_ref=src,
        dst_ref=dst,
        send_sem=send_sem,
        recv_sem=recv_sem,
        device_id=device,
        device_id_type=MESH,
    )


class Refs:
    pass


def step_kernel(nt_dev, nd, *refs):
    names = (
        "tok", "cot", "gain", "bias", "wqkv_h", "bqkv", "wout_h", "bout", "win_h", "bin",
        "wdown_h", "bdown", "cos_h", "sin_h", "x", "g", "ogain", "obias", "obqkv", "obout",
        "obin", "obdown", "oq", "oo", "oi", "od", "wqkv", "wout", "win", "wdown", "cosine",
        "sine", "xt", "ct", "h0", "h1", "qm", "kv", "kt", "vt", "ob", "ot", "lse", "u", "act",
        "mu", "rs", "part", "psend", "rsbuf", "agbuf", "dz", "do", "dom", "delta", "dqt",
        "dkvo", "dkvi", "own", "dqkv", "du", "dh0", "ge", "gl", "r1e", "r1l", "r2e", "r2l",
        "s3e", "s3l", "r3e", "r3l", "k3e", "k3l", "sm", "sr1", "sr2", "sr3", "lnacc", "lsem",
        "kvs", "kvr", "dks", "dkr", "ars", "arr", "g1s", "g1r", "g2s", "g2r", "g3s", "g3r",
        "s1s", "s1r", "s2s", "s2r", "s3s", "s3r",
    )
    assert len(names) == len(refs)
    v = Refs()
    v.__dict__.update(zip(names, refs))
    rows, depth = v.x.shape
    group = SEQ // rows
    nx = nd // group
    chunk = rows // nt_dev
    grow = depth // nd
    width = v.wout.shape[1]
    ff = v.win.shape[2]

    me_t = lax.axis_index("tensor")
    me_d = lax.axis_index("dp")
    rank = lax.rem(me_d, group)
    core = lax.rem(me_d, 2)
    zlo = lax.rem(me_d // 2, 2)
    xc = me_d // group
    other_core = me_d + 1 - 2 * core
    other_z = me_d + 2 - 4 * zlo

    barrier = pltpu.get_barrier_semaphore()
    for k in range(1, nt_dev):
        pl.semaphore_signal(
            barrier, inc=1, device_id={"tensor": lax.rem(me_t + k, nt_dev)}, device_id_type=MESH
        )
    for k in range(1, nd):
        pl.semaphore_signal(
            barrier, inc=1, device_id={"dp": lax.rem(me_d + k, nd)}, device_id_type=MESH
        )

    def load(src, dst, index):
        copy = pltpu.make_async_copy(src, dst, v.lsem.at[index])
        copy.start()
        return copy

    load_tok = load(v.tok, v.xt, 0)
    load_cos = load(v.cos_h.at[rows_at(rank, rows)], v.cosine, 1)
    load_sin = load(v.sin_h.at[rows_at(rank, rows)], v.sine, 2)
    load_qkv = []
    load_rest = []
    for l in range(LAYERS):
        load_qkv.append(
            [
                load(
                    v.wqkv_h.at[l, c],
                    v.wqkv.at[l, :, pl.ds(c * width, width)],
                    4 + 6 * l + c,
                )
                for c in range(3)
            ]
        )
        load_rest.append(
            [
                load(v.win_h.at[l], v.win.at[l], 4 + 6 * l + 3),
                load(v.wdown_h.at[l], v.wdown.at[l], 4 + 6 * l + 4),
                load(v.wout_h.at[l], v.wout.at[l], 4 + 6 * l + 5),
            ]
        )
    load_cot = load(v.cot, v.ct, 3)

    def norm_rows(l, at, x):
        mean = jnp.mean(x, axis=-1, keepdims=True)
        center = x - mean
        spread = jnp.mean(center * center, axis=-1, keepdims=True)
        r = lax.rsqrt(spread + EPS)
        xhat = center * r
        v.mu[l, at, :] = mean
        v.rs[l, at, :] = r
        v.h0[l, at, :] = (xhat * v.gain[l, 0:1, :] + v.bias[l, 0:1, :]).astype(BF16)
        v.h1[l, at, :] = (xhat * v.gain[l, 1:2, :] + v.bias[l, 1:2, :]).astype(BF16)

    def stream_rows(l, at):
        if l == 0:
            return v.xt[at, :].astype(F32)
        return v.x[at, :]

    def rs_copy(s, j):
        return remote(
            v.psend.at[s, j],
            v.rsbuf.at[s, me_t],
            v.ars.at[s, 0, j],
            v.arr.at[s, 0, me_t],
            tensor=j,
        )

    def rs_start(s, j):
        @pl.when(j != me_t)
        def _():
            rs_copy(s, j).start()

    def rs_finish(s):
        v.rsbuf[s, me_t] = v.psend[s, me_t]

        def one(k, carry):
            src = lax.rem(me_t + k, nt_dev)
            remote(
                v.psend.at[s, src],
                v.rsbuf.at[s, src],
                v.ars.at[s, 0, src],
                v.arr.at[s, 0, src],
                tensor=src,
            ).wait()
            return carry

        lax.fori_loop(1, nt_dev, one, 0)

    def rs_sum(s, at):
        total = v.rsbuf[s, 0, at, :].astype(F32)
        for k in range(1, nt_dev):
            total = total + v.rsbuf[s, k, at, :].astype(F32)
        return total

    def ag_copy(s, k):
        return remote(
            v.agbuf.at[s, me_t],
            v.agbuf.at[s, me_t],
            v.ars.at[s, 1, k],
            v.arr.at[s, 1, me_t],
            tensor=lax.rem(me_t + k, nt_dev),
        )

    def ag_start(s):
        for k in range(1, nt_dev):
            ag_copy(s, k).start()

    def ag_each(s, use):
        def one(k, carry):
            src = lax.rem(me_t + k, nt_dev)

            @pl.when(k > 0)
            def _():
                remote(
                    v.agbuf.at[s, src],
                    v.agbuf.at[s, src],
                    v.ars.at[s, 1, k],
                    v.arr.at[s, 1, src],
                    tensor=src,
                ).wait_recv()

            for i in range(chunk // ST):
                use(
                    pl.ds(pl.multiple_of(src * chunk + i * ST, ST), ST),
                    v.agbuf[s, src, i * ST : (i + 1) * ST, :].astype(F32),
                )
            return carry

        lax.fori_loop(0, nt_dev, one, 0)
        for k in range(1, nt_dev):
            ag_copy(s, k).wait_send()

    def kv_copy(l, s):
        return remote(
            v.kv.at[l, rank], v.kv.at[l, rank], v.kvs.at[l, s - 1], v.kvr.at[l, s - 1], dp=me_d + s
        )

    def kv_in(l, s):
        return remote(
            v.kv.at[l, rank - s],
            v.kv.at[l, rank - s],
            v.kvs.at[l, s - 1],
            v.kvr.at[l, s - 1],
            dp=me_d - s,
        )

    def dkv_copy(l, s):
        return remote(
            v.dkvo.at[l, rank - s],
            v.dkvi.at[l, s - 1],
            v.dks.at[l, s - 1],
            v.dkr.at[l, s - 1],
            dp=me_d - s,
        )

    def dkv_in(l, s):
        return remote(
            v.dkvo.at[l, rank],
            v.dkvi.at[l, s - 1],
            v.dks.at[l, s - 1],
            v.dkr.at[l, s - 1],
            dp=me_d + s,
        )

    def transpose_block(l, b):
        block = v.kv[l, b].astype(F32)
        v.kt[l, b] = block[:, :width].T.astype(BF16)
        v.vt[l, b] = block[:, width:].T.astype(BF16)

    def qkv_and_send(l, barrier_wait):
        for c in load_qkv[l]:
            c.wait()
        if l == 0:
            load_cos.wait()
            load_sin.wait()

        def one(i, carry):
            at = rows_at(i, MT)
            mixed = nn(v.h0[l, at, :], v.wqkv[l])
            cosine, sine = v.cosine[at, :], v.sine[at, :]
            q = rotate(mixed[:, :width] + v.bqkv[0, l : l + 1, :], cosine, sine).astype(BF16)
            k = rotate(mixed[:, width : 2 * width] + v.bqkv[1, l : l + 1, :], cosine, sine)
            val = mixed[:, 2 * width :] + v.bqkv[2, l : l + 1, :]
            scaled = (q.astype(F32) * 0.125).astype(BF16)
            v.qm[l, 0, at, :] = head_only(scaled, 0)
            v.qm[l, 1, at, :] = head_only(scaled, 1)
            v.kv[l, rank, at, :width] = k.astype(BF16)
            v.kv[l, rank, at, width:] = val.astype(BF16)
            return carry

        lax.fori_loop(0, rows // MT, one, 0)
        if barrier_wait:
            with jax.named_scope("barrier"):
                pl.semaphore_wait(barrier, nt_dev - 1 + nd - 1)
        for s in range(1, group):

            @pl.when(rank + s < group)
            def _():
                kv_copy(l, s).start()

    def feed_forward(l):
        for c in load_rest[l]:
            c.wait()

        def up(i, carry):
            at = rows_at(i, MT)
            v.u[l, at, :] = nn(v.h1[l, at, :], v.win[l]) + v.bin[l : l + 1, :]
            return carry

        lax.fori_loop(0, rows // MT, up, 0)

        def activate(i, carry):
            at = rows_at(i, ST)
            u = v.u[l, at, :]
            v.act[l, at, :] = (0.5 * u * (1.0 + lax.erf(u * np.float32(0.5**0.5)))).astype(BF16)
            return carry

        lax.fori_loop(0, rows // ST, activate, 0)

        def down(i, carry):
            at = rows_at(i, MT)
            v.part[at, :] = nn(v.act[l, at, :], v.wdown[l])
            return carry

        lax.fori_loop(0, rows // MT, down, 0)

    def attention(l, s):
        transpose_block(l, rank)
        for k in range(1, group):

            @pl.when(rank >= k)
            def _():
                kv_in(l, k).wait_recv()
                transpose_block(l, rank - k)

        for qt in range(rows // QT):
            q_at = slice(qt * QT, (qt + 1) * QT)
            for h in range(2):
                qh = v.qm[l, h, q_at, :]
                head_rows = slice(h * HEAD_DIM, (h + 1) * HEAD_DIM)

                def block(b, carry, masked):
                    top, total, out = carry
                    sc = nt(v.kv[l, b, :, :width], qh)
                    if masked:
                        key = lax.broadcasted_iota(jnp.int32, sc.shape, 0)
                        query = lax.broadcasted_iota(jnp.int32, sc.shape, 1) + qt * QT
                        sc = jnp.where(key <= query, sc, -1e30)
                    new = jnp.maximum(top, jnp.max(sc, axis=0, keepdims=True))
                    p = jnp.exp(sc - new)
                    fade = jnp.exp(top - new)
                    total = total * fade + jnp.sum(p, axis=0, keepdims=True)
                    out = out * fade + nn(v.vt[l, b, head_rows, :], p.astype(BF16))
                    return new, total, out

                carry = (
                    jnp.full((1, QT), -1e30, F32),
                    jnp.zeros((1, QT), F32),
                    jnp.zeros((HEAD_DIM, QT), F32),
                )
                carry = lax.fori_loop(0, rank, functools.partial(block, masked=False), carry)
                top, total, out = block(rank, carry, True)
                v.ot[l, head_rows, q_at] = out / total
                v.lse[l, h : h + 1, q_at] = top + jnp.log(total)
            v.ob[l, q_at, :] = v.ot[l, :, q_at].T.astype(BF16)
            both = nn(v.ob[l, q_at, :], v.wout[l]) + v.part[q_at, :]
            first = qt * QT // chunk
            v.psend[s, first : first + QT // chunk] = both.astype(BF16).reshape(
                QT // chunk, chunk, depth
            )
            for j in range(first, first + QT // chunk):
                rs_start(s, j)

    def branch_reduce(s):
        rs_finish(s)
        for i in range(chunk // 16):
            at = slice(i * 16, (i + 1) * 16)
            v.agbuf[s, me_t, at, :] = rs_sum(s, at).astype(BF16)
        ag_start(s)

    grads = {0: (v.ge, v.r1e, v.r2e, v.s3e, v.r3e, v.k3e), 1: (v.gl, v.r1l, v.r2l, v.s3l, v.r3l, v.k3l)}

    def core_copy(l, p):
        g, r1 = grads[p][:2]
        return remote(
            g.at[l, 1 - core], r1.at[l], v.g1s.at[l, p], v.g1r.at[l, p], dp=other_core
        )

    def x_copy(l, p, k):
        r1, r2 = grads[p][1:3]
        to = lax.rem(xc + k, nx)
        return remote(
            r1.at[l, pl.ds(2 * to, 2)],
            r2.at[l, k - 1],
            v.g2s.at[l, p, k - 1],
            v.g2r.at[l, p, k - 1],
            dp=to * group + zlo * 2 + core,
        )

    def z_copy(l, p):
        return remote(
            grads[p][3].at[l], grads[p][4].at[l], v.g3s.at[l, p], v.g3r.at[l, p], dp=other_z
        )

    def grad_core(l, p):
        core_copy(l, p).start()

    def grad_x(l, p):
        core_copy(l, p).wait()
        g, r1 = grads[p][:2]

        def one(i, carry):
            for j in range(grow // 16):
                at = slice(j * 16, (j + 1) * 16)
                r1[l, i, at, :] = (
                    r1[l, i, at, :].astype(F32) + g[l, core, i, at, :].astype(F32)
                ).astype(BF16)
            return carry

        lax.fori_loop(0, nd // 2, one, 0)
        for k in range(1, nx):
            x_copy(l, p, k).start()

    def grad_z(l, p):
        _, r1, r2, s3, r3, k3 = grads[p]
        for k in range(1, nx):
            x_copy(l, p, k).wait()

        def total(z, at):
            value = r1[l, 2 * xc + z, at, :].astype(F32)
            for k in range(1, nx):
                value = value + r2[l, k - 1, z, at, :].astype(F32)
            return value

        for j in range(grow // 16):
            at = slice(j * 16, (j + 1) * 16)
            s3[l, at, :] = total(1 - zlo, at).astype(BF16)
        z_copy(l, p).start()
        for j in range(grow // 16):
            at = slice(j * 16, (j + 1) * 16)
            k3[l, at, :] = total(zlo, at)

    def grad_end(l, p):
        z_copy(l, p).wait()
        _, _, _, _, r3, k3 = grads[p]
        for j in range(grow // 16):
            at = slice(j * 16, (j + 1) * 16)
            total = k3[l, at, :] + r3[l, at, :].astype(F32)
            if p == 0:
                v.oo[l, at, :] = total[:, :width]
                v.od[l, at, :] = total[:, width : width + ff]
                v.oi[l, at, :] = total[:, width + ff :]
            else:
                for c in range(3):
                    v.oq[l, c, at, :] = total[:, c * width : (c + 1) * width]

    def start_gradient(l, at, gradient):
        v.dz[at, :] = gradient.astype(BF16)

    def attention_back(l):
        v.do[...] = nt(v.dz[...], v.wout[l]).astype(BF16)
        do = v.do[...]
        v.dom[0] = head_only(do, 0)
        v.dom[1] = head_only(do, 1)
        product = do.astype(F32).T * v.ot[l]
        v.delta[0:1, :] = jnp.sum(product[:HEAD_DIM], axis=0, keepdims=True)
        v.delta[1:2, :] = jnp.sum(product[HEAD_DIM:], axis=0, keepdims=True)
        v.dqt[...] = jnp.zeros_like(v.dqt)

        def piece(b, i, masked):
            at = rows_at(i, KT)
            keys = v.kv[l, b, at, :width]
            values = v.kv[l, b, at, width:]
            dk = jnp.zeros((KT, width), F32)
            dv = jnp.zeros((KT, width), F32)
            for h in range(2):
                head_rows = slice(h * HEAD_DIM, (h + 1) * HEAD_DIM)
                sc = nt(keys, v.qm[l, h])
                if masked:
                    key = lax.broadcasted_iota(jnp.int32, sc.shape, 0) + i * KT
                    query = lax.broadcasted_iota(jnp.int32, sc.shape, 1)
                    sc = jnp.where(key <= query, sc, -1e30)
                p = jnp.exp(sc - v.lse[l, h : h + 1, :])
                dp = nt(values, v.dom[h])
                ds = (p * (dp - v.delta[h : h + 1, :])).astype(BF16)
                dv = dv + nn(p.astype(BF16), v.dom[h])
                dk = dk + nn(ds, v.qm[l, h])
                v.dqt[head_rows, :] += nn(v.kt[l, b, head_rows, at], ds)
            return dk, dv

        def far(b, carry):
            def inner(i, c):
                dk, dv = piece(b, i, False)
                at = rows_at(i, KT)
                v.dkvo[l, b, at, :width] = dk.astype(BF16)
                v.dkvo[l, b, at, width:] = dv.astype(BF16)
                return c

            lax.fori_loop(0, rows // KT, inner, 0)
            for s in range(1, group):

                @pl.when(rank - b == s)
                def _():
                    dkv_copy(l, s).start()

            return carry

        lax.fori_loop(0, rank, far, 0)

        def near(i, c):
            dk, dv = piece(rank, i, True)
            at = rows_at(i, KT)
            v.own[at, :width] = dk
            v.own[at, width:] = dv
            return c

        lax.fori_loop(0, rows // KT, near, 0)

    def feed_forward_back(l):
        def up(i, carry):
            at = rows_at(i, MT)
            v.part[at, :ff] = nt(v.dz[at, :], v.wdown[l])
            return carry

        lax.fori_loop(0, rows // MT, up, 0)

        def slope(i, acc):
            at = rows_at(i, ST)
            u = v.u[l, at, :]
            inner = 0.5 * (1.0 + lax.erf(u * np.float32(0.5**0.5)))
            inner = inner + u * jnp.exp(-0.5 * u * u) * np.float32((2.0 * np.pi) ** -0.5)
            du = (v.part[at, :ff] * inner).astype(BF16)
            v.du[at, :] = du
            return acc + jnp.sum(du.astype(F32).reshape(ST // 8, 8, ff), axis=0)

        acc = lax.fori_loop(0, rows // ST, slope, jnp.zeros((8, ff), F32))
        v.sm[l, 5:6, :ff] = jnp.sum(acc, axis=0, keepdims=True)

        def down(i, carry):
            at = rows_at(i, MT)
            v.part[at, :] = nt(v.du[at, :], v.win[l])
            return carry

        lax.fori_loop(0, rows // MT, down, 0)

    def early_grads(l):
        def one(i, carry):
            at = rows_at(i, 2 * grow)
            dzt = v.dz[:, at].astype(F32).T.astype(BF16)
            ht = v.h1[l, :, at].astype(F32).T.astype(BF16)
            wo = nn(dzt, v.ob[l]).astype(BF16)
            wd = nn(dzt, v.act[l]).astype(BF16)
            wi = nn(ht, v.du[...]).astype(BF16)
            for c in range(2):
                part = slice(c * grow, (c + 1) * grow)
                v.ge[l, c, i, :, :width] = wo[part]
                v.ge[l, c, i, :, width : width + ff] = wd[part]
                v.ge[l, c, i, :, width + ff :] = wi[part]
            return carry

        lax.fori_loop(0, depth // (2 * grow), one, 0)

    def late_grads(l):
        def one(i, carry):
            at = rows_at(i, 2 * grow)
            ht = v.h0[l, :, at].astype(F32).T.astype(BF16)
            wq = nn(ht, v.dqkv[...]).astype(BF16)
            for c in range(2):
                v.gl[l, c, i] = wq[c * grow : (c + 1) * grow]
            return carry

        lax.fori_loop(0, depth // (2 * grow), one, 0)

    def qkv_back(l):
        for s in range(1, group):

            @pl.when(rank + s < group)
            def _():
                dkv_in(l, s).wait_recv()
                v.own[...] += v.dkvi[l, s - 1].astype(F32)

        cosine, sine = v.cosine[...], -v.sine[...]
        v.dqkv[:, :width] = rotate(v.dqt[...].T * 0.125, cosine, sine).astype(BF16)
        v.dqkv[:, width : 2 * width] = rotate(v.own[:, :width], cosine, sine).astype(BF16)
        v.dqkv[:, 2 * width : 3 * width] = v.own[:, width:].astype(BF16)
        v.sm[l, 5:6, ff : ff + 3 * width] = jnp.sum(
            v.dqkv[...].astype(F32), axis=0, keepdims=True
        )

        def one(i, carry):
            at = rows_at(i, MT)
            v.dh0[at, :] = nt(v.dqkv[at, :], v.wqkv[l])
            return carry

        lax.fori_loop(0, rows // MT, one, 0)

        def send(k, carry):
            j = lax.rem(me_t + k, nt_dev)
            for i in range(chunk // ST):
                at = pl.ds(pl.multiple_of(j * chunk + i * ST, ST), ST)
                both = v.dh0[at, :] * v.gain[l, 0:1, :] + v.part[at, :] * v.gain[l, 1:2, :]
                v.psend[0, j, i * ST : (i + 1) * ST, :] = both.astype(BF16)
            rs_start(0, j)
            return carry

        lax.fori_loop(1, nt_dev + 1, send, 0)

    def norm_grads(l):
        v.lnacc[...] = jnp.zeros_like(v.lnacc)

        def fold(value):
            return jnp.sum(value.reshape(2, 8, depth), axis=0)

        def one(i, carry):
            at = rows_at(i, 16)
            xhat = (stream_rows(l, at) - v.mu[l, at, :]) * v.rs[l, at, :]
            first, second = v.dh0[at, :], v.part[at, :]
            v.lnacc[0] += fold(first * xhat)
            v.lnacc[1] += fold(second * xhat)
            v.lnacc[2] += fold(first)
            v.lnacc[3] += fold(second)
            v.lnacc[4] += fold(v.dz[at, :].astype(F32))
            return carry

        lax.fori_loop(0, rows // 16, one, 0)
        for i in range(5):
            v.sm[l, i : i + 1, :] = jnp.sum(v.lnacc[i], axis=0, keepdims=True)

    def stream_reduce(l):
        rs_finish(0)
        for i in range(chunk // 16):
            at = pl.ds(pl.multiple_of(me_t * chunk + i * 16, 16), 16)
            gd = rs_sum(0, slice(i * 16, (i + 1) * 16))
            r = v.rs[l, at, :]
            xhat = (stream_rows(l, at) - v.mu[l, at, :]) * r
            mean = jnp.mean(gd, axis=-1, keepdims=True)
            along = jnp.mean(gd * xhat, axis=-1, keepdims=True)
            dx = r * (gd - mean - xhat * along)
            v.agbuf[0, me_t, i * 16 : (i + 1) * 16, :] = dx.astype(BF16)
        ag_start(0)

    def small_core():
        return remote(v.sm, v.sr1, v.s1s, v.s1r, dp=other_core)

    def small_dp(k):
        to = lax.rem(me_d + 2 * k, nd)
        return remote(v.sm, v.sr2.at[k - 1], v.s2s.at[k - 1], v.s2r.at[k - 1], dp=to)

    def small_tensor(k):
        to = lax.rem(me_t + k, nt_dev)
        return remote(
            v.sm,
            v.sr3.at[k - 1],
            v.s3s.at[k - 1],
            v.s3r.at[k - 1],
            tensor=to,
        )

    with jax.named_scope("tok"):
        load_tok.wait()

    def first_norm(i, carry):
        at = rows_at(i, ST)
        norm_rows(0, at, v.xt[at, :].astype(F32))
        return carry

    with jax.named_scope("norm0"):
        lax.fori_loop(0, rows // ST, first_norm, 0)
    v.sm[...] = jnp.zeros_like(v.sm)
    with jax.named_scope("qkv0"):
        qkv_and_send(0, True)
    with jax.named_scope("ffn0"):
        feed_forward(0)
    with jax.named_scope("attn0"):
        attention(0, 0)
    with jax.named_scope("reduce0"):
        branch_reduce(0)

    def next_stream(at, z):
        x = v.xt[at, :].astype(F32) + (z + (v.bout[0:1, :] + v.bdown[0:1, :]))
        v.x[at, :] = x
        norm_rows(1, at, x)

    with jax.named_scope("gather0"):
        ag_each(0, next_stream)
    with jax.named_scope("qkv1"):
        qkv_and_send(1, False)
    with jax.named_scope("ffn1"):
        feed_forward(1)
    with jax.named_scope("attn1"):
        attention(1, 1)

    with jax.named_scope("cot"):
        load_cot.wait()

    def first_gradient(i, carry):
        at = rows_at(i, ST)
        v.dz[at, :] = v.ct[at, :]
        v.g[at, :] = v.ct[at, :].astype(F32)
        return carry

    with jax.named_scope("dz1"):
        lax.fori_loop(0, rows // ST, first_gradient, 0)
    with jax.named_scope("attn_grad1"):
        attention_back(1)
    with jax.named_scope("ffn_grad1"):
        feed_forward_back(1)
    with jax.named_scope("reduce1"):
        branch_reduce(1)
    with jax.named_scope("early1"):
        early_grads(1)
    grad_core(1, 0)
    with jax.named_scope("qkv_grad1"):
        qkv_back(1)
    with jax.named_scope("late1"):
        late_grads(1)
    grad_core(1, 1)
    with jax.named_scope("gx10"):
        grad_x(1, 0)
    with jax.named_scope("norm_grad1"):
        norm_grads(1)
    with jax.named_scope("stream_reduce1"):
        stream_reduce(1)
    with jax.named_scope("gx11"):
        grad_x(1, 1)

    def last_stream(at, z):
        v.x[at, :] = v.x[at, :] + (z + (v.bout[1:2, :] + v.bdown[1:2, :]))

    with jax.named_scope("gather1"):
        ag_each(1, last_stream)

    def next_gradient(at, dx):
        gradient = v.g[at, :] + dx
        v.g[at, :] = gradient
        v.dz[at, :] = gradient.astype(BF16)

    with jax.named_scope("gather2"):
        ag_each(0, next_gradient)
    with jax.named_scope("attn_grad0"):
        attention_back(0)
    with jax.named_scope("gz10"):
        grad_z(1, 0)
    with jax.named_scope("gz11"):
        grad_z(1, 1)
    with jax.named_scope("ffn_grad0"):
        feed_forward_back(0)
    with jax.named_scope("early0"):
        early_grads(0)
    grad_core(0, 0)
    with jax.named_scope("gend10"):
        grad_end(1, 0)
    with jax.named_scope("gend11"):
        grad_end(1, 1)
    with jax.named_scope("qkv_grad0"):
        qkv_back(0)
    with jax.named_scope("gx00"):
        grad_x(0, 0)
    with jax.named_scope("late0"):
        late_grads(0)
    grad_core(0, 1)
    with jax.named_scope("norm_grad0"):
        norm_grads(0)
    small_core().start()
    with jax.named_scope("stream_reduce0"):
        stream_reduce(0)
    with jax.named_scope("gx01"):
        grad_x(0, 1)
    small_core().wait()
    v.sm[...] += v.sr1[...]
    for k in range(1, nd // 2):
        small_dp(k).start()

    def last_gradient(at, dx):
        v.g[at, :] = v.g[at, :] + dx

    with jax.named_scope("gather3"):
        ag_each(0, last_gradient)
    for k in range(1, nd // 2):
        small_dp(k).wait()
    total = v.sm[...]
    for k in range(1, nd // 2):
        total = total + v.sr2[k - 1]
    v.sm[...] = total
    for k in range(1, nt_dev):
        small_tensor(k).start()
    with jax.named_scope("gz00"):
        grad_z(0, 0)
    with jax.named_scope("gz01"):
        grad_z(0, 1)
    for l in range(LAYERS):
        v.obout[l : l + 1, :] = v.sm[l, 4:5, :]
        v.obdown[l : l + 1, :] = v.sm[l, 4:5, :]
        v.obin[l : l + 1, :] = v.sm[l, 5:6, :ff]
        for c in range(3):
            v.obqkv[c, l : l + 1, :] = v.sm[l, 5:6, ff + c * width : ff + (c + 1) * width]
    for k in range(1, nt_dev):
        small_tensor(k).wait()
    total = v.sm[...]
    for k in range(1, nt_dev):
        total = total + v.sr3[k - 1]
    v.ogain[...] = total[:, 0:2, :]
    v.obias[...] = total[:, 2:4, :]
    with jax.named_scope("gend00"):
        grad_end(0, 0)
    with jax.named_scope("gend01"):
        grad_end(0, 1)
    for l in range(LAYERS):
        for s in range(1, group):

            @pl.when(rank + s < group)
            def _():
                kv_copy(l, s).wait_send()

            @pl.when(rank >= s)
            def _():
                dkv_copy(l, s).wait_send()


def on_device(nt_dev, nd, *args):
    tokens, cotangent, ln_gain, ln_bias, w_qkv, b_qkv, w_out, b_out, w_in, b_in, w_down, b_down = args
    rows, depth = tokens.shape
    width = w_out.shape[1]
    ff = w_in.shape[2]
    group = SEQ // rows
    chunk = rows // nt_dev
    grow = depth // nd
    half = nd // 2
    nx = nd // group
    early = width + 2 * ff
    late = 3 * width
    cosine, sine = rope_constants()
    vm = pltpu.VMEM
    dma = pltpu.SemaphoreType.DMA
    two = LAYERS
    scratch = [
        vm((two, depth, 3 * width), BF16),
        vm((two, width, depth), BF16),
        vm((two, depth, ff), BF16),
        vm((two, ff, depth), BF16),
        vm((rows, LANES), F32),
        vm((rows, LANES), F32),
        vm((rows, depth), BF16),
        vm((rows, depth), BF16),
        vm((two, rows, depth), BF16),
        vm((two, rows, depth), BF16),
        vm((two, 2, rows, width), BF16),
        vm((two, group, rows, 2 * width), BF16),
        vm((two, group, width, rows), BF16),
        vm((two, group, width, rows), BF16),
        vm((two, rows, width), BF16),
        vm((two, width, rows), F32),
        vm((two, 8, rows), F32),
        vm((two, rows, ff), F32),
        vm((two, rows, ff), BF16),
        vm((two, rows, 1), F32),
        vm((two, rows, 1), F32),
        vm((rows, depth), F32),
        vm((2, nt_dev, chunk, depth), BF16),
        vm((2, nt_dev, chunk, depth), BF16),
        vm((2, nt_dev, chunk, depth), BF16),
        vm((rows, depth), BF16),
        vm((rows, width), BF16),
        vm((2, rows, width), BF16),
        vm((8, rows), F32),
        vm((width, rows), F32),
        vm((two, group, rows, 2 * width), BF16),
        vm((two, group - 1, rows, 2 * width), BF16),
        vm((rows, 2 * width), F32),
        vm((rows, 3 * width), BF16),
        vm((rows, ff), BF16),
        vm((rows, depth), F32),
        vm((two, 2, half, grow, early), BF16),
        vm((two, 2, half, grow, late), BF16),
        vm((two, half, grow, early), BF16),
        vm((two, half, grow, late), BF16),
        vm((two, nx - 1, 2, grow, early), BF16),
        vm((two, nx - 1, 2, grow, late), BF16),
        vm((two, grow, early), BF16),
        vm((two, grow, late), BF16),
        vm((two, grow, early), BF16),
        vm((two, grow, late), BF16),
        vm((two, grow, early), F32),
        vm((two, grow, late), F32),
        vm((two, 8, depth), F32),
        vm((two, 8, depth), F32),
        vm((half - 1, two, 8, depth), F32),
        vm((nt_dev - 1, two, 8, depth), F32),
        vm((5, 8, depth), F32),
        dma((16,)),
        dma((two, group - 1)),
        dma((two, group - 1)),
        dma((two, group - 1)),
        dma((two, group - 1)),
        dma((2, 2, nt_dev)),
        dma((2, 2, nt_dev)),
        dma((two, 2)),
        dma((two, 2)),
        dma((two, 2, nx - 1)),
        dma((two, 2, nx - 1)),
        dma((two, 2)),
        dma((two, 2)),
        dma(()),
        dma(()),
        dma((half - 1,)),
        dma((half - 1,)),
        dma((nt_dev - 1,)),
        dma((nt_dev - 1,)),
    ]
    here = pl.BlockSpec(memory_space=pltpu.VMEM)
    away = pl.BlockSpec(memory_space=pl.ANY)
    shapes = [
        (rows, depth),
        (rows, depth),
        (two, 2, depth),
        (two, 2, depth),
        (3, two, width),
        (two, depth),
        (two, ff),
        (two, depth),
        (two, 3, grow, width),
        (two, grow, width),
        (two, grow, ff),
        (two, grow, ff),
    ]
    out = pl.pallas_call(
        functools.partial(step_kernel, nt_dev, nd),
        out_shape=[jax.ShapeDtypeStruct(s, F32) for s in shapes],
        in_specs=[away, away, here, here, away, here, away, here, away, here, away, here, away, away],
        out_specs=[here] * len(shapes),
        scratch_shapes=scratch,
        compiler_params=pltpu.CompilerParams(
            collective_id=0, has_side_effects=True, vmem_limit_bytes=64 * 1024 * 1024 - 65536
        ),
    )(
        tokens,
        cotangent,
        ln_gain,
        ln_bias,
        w_qkv.transpose(0, 2, 1, 3),
        b_qkv.transpose(1, 0, 2),
        w_out,
        b_out,
        w_in,
        b_in,
        w_down,
        b_down,
        jnp.asarray(cosine),
        jnp.asarray(sine),
    )
    x, g, gain, bias, bqkv, bout, b_in_g, bdown, wq, wo, wi, wd = out
    return (
        x,
        g,
        gain,
        bias,
        wq.transpose(0, 2, 1, 3),
        bqkv.transpose(1, 0, 2),
        wo.transpose(0, 2, 1),
        bout,
        wi,
        b_in_g,
        wd.transpose(0, 2, 1),
        bdown,
    )


def solution(mesh):
    return jax.shard_map(
        functools.partial(on_device, mesh.shape["tensor"], mesh.shape["dp"]),
        mesh=mesh,
        in_specs=(
            P("dp", None),
            P("dp", None),
            P(),
            P(),
            P(None, None, None, "tensor"),
            P(None, None, "tensor"),
            P(None, "tensor", None),
            P(),
            P(None, None, "tensor"),
            P(None, "tensor"),
            P(None, "tensor", None),
            P(),
        ),
        out_specs=(
            P("dp", None),
            P("dp", None),
            P(),
            P(),
            P(None, "dp", None, "tensor"),
            P(None, None, "tensor"),
            P(None, "tensor", "dp"),
            P(),
            P(None, "dp", "tensor"),
            P(None, "tensor"),
            P(None, "tensor", "dp"),
            P(),
        ),
        check_vma=False,
    )
```

```python
import functools

import jax
import jax.numpy as jnp
import numpy as np
from jax import lax
from jax.experimental import pallas as pl
from jax.experimental.pallas import tpu as pltpu
from jax.sharding import PartitionSpec as P

HEAD_DIM = 64
ROT = 16
SEQ = 2048
LAYERS = 2
EPS = 1e-05
F32 = jnp.float32
BF16 = jnp.bfloat16
MESH = pl.DeviceIdType.MESH
LANES = 128
QT = 256
KT = 256
MT = 256
ST = 32
PARTS = 8


def nn(a, b):
    return jnp.dot(a, b, preferred_element_type=F32)


def nt(a, b):
    return lax.dot_general(a, b, (((1,), (1,)), ((), ())), preferred_element_type=F32)


def rope_constants():
    half = ROT // 2
    exponent = np.arange(0, ROT, 2).astype(np.float32) / np.float32(ROT)
    inverse = (np.float32(1.0) / np.float32(10000.0) ** exponent).astype(np.float32)
    angles = np.arange(SEQ).astype(np.float32)[:, None] * inverse[None, :]
    cosine = np.ones((SEQ, LANES), np.float32)
    sine = np.zeros((SEQ, LANES), np.float32)
    for start in range(0, LANES, HEAD_DIM):
        cosine[:, start : start + half] = np.cos(angles)
        cosine[:, start + half : start + ROT] = np.cos(angles)
        sine[:, start : start + half] = -np.sin(angles)
        sine[:, start + half : start + ROT] = np.sin(angles)
    return cosine, sine


def rotate(values, cosine, sine):
    half = ROT // 2
    lane = lax.broadcasted_iota(jnp.int32, values.shape, 1)
    partner = jnp.where(
        lane % HEAD_DIM < half,
        pltpu.roll(values, LANES - half, 1),
        pltpu.roll(values, half, 1),
    )
    return values * cosine + partner * sine


def head_only(values, head):
    lane = lax.broadcasted_iota(jnp.int32, values.shape, 1)
    return jnp.where(lane // HEAD_DIM == head, values, jnp.zeros_like(values))


def rows_at(step, size):
    return pl.ds(pl.multiple_of(step * size, size), size)


def remote(src, dst, send_sem, recv_sem, **device):
    return pltpu.make_async_remote_copy(
        src_ref=src,
        dst_ref=dst,
        send_sem=send_sem,
        recv_sem=recv_sem,
        device_id=device,
        device_id_type=MESH,
    )


class Refs:
    pass


def step_kernel(nt_dev, nd, *refs):
    names = (
        "tok", "cot", "gain", "bias", "wqkv_h", "bqkv", "wout_h", "bout", "win_h", "bin",
        "wdown_h", "bdown", "cos_h", "sin_h", "ox", "og", "ogain", "obias", "obqkv", "obout",
        "obin", "obdown", "oq", "oo", "oi", "od", "wqkv", "wout", "win", "wdown", "cosine",
        "sine", "x", "g", "xt", "ct", "h0", "h1", "qm", "kv", "kt", "vt", "ob", "ot", "lse",
        "u", "act", "mu", "rs", "part", "psend", "rsbuf", "agbuf", "dz", "do", "dom", "delta",
        "dqt", "dkvo", "dkvi", "own", "dqkv", "du", "dact", "binacc", "dh0", "ge", "gl", "r1e",
        "r1l", "r2e", "r2l", "s3e", "s3l", "r3e", "r3l", "k3e", "k3l", "ln", "other", "ln1",
        "other1", "ln2", "other2", "lnc", "ln3", "lnall", "lnacc", "lsem", "kvs", "kvr", "dks",
        "dkr", "ars", "arr", "g1s", "g1r", "g2s", "g2r", "g3s", "g3r", "s1s", "s1r", "s2s",
        "s2r", "s3s", "s3r", "s4s", "s4r",
    )
    assert len(names) == len(refs)
    v = Refs()
    v.__dict__.update(zip(names, refs))
    rows, depth = v.x.shape
    group = SEQ // rows
    nx = nd // group
    chunk = rows // nt_dev
    grow = depth // nd
    width = v.wout.shape[1]
    ff = v.win.shape[2]

    me_t = lax.axis_index("tensor")
    me_d = lax.axis_index("dp")
    rank = lax.rem(me_d, group)
    core = lax.rem(me_d, 2)
    zlo = lax.rem(me_d // 2, 2)
    xc = me_d // group
    other_core = me_d + 1 - 2 * core
    other_z = me_d + 2 - 4 * zlo

    barrier = pltpu.get_barrier_semaphore()
    for k in range(1, nt_dev):
        pl.semaphore_signal(
            barrier, inc=1, device_id={"tensor": lax.rem(me_t + k, nt_dev)}, device_id_type=MESH
        )
    for k in range(1, nd):
        pl.semaphore_signal(
            barrier, inc=1, device_id={"dp": lax.rem(me_d + k, nd)}, device_id_type=MESH
        )

    def load(src, dst, index):
        copy = pltpu.make_async_copy(src, dst, v.lsem.at[index])
        copy.start()
        return copy

    load_tok = load(v.tok, v.xt, 0)
    load_cos = load(v.cos_h.at[rows_at(rank, rows)], v.cosine, 1)
    load_sin = load(v.sin_h.at[rows_at(rank, rows)], v.sine, 2)
    load_qkv = []
    load_rest = []
    for l in range(LAYERS):
        load_qkv.append(
            [
                load(
                    v.wqkv_h.at[l, c],
                    v.wqkv.at[l, :, pl.ds(c * width, width)],
                    4 + 6 * l + c,
                )
                for c in range(3)
            ]
        )
        load_rest.append(
            [
                load(v.win_h.at[l], v.win.at[l], 4 + 6 * l + 3),
                load(v.wdown_h.at[l], v.wdown.at[l], 4 + 6 * l + 4),
                load(v.wout_h.at[l], v.wout.at[l], 4 + 6 * l + 5),
            ]
        )
    load_cot = load(v.cot, v.ct, 3)

    def norm_rows(l, at, x):
        mean = jnp.mean(x, axis=-1, keepdims=True)
        center = x - mean
        spread = jnp.mean(center * center, axis=-1, keepdims=True)
        r = lax.rsqrt(spread + EPS)
        xhat = center * r
        v.mu[l, at, :] = mean
        v.rs[l, at, :] = r
        v.h0[l, at, :] = (xhat * v.gain[l, 0:1, :] + v.bias[l, 0:1, :]).astype(BF16)
        v.h1[l, at, :] = (xhat * v.gain[l, 1:2, :] + v.bias[l, 1:2, :]).astype(BF16)

    def stream_rows(l, at):
        if l == 0:
            return v.xt[at, :].astype(F32)
        return v.x[at, :]

    def rs_copy(s, j):
        return remote(
            v.psend.at[s, j],
            v.rsbuf.at[s, me_t],
            v.ars.at[s, 0, j],
            v.arr.at[s, 0, me_t],
            tensor=j,
        )

    def rs_start(s, j):
        @pl.when(j != me_t)
        def _():
            rs_copy(s, j).start()

    def rs_finish(s):
        v.rsbuf[s, me_t] = v.psend[s, me_t]

        def one(k, carry):
            src = lax.rem(me_t + k, nt_dev)
            remote(
                v.psend.at[s, src],
                v.rsbuf.at[s, src],
                v.ars.at[s, 0, src],
                v.arr.at[s, 0, src],
                tensor=src,
            ).wait()
            return carry

        lax.fori_loop(1, nt_dev, one, 0)

    def rs_sum(s, at):
        total = v.rsbuf[s, 0, at, :].astype(F32)
        for k in range(1, nt_dev):
            total = total + v.rsbuf[s, k, at, :].astype(F32)
        return total

    def ag_copy(s, k):
        return remote(
            v.agbuf.at[s, me_t],
            v.agbuf.at[s, me_t],
            v.ars.at[s, 1, k],
            v.arr.at[s, 1, me_t],
            tensor=lax.rem(me_t + k, nt_dev),
        )

    def ag_start(s):
        for k in range(1, nt_dev):
            ag_copy(s, k).start()

    def ag_pairs(s, first, last, use, after):
        def one(m, carry):
            pair = lax.rem(me_t // 2 + m, nt_dev // 2)
            for i in range(2):
                src = 2 * pair + i

                @pl.when(src != me_t)
                def _():
                    remote(
                        v.agbuf.at[s, src],
                        v.agbuf.at[s, src],
                        v.ars.at[s, 1, 1],
                        v.arr.at[s, 1, src],
                        tensor=src,
                    ).wait_recv()

                for j in range(chunk // ST):
                    use(
                        pl.ds(pl.multiple_of(src * chunk + j * ST, ST), ST),
                        v.agbuf[s, src, j * ST : (j + 1) * ST, :].astype(F32),
                    )
            after(rows_at(pair, 2 * chunk))
            return carry

        lax.fori_loop(first, last, one, 0)

    def ag_sent(s):
        for k in range(1, nt_dev):
            ag_copy(s, k).wait_send()

    def kv_copy(l, step):
        slot, to = [(rank, other_core), (rank, other_z), (rank - 2, other_core)][step]
        block = v.kv.at[l, slot]
        return remote(block, block, v.kvs.at[l, step], v.kvr.at[l, step], dp=to)

    def kv_in(l, step):
        slot = [rank - 1, rank - 2, rank - 1 - 2 * core][step]
        block = v.kv.at[l, slot]
        return remote(block, block, v.kvs.at[l, step], v.kvr.at[l, step], dp=other_core)

    def dkv_copy(l, step):
        return remote(
            v.dkvo.at[l, step],
            v.dkvi.at[l, step],
            v.dks.at[l, step],
            v.dkr.at[l, step],
            dp=other_z if step == 1 else other_core,
        )

    def transpose_block(l, b):
        block = v.kv[l, b].astype(F32)
        v.kt[l, b] = block[:, :width].T.astype(BF16)
        v.vt[l, b] = block[:, width:].T.astype(BF16)

    def qkv_rows(l, at, size):
        mixed = nn(v.h0[l, at, :], v.wqkv[l])
        cosine, sine = v.cosine[at, :], v.sine[at, :]
        q = rotate(mixed[:, :width] + v.bqkv[0, l : l + 1, :], cosine, sine).astype(BF16)
        k = rotate(mixed[:, width : 2 * width] + v.bqkv[1, l : l + 1, :], cosine, sine)
        val = mixed[:, 2 * width :] + v.bqkv[2, l : l + 1, :]
        scaled = (q.astype(F32) * 0.125).astype(BF16)
        v.qm[l, 0, at, :] = head_only(scaled, 0)
        v.qm[l, 1, at, :] = head_only(scaled, 1)
        v.kv[l, rank, at, :width] = k.astype(BF16)
        v.kv[l, rank, at, width:] = val.astype(BF16)

    def kv_send(l):
        @pl.when(zlo == 0)
        def _():
            kv_copy(l, 1).start()

        @pl.when(core == 0)
        def _():
            kv_copy(l, 0).start()

    def kv_relay(l):
        @pl.when(zlo == 1)
        def _():
            kv_in(l, 1).wait_recv()
            kv_copy(l, 2).start()

    def kv_finish(l):
        transpose_block(l, rank)

        @pl.when(core == 1)
        def _():
            kv_in(l, 0).wait_recv()
            transpose_block(l, rank - 1)

        @pl.when(zlo == 1)
        def _():
            transpose_block(l, rank - 2)
            kv_in(l, 2).wait_recv()
            transpose_block(l, rank - 1 - 2 * core)

    def feed_forward(l):
        for c in load_rest[l]:
            c.wait()

        def up(i, carry):
            at = rows_at(i, MT)
            v.u[l, at, :] = nn(v.h1[l, at, :], v.win[l]) + v.bin[l : l + 1, :]
            return carry

        lax.fori_loop(0, rows // MT, up, 0)

        def activate(i, carry):
            at = rows_at(i, ST)
            u = v.u[l, at, :]
            v.act[l, at, :] = (0.5 * u * (1.0 + lax.erf(u * np.float32(0.5**0.5)))).astype(BF16)
            return carry

        lax.fori_loop(0, rows // ST, activate, 0)

        def down(i, carry):
            at = rows_at(i, MT)
            v.part[at, :] = nn(v.act[l, at, :], v.wdown[l])
            return carry

        lax.fori_loop(0, rows // MT, down, 0)

    def attention(l, s):
        for qt in range(rows // QT):
            q_at = slice(qt * QT, (qt + 1) * QT)
            head_rows = [slice(h * HEAD_DIM, (h + 1) * HEAD_DIM) for h in range(2)]

            def block(b, carry, masked):
                keys = v.kv[l, b, :, :width]
                scores = [nt(keys, v.qm[l, h, q_at, :]) for h in range(2)]
                result = []
                for h in range(2):
                    top, total, out = carry[h]
                    sc = scores[h]
                    if masked:
                        key = lax.broadcasted_iota(jnp.int32, sc.shape, 0)
                        query = lax.broadcasted_iota(jnp.int32, sc.shape, 1) + qt * QT
                        sc = jnp.where(key <= query, sc, -1e30)
                    new = jnp.maximum(top, jnp.max(sc, axis=0, keepdims=True))
                    p = jnp.exp(sc - new)
                    fade = jnp.exp(top - new)
                    total = total * fade + jnp.sum(p, axis=0, keepdims=True)
                    out = out * fade + nn(v.vt[l, b, head_rows[h], :], p.astype(BF16))
                    result.append((new, total, out))
                return tuple(result)

            start = (
                jnp.full((1, QT), -1e30, F32),
                jnp.zeros((1, QT), F32),
                jnp.zeros((HEAD_DIM, QT), F32),
            )
            carry = lax.fori_loop(0, rank, functools.partial(block, masked=False), (start, start))
            carry = block(rank, carry, True)
            for h in range(2):
                top, total, out = carry[h]
                v.ot[l, head_rows[h], q_at] = out / total
                v.lse[l, h : h + 1, q_at] = top + jnp.log(total)
            v.ob[l, q_at, :] = v.ot[l, :, q_at].T.astype(BF16)
            both = nn(v.ob[l, q_at, :], v.wout[l]) + v.part[q_at, :]
            first = qt * QT // chunk
            v.psend[s, first : first + QT // chunk] = both.astype(BF16).reshape(
                QT // chunk, chunk, depth
            )
            for j in range(first, first + QT // chunk):
                rs_start(s, j)

    def branch_reduce(s):
        rs_finish(s)
        for i in range(chunk // 16):
            at = slice(i * 16, (i + 1) * 16)
            v.agbuf[s, me_t, at, :] = rs_sum(s, at).astype(BF16)
        ag_start(s)

    grads = {0: (v.ge, v.r1e, v.r2e, v.s3e, v.r3e, v.k3e), 1: (v.gl, v.r1l, v.r2l, v.s3l, v.r3l, v.k3l)}

    def core_copy(l, p):
        g, r1 = grads[p][:2]
        return remote(
            g.at[l, 1 - core], r1.at[l], v.g1s.at[l, p], v.g1r.at[l, p], dp=other_core
        )

    def x_copy(l, p, k):
        r1, r2 = grads[p][1:3]
        to = lax.rem(xc + k, nx)
        return remote(
            r1.at[l, pl.ds(2 * to, 2)],
            r2.at[l, k - 1],
            v.g2s.at[l, p, k - 1],
            v.g2r.at[l, p, k - 1],
            dp=to * group + zlo * 2 + core,
        )

    def z_copy(l, p):
        return remote(
            grads[p][3].at[l], grads[p][4].at[l], v.g3s.at[l, p], v.g3r.at[l, p], dp=other_z
        )

    def grad_core(l, p):
        core_copy(l, p).start()

    def grad_x(l, p):
        core_copy(l, p).wait()
        g, r1 = grads[p][:2]

        def one(i, carry):
            for j in range(grow // 16):
                at = slice(j * 16, (j + 1) * 16)
                r1[l, i, at, :] = (
                    r1[l, i, at, :].astype(F32) + g[l, core, i, at, :].astype(F32)
                ).astype(BF16)
            return carry

        lax.fori_loop(0, nd // 2, one, 0)
        for k in range(1, nx):
            x_copy(l, p, k).start()

    def grad_z(l, p):
        _, r1, r2, s3, r3, k3 = grads[p]
        for k in range(1, nx):
            x_copy(l, p, k).wait()

        def total(z, at):
            value = r1[l, 2 * xc + z, at, :].astype(F32)
            for k in range(1, nx):
                value = value + r2[l, k - 1, z, at, :].astype(F32)
            return value

        for j in range(grow // 16):
            at = slice(j * 16, (j + 1) * 16)
            s3[l, at, :] = total(1 - zlo, at).astype(BF16)
        z_copy(l, p).start()
        for j in range(grow // 16):
            at = slice(j * 16, (j + 1) * 16)
            k3[l, at, :] = total(zlo, at)

    def grad_end(l, p):
        z_copy(l, p).wait()
        _, _, _, _, r3, k3 = grads[p]
        for j in range(grow // 16):
            at = slice(j * 16, (j + 1) * 16)
            total = k3[l, at, :] + r3[l, at, :].astype(F32)
            if p == 0:
                v.oo[l, at, :] = total[:, :width]
                v.od[l, at, :] = total[:, width : width + ff]
                v.oi[l, at, :] = total[:, width + ff :]
            else:
                for c in range(3):
                    v.oq[l, c, at, :] = total[:, c * width : (c + 1) * width]

    def start_gradient(l, at, gradient):
        v.dz[at, :] = gradient.astype(BF16)

    def attention_back(l):
        do = v.do[...]
        product = do.astype(F32).T * v.ot[l]
        v.delta[0:1, :] = jnp.sum(product[:HEAD_DIM], axis=0, keepdims=True)
        v.delta[1:2, :] = jnp.sum(product[HEAD_DIM:], axis=0, keepdims=True)
        v.dqt[...] = jnp.zeros_like(v.dqt)

        def piece(b, i, masked):
            at = rows_at(i, KT)
            keys = v.kv[l, b, at, :width]
            values = v.kv[l, b, at, width:]
            dk = jnp.zeros((KT, width), F32)
            dv = jnp.zeros((KT, width), F32)
            for h in range(2):
                head_rows = slice(h * HEAD_DIM, (h + 1) * HEAD_DIM)
                sc = nt(keys, v.qm[l, h])
                if masked:
                    key = lax.broadcasted_iota(jnp.int32, sc.shape, 0) + i * KT
                    query = lax.broadcasted_iota(jnp.int32, sc.shape, 1)
                    sc = jnp.where(key <= query, sc, -1e30)
                p = jnp.exp(sc - v.lse[l, h : h + 1, :])
                dp = nt(values, v.dom[h])
                ds = (p * (dp - v.delta[h : h + 1, :])).astype(BF16)
                dv = dv + nn(p.astype(BF16), v.dom[h])
                dk = dk + nn(ds, v.qm[l, h])
                v.dqt[head_rows, :] += nn(v.kt[l, b, head_rows, at], ds)
            return dk, dv

        def far(b, slot, received):
            def inner(i, c):
                dk, dv = piece(b, i, False)
                at = rows_at(i, KT)
                if received:
                    dk = dk + v.dkvi[l, 0, at, :width].astype(F32)
                    dv = dv + v.dkvi[l, 0, at, width:].astype(F32)
                v.dkvo[l, slot, at, :width] = dk.astype(BF16)
                v.dkvo[l, slot, at, width:] = dv.astype(BF16)
                return c

            lax.fori_loop(0, rows // KT, inner, 0)
            dkv_copy(l, slot).start()

        @pl.when(zlo == 1)
        def _():
            far(1 - core, 0, False)
            dkv_copy(l, 0).wait_recv()
            far(core, 1, True)

        @pl.when(core == 1)
        def _():
            far(rank - 1, 2, False)

        def near(i, c):
            dk, dv = piece(rank, i, True)
            at = rows_at(i, KT)
            v.own[at, :width] = dk
            v.own[at, width:] = dv
            return c

        lax.fori_loop(0, rows // KT, near, 0)

    def back_rows(l, at, size):
        do = nt(v.dz[at, :], v.wout[l]).astype(BF16)
        v.do[at, :] = do
        v.dom[0, at, :] = head_only(do, 0)
        v.dom[1, at, :] = head_only(do, 1)
        v.dact[at, :] = nt(v.dz[at, :], v.wdown[l])
        start = at.start if isinstance(at, pl.Slice) else at

        def slope(i, acc):
            rows_now = pl.ds(pl.multiple_of(start + i * ST, ST), ST)
            u = v.u[l, rows_now, :]
            inner = 0.5 * (1.0 + lax.erf(u * np.float32(0.5**0.5)))
            inner = inner + u * jnp.exp(-0.5 * u * u) * np.float32((2.0 * np.pi) ** -0.5)
            du = (v.dact[rows_now, :] * inner).astype(BF16)
            v.du[rows_now, :] = du
            return acc + jnp.sum(du.astype(F32).reshape(ST // 8, 8, ff), axis=0)

        v.binacc[l] += lax.fori_loop(0, size // ST, slope, jnp.zeros((8, ff), F32))
        v.part[at, :] = nt(v.du[at, :], v.win[l])

    def early_grads(l):
        def one(i, carry):
            at = rows_at(i, 2 * grow)
            dzt = v.dz[:, at].astype(F32).T.astype(BF16)
            ht = v.h1[l, :, at].astype(F32).T.astype(BF16)
            wo = nn(dzt, v.ob[l]).astype(BF16)
            wd = nn(dzt, v.act[l]).astype(BF16)
            wi = nn(ht, v.du[...]).astype(BF16)
            for c in range(2):
                part = slice(c * grow, (c + 1) * grow)
                v.ge[l, c, i, :, :width] = wo[part]
                v.ge[l, c, i, :, width : width + ff] = wd[part]
                v.ge[l, c, i, :, width + ff :] = wi[part]
            return carry

        lax.fori_loop(0, depth // (2 * grow), one, 0)

    def late_grads(l):
        def one(i, carry):
            at = rows_at(i, 2 * grow)
            ht = v.h0[l, :, at].astype(F32).T.astype(BF16)
            wq = nn(ht, v.dqkv[...]).astype(BF16)
            for c in range(2):
                v.gl[l, c, i] = wq[c * grow : (c + 1) * grow]
            return carry

        lax.fori_loop(0, depth // (2 * grow), one, 0)

    def qkv_back(l):
        for step, here in ((2, core == 0), (1, zlo == 0)):

            @pl.when(here)
            def _():
                dkv_copy(l, step).wait_recv()
                v.own[...] += v.dkvi[l, step].astype(F32)

        cosine, sine = v.cosine[...], -v.sine[...]
        v.dqkv[:, :width] = rotate(v.dqt[...].T * 0.125, cosine, sine).astype(BF16)
        v.dqkv[:, width : 2 * width] = rotate(v.own[:, :width], cosine, sine).astype(BF16)
        v.dqkv[:, 2 * width : 3 * width] = v.own[:, width:].astype(BF16)
        v.other[4 * l + 3 : 4 * l + 4, : 3 * width] = jnp.sum(
            v.dqkv[...].astype(F32), axis=0, keepdims=True
        )

        def one(i, carry):
            at = rows_at(i, MT)
            v.dh0[at, :] = nt(v.dqkv[at, :], v.wqkv[l])
            return carry

        lax.fori_loop(0, rows // MT, one, 0)

        def send(k, carry):
            j = lax.rem(me_t + k, nt_dev)
            for i in range(chunk // ST):
                at = pl.ds(pl.multiple_of(j * chunk + i * ST, ST), ST)
                both = v.dh0[at, :] * v.gain[l, 0:1, :] + v.part[at, :] * v.gain[l, 1:2, :]
                v.psend[0, j, i * ST : (i + 1) * ST, :] = both.astype(BF16)
            rs_start(0, j)
            return carry

        lax.fori_loop(1, nt_dev + 1, send, 0)

    def norm_grads(l):
        v.lnacc[...] = jnp.zeros_like(v.lnacc)

        def fold(value):
            return jnp.sum(value.reshape(2, 8, depth), axis=0)

        def one(i, carry):
            at = rows_at(i, 16)
            xhat = (stream_rows(l, at) - v.mu[l, at, :]) * v.rs[l, at, :]
            first, second = v.dh0[at, :], v.part[at, :]
            v.lnacc[0] += fold(first * xhat)
            v.lnacc[1] += fold(second * xhat)
            v.lnacc[2] += fold(first)
            v.lnacc[3] += fold(second)
            v.lnacc[4] += fold(v.dz[at, :].astype(F32))
            return carry

        lax.fori_loop(0, rows // 16, one, 0)
        for i in range(4):
            v.ln[4 * l + i : 4 * l + i + 1, :] = jnp.sum(v.lnacc[i], axis=0, keepdims=True)
        column = jnp.sum(v.lnacc[4], axis=0, keepdims=True)
        v.other[4 * l : 4 * l + 1, :] = column[:, :ff]
        v.other[4 * l + 1 : 4 * l + 2, :] = column[:, ff:]
        v.other[4 * l + 2 : 4 * l + 3, :] = jnp.sum(v.binacc[l], axis=0, keepdims=True)

    def stream_reduce(l):
        rs_finish(0)
        for i in range(chunk // 16):
            at = pl.ds(pl.multiple_of(me_t * chunk + i * 16, 16), 16)
            gd = rs_sum(0, slice(i * 16, (i + 1) * 16))
            r = v.rs[l, at, :]
            xhat = (stream_rows(l, at) - v.mu[l, at, :]) * r
            mean = jnp.mean(gd, axis=-1, keepdims=True)
            along = jnp.mean(gd * xhat, axis=-1, keepdims=True)
            dx = r * (gd - mean - xhat * along)
            v.agbuf[0, me_t, i * 16 : (i + 1) * 16, :] = dx.astype(BF16)
        ag_start(0)

    def small_core(i):
        mine, theirs = [(v.ln, v.ln1), (v.other, v.other1)][i]
        return remote(mine, theirs, v.s1s.at[i], v.s1r.at[i], dp=other_core)

    def small_scatter(k):
        to = lax.rem(me_t + k, nt_dev)
        columns = pl.ds(pl.multiple_of(to * LANES, LANES), LANES)
        return remote(
            v.ln.at[:, columns], v.ln2.at[k - 1], v.s2s.at[k - 1], v.s2r.at[k - 1], tensor=to
        )

    def small_dp(k, i):
        to = lax.rem(me_d + 2 * k, nd)
        mine, theirs = [(v.lnc, v.ln3), (v.other, v.other2)][i]
        return remote(mine, theirs.at[k - 1], v.s3s.at[i, k - 1], v.s3r.at[i, k - 1], dp=to)

    def small_gather(k):
        to = lax.rem(me_t + k, nt_dev)
        block = v.lnall.at[me_t]
        return remote(block, block, v.s4s.at[k - 1], v.s4r.at[me_t], tensor=to)

    def small_start():
        for i in range(2):
            small_core(i).start()

    def small_second():
        for i in range(2):
            small_core(i).wait()
        v.ln[...] += v.ln1[...]
        v.other[...] += v.other1[...]
        for k in range(1, nt_dev):
            small_scatter(k).start()
        for k in range(1, nd // 2):
            small_dp(k, 1).start()

    def small_third():
        mine = pl.ds(pl.multiple_of(me_t * LANES, LANES), LANES)
        total = v.ln[:, mine]
        for k in range(1, nt_dev):
            small_scatter(k).wait()
            total = total + v.ln2[k - 1]
        v.lnc[...] = total
        for k in range(1, nd // 2):
            small_dp(k, 0).start()

    def small_fourth():
        total = v.lnc[...]
        for k in range(1, nd // 2):
            small_dp(k, 0).wait()
            total = total + v.ln3[k - 1]
        v.lnall[me_t] = total
        for k in range(1, nt_dev):
            small_gather(k).start()
        total = v.other[...]
        for k in range(1, nd // 2):
            small_dp(k, 1).wait()
            total = total + v.other2[k - 1]
        for l in range(LAYERS):
            for half in range(2):
                at = slice(half * ff, (half + 1) * ff)
                row = total[4 * l + half : 4 * l + half + 1, :]
                v.obout[l : l + 1, at] = row
                v.obdown[l : l + 1, at] = row
            v.obin[l : l + 1, :] = total[4 * l + 2 : 4 * l + 3, :]
            for c in range(3):
                at = slice(c * width, (c + 1) * width)
                v.obqkv[c, l : l + 1, :] = total[4 * l + 3 : 4 * l + 4, at]

    def small_end():
        for k in range(1, nt_dev):
            src = lax.rem(me_t + k, nt_dev)
            block = v.lnall.at[src]
            remote(block, block, v.s4s.at[k - 1], v.s4r.at[src], tensor=src).wait()
        for j in range(nt_dev):
            at = slice(j * LANES, (j + 1) * LANES)
            block = v.lnall[j]
            for l in range(LAYERS):
                v.ogain[l, :, at] = block[4 * l : 4 * l + 2, :]
                v.obias[l, :, at] = block[4 * l + 2 : 4 * l + 4, :]

    def nothing(at):
        pass

    with jax.named_scope("tok"):
        load_tok.wait()

    def first_norm(i, carry):
        at = rows_at(i, ST)
        norm_rows(0, at, v.xt[at, :].astype(F32))
        return carry

    with jax.named_scope("norm0"):
        lax.fori_loop(0, rows // ST, first_norm, 0, unroll=2)
    with jax.named_scope("qkv0"):
        for c in load_qkv[0]:
            c.wait()
        load_cos.wait()
        load_sin.wait()

        def first_qkv(i, carry):
            qkv_rows(0, rows_at(i, MT), MT)
            return carry

        lax.fori_loop(0, rows // MT, first_qkv, 0)
    with jax.named_scope("barrier"):
        pl.semaphore_wait(barrier, nt_dev - 1 + nd - 1)
    kv_send(0)
    v.ln[...] = jnp.zeros_like(v.ln)
    v.other[...] = jnp.zeros_like(v.other)
    v.binacc[...] = jnp.zeros_like(v.binacc)
    with jax.named_scope("ffn0"):
        feed_forward(0)
    with jax.named_scope("kv0"):
        kv_relay(0)
        kv_finish(0)
    with jax.named_scope("attn0"):
        attention(0, 0)
    with jax.named_scope("reduce0"):
        branch_reduce(0)

    def next_stream(at, z):
        x = v.xt[at, :].astype(F32) + (z + (v.bout[0:1, :] + v.bdown[0:1, :]))
        v.x[at, :] = x
        norm_rows(1, at, x)

    def next_qkv(at):
        qkv_rows(1, at, 2 * chunk)

    with jax.named_scope("gather0"):
        for c in load_qkv[1]:
            c.wait()
        ag_pairs(0, 0, nt_dev // 2, next_stream, next_qkv)
        kv_send(1)
        ag_sent(0)
    with jax.named_scope("ffn1"):
        feed_forward(1)
    with jax.named_scope("kv1"):
        kv_relay(1)
        kv_finish(1)
    with jax.named_scope("attn1"):
        attention(1, 1)

    with jax.named_scope("dz1"):
        load_cot.wait()

        def first_gradient(i, carry):
            at = rows_at(i, ST)
            v.dz[at, :] = v.ct[at, :]
            v.g[at, :] = v.ct[at, :].astype(F32)
            return carry

        lax.fori_loop(0, rows // ST, first_gradient, 0)

    with jax.named_scope("back1"):

        def first_back(i, carry):
            back_rows(1, rows_at(i, MT), MT)
            return carry

        lax.fori_loop(0, rows // MT, first_back, 0)
    with jax.named_scope("attn_grad1"):
        attention_back(1)

    def early(l, z):
        @pl.when(zlo == z)
        def _():
            early_grads(l)
            grad_core(l, 0)

    with jax.named_scope("early1"):
        early(1, 0)
    with jax.named_scope("qkv_grad1"):
        qkv_back(1)
    with jax.named_scope("early1b"):
        early(1, 1)
    with jax.named_scope("late1"):
        late_grads(1)
        grad_core(1, 1)
    with jax.named_scope("norm_grad1"):
        norm_grads(1)
    with jax.named_scope("gx10"):
        grad_x(1, 0)
    with jax.named_scope("stream_reduce1"):
        stream_reduce(1)
    with jax.named_scope("gx11"):
        grad_x(1, 1)

    def next_gradient(at, dx):
        gradient = v.g[at, :] + dx
        v.g[at, :] = gradient
        v.dz[at, :] = gradient.astype(BF16)

    def next_back(at):
        back_rows(0, at, 2 * chunk)

    with jax.named_scope("gather2"):
        ag_pairs(0, 0, nt_dev // 2, next_gradient, next_back)
        ag_sent(0)
    with jax.named_scope("reduce1"):
        branch_reduce(1)
    with jax.named_scope("attn_grad0"):
        attention_back(0)
    with jax.named_scope("gz1"):
        grad_z(1, 0)
        grad_z(1, 1)
    with jax.named_scope("early0"):
        early(0, 0)
    with jax.named_scope("qkv_grad0"):
        qkv_back(0)
    with jax.named_scope("early0b"):
        early(0, 1)
    with jax.named_scope("late0"):
        late_grads(0)
        grad_core(0, 1)
    with jax.named_scope("norm_grad0"):
        norm_grads(0)
        small_start()
    with jax.named_scope("gx00"):
        grad_x(0, 0)

    def last_stream(at, z):
        v.x[at, :] = v.x[at, :] + (z + (v.bout[1:2, :] + v.bdown[1:2, :]))

    store_x = pltpu.make_async_copy(v.x, v.ox, v.lsem.at[0])
    store_g = pltpu.make_async_copy(v.g, v.og, v.lsem.at[1])
    with jax.named_scope("small_second"):
        small_second()
    with jax.named_scope("stream_reduce0"):
        stream_reduce(0)
    with jax.named_scope("gx01"):
        grad_x(0, 1)
    with jax.named_scope("small_third"):
        small_third()
    with jax.named_scope("gather1"):
        ag_pairs(1, 0, nt_dev // 2, last_stream, nothing)
        ag_sent(1)
        store_x.start()
    with jax.named_scope("gend1"):
        grad_end(1, 0)
        grad_end(1, 1)

    def last_gradient(at, dx):
        v.g[at, :] = v.g[at, :] + dx

    with jax.named_scope("gather3"):
        ag_pairs(0, 0, nt_dev // 4, last_gradient, nothing)
    with jax.named_scope("small_fourth"):
        small_fourth()
    with jax.named_scope("gather3b"):
        ag_pairs(0, nt_dev // 4, nt_dev // 2, last_gradient, nothing)
        store_g.start()
        ag_sent(0)
    with jax.named_scope("gz0"):
        grad_z(0, 0)
        grad_z(0, 1)
    with jax.named_scope("small_end"):
        small_end()
    with jax.named_scope("gend0"):
        grad_end(0, 0)
        grad_end(0, 1)
        store_x.wait()
        store_g.wait()
    for l in range(LAYERS):
        for step, here in ((0, core == 0), (1, zlo == 0), (2, zlo == 1)):

            @pl.when(here)
            def _():
                kv_copy(l, step).wait_send()

        for step, here in ((0, zlo == 1), (1, zlo == 1), (2, core == 1)):

            @pl.when(here)
            def _():
                dkv_copy(l, step).wait_send()


def store_kernel(count, *refs):
    given, kept = refs[:count], refs[count : 2 * count]
    held = refs[2 * count : 2 * count + 2]
    sems = refs[2 * count + 2]
    rows = held[0].shape[0] // PARTS
    parts = [(i, slice(j * rows, (j + 1) * rows), i * PARTS + j) for j in range(PARTS) for i in range(2)]
    loads = [
        pltpu.make_async_copy(given[i].at[at], held[i].at[at], sems.at[0, n]) for i, at, n in parts
    ]
    stores = [
        pltpu.make_async_copy(held[i].at[at], kept[i].at[at], sems.at[1, n]) for i, at, n in parts
    ]
    others = [
        pltpu.make_async_copy(given[i], kept[i], sems.at[2, i]) for i in range(2, count)
    ]
    for copy in loads + others:
        copy.start()
    for load, store in zip(loads, stores):
        load.wait()
        store.start()
    for copy in stores + others:
        copy.wait()


def on_device(nt_dev, nd, *args):
    tokens, cotangent, ln_gain, ln_bias, w_qkv, b_qkv, w_out, b_out, w_in, b_in, w_down, b_down = args
    rows, depth = tokens.shape
    width = w_out.shape[1]
    ff = w_in.shape[2]
    group = SEQ // rows
    chunk = rows // nt_dev
    grow = depth // nd
    half = nd // 2
    nx = nd // group
    early = width + 2 * ff
    late = 3 * width
    cosine, sine = rope_constants()
    vm = pltpu.VMEM
    dma = pltpu.SemaphoreType.DMA
    two = LAYERS
    scratch = [
        vm((two, depth, 3 * width), BF16),
        vm((two, width, depth), BF16),
        vm((two, depth, ff), BF16),
        vm((two, ff, depth), BF16),
        vm((rows, LANES), F32),
        vm((rows, LANES), F32),
        vm((rows, depth), F32),
        vm((rows, depth), F32),
        vm((rows, depth), BF16),
        vm((rows, depth), BF16),
        vm((two, rows, depth), BF16),
        vm((two, rows, depth), BF16),
        vm((two, 2, rows, width), BF16),
        vm((two, group, rows, 2 * width), BF16),
        vm((two, group, width, rows), BF16),
        vm((two, group, width, rows), BF16),
        vm((two, rows, width), BF16),
        vm((two, width, rows), F32),
        vm((two, 8, rows), F32),
        vm((two, rows, ff), F32),
        vm((two, rows, ff), BF16),
        vm((two, rows, 1), F32),
        vm((two, rows, 1), F32),
        vm((rows, depth), F32),
        vm((2, nt_dev, chunk, depth), BF16),
        vm((2, nt_dev, chunk, depth), BF16),
        vm((2, nt_dev, chunk, depth), BF16),
        vm((rows, depth), BF16),
        vm((rows, width), BF16),
        vm((2, rows, width), BF16),
        vm((8, rows), F32),
        vm((width, rows), F32),
        vm((two, 3, rows, 2 * width), BF16),
        vm((two, 3, rows, 2 * width), BF16),
        vm((rows, 2 * width), F32),
        vm((rows, 3 * width), BF16),
        vm((rows, ff), BF16),
        vm((rows, ff), F32),
        vm((two, 8, ff), F32),
        vm((rows, depth), F32),
        vm((two, 2, half, grow, early), BF16),
        vm((two, 2, half, grow, late), BF16),
        vm((two, half, grow, early), BF16),
        vm((two, half, grow, late), BF16),
        vm((two, nx - 1, 2, grow, early), BF16),
        vm((two, nx - 1, 2, grow, late), BF16),
        vm((two, grow, early), BF16),
        vm((two, grow, late), BF16),
        vm((two, grow, early), BF16),
        vm((two, grow, late), BF16),
        vm((two, grow, early), F32),
        vm((two, grow, late), F32),
        vm((8, depth), F32),
        vm((8, ff), F32),
        vm((8, depth), F32),
        vm((8, ff), F32),
        vm((nt_dev - 1, 8, LANES), F32),
        vm((half - 1, 8, ff), F32),
        vm((8, LANES), F32),
        vm((half - 1, 8, LANES), F32),
        vm((nt_dev, 8, LANES), F32),
        vm((5, 8, depth), F32),
        dma((16,)),
        dma((two, 3)),
        dma((two, 3)),
        dma((two, 3)),
        dma((two, 3)),
        dma((2, 2, nt_dev)),
        dma((2, 2, nt_dev)),
        dma((two, 2)),
        dma((two, 2)),
        dma((two, 2, nx - 1)),
        dma((two, 2, nx - 1)),
        dma((two, 2)),
        dma((two, 2)),
        dma((2,)),
        dma((2,)),
        dma((nt_dev - 1,)),
        dma((nt_dev - 1,)),
        dma((2, half - 1)),
        dma((2, half - 1)),
        dma((nt_dev - 1,)),
        dma((nt_dev,)),
    ]
    here = pl.BlockSpec(memory_space=pltpu.VMEM)
    away = pl.BlockSpec(memory_space=pl.ANY)
    shapes = [
        (rows, depth),
        (rows, depth),
        (two, 2, depth),
        (two, 2, depth),
        (3, two, width),
        (two, depth),
        (two, ff),
        (two, depth),
        (two, 3, grow, width),
        (two, grow, width),
        (two, grow, ff),
        (two, grow, ff),
    ]
    out = pl.pallas_call(
        functools.partial(step_kernel, nt_dev, nd),
        out_shape=[jax.ShapeDtypeStruct(s, F32) for s in shapes],
        in_specs=[away, away, here, here, away, here, away, here, away, here, away, here, away, away],
        out_specs=[away] * 2 + [here] * (len(shapes) - 2),
        scratch_shapes=scratch,
        compiler_params=pltpu.CompilerParams(
            collective_id=0, has_side_effects=True, vmem_limit_bytes=64 * 1024 * 1024 - 65536
        ),
    )(
        tokens,
        cotangent,
        ln_gain,
        ln_bias,
        w_qkv.transpose(0, 2, 1, 3),
        b_qkv.transpose(1, 0, 2),
        w_out,
        b_out,
        w_in,
        b_in,
        w_down,
        b_down,
        jnp.asarray(cosine),
        jnp.asarray(sine),
    )
    out = pl.pallas_call(
        functools.partial(store_kernel, len(shapes)),
        out_shape=[jax.ShapeDtypeStruct(s, F32) for s in shapes],
        in_specs=[away] * 2 + [here] * (len(shapes) - 2),
        out_specs=[away] * len(shapes),
        scratch_shapes=[vm((rows, depth), F32), vm((rows, depth), F32), dma((3, 16))],
    )(*out)
    x, g, gain, bias, bqkv, bout, b_in_g, bdown, wq, wo, wi, wd = out
    return (
        x,
        g,
        gain,
        bias,
        wq.transpose(0, 2, 1, 3),
        bqkv.transpose(1, 0, 2),
        wo.transpose(0, 2, 1),
        bout,
        wi,
        b_in_g,
        wd.transpose(0, 2, 1),
        bdown,
    )


def solution(mesh):
    return jax.shard_map(
        functools.partial(on_device, mesh.shape["tensor"], mesh.shape["dp"]),
        mesh=mesh,
        in_specs=(
            P("dp", None),
            P("dp", None),
            P(),
            P(),
            P(None, None, None, "tensor"),
            P(None, None, "tensor"),
            P(None, "tensor", None),
            P(),
            P(None, None, "tensor"),
            P(None, "tensor"),
            P(None, "tensor", None),
            P(),
        ),
        out_specs=(
            P("dp", None),
            P("dp", None),
            P(),
            P(),
            P(None, "dp", None, "tensor"),
            P(None, None, "tensor"),
            P(None, "tensor", "dp"),
            P(),
            P(None, "dp", "tensor"),
            P(None, "tensor"),
            P(None, "tensor", "dp"),
            P(),
        ),
        check_vma=False,
    )
```

```python
import functools

import jax
import jax.numpy as jnp
import numpy as np
from jax import lax
from jax.experimental import pallas as pl
from jax.experimental.pallas import tpu as pltpu
from jax.sharding import PartitionSpec as P

HEAD_DIM = 64
ROT = 16
SEQ = 2048
LAYERS = 2
EPS = 1e-05
F32 = jnp.float32
BF16 = jnp.bfloat16
MESH = pl.DeviceIdType.MESH
LANES = 128
QT = 256
KT = 256
MT = 256
ST = 32
PARTS = 8


def nn(a, b):
    return jnp.dot(a, b, preferred_element_type=F32)


def nt(a, b):
    return lax.dot_general(a, b, (((1,), (1,)), ((), ())), preferred_element_type=F32)


def rope_constants():
    half = ROT // 2
    exponent = np.arange(0, ROT, 2).astype(np.float32) / np.float32(ROT)
    inverse = (np.float32(1.0) / np.float32(10000.0) ** exponent).astype(np.float32)
    angles = np.arange(SEQ).astype(np.float32)[:, None] * inverse[None, :]
    cosine = np.ones((SEQ, LANES), np.float32)
    sine = np.zeros((SEQ, LANES), np.float32)
    for start in range(0, LANES, HEAD_DIM):
        cosine[:, start : start + half] = np.cos(angles)
        cosine[:, start + half : start + ROT] = np.cos(angles)
        sine[:, start : start + half] = -np.sin(angles)
        sine[:, start + half : start + ROT] = np.sin(angles)
    return cosine, sine


def rotate(values, cosine, sine):
    half = ROT // 2
    lane = lax.broadcasted_iota(jnp.int32, values.shape, 1)
    partner = jnp.where(
        lane % HEAD_DIM < half,
        pltpu.roll(values, LANES - half, 1),
        pltpu.roll(values, half, 1),
    )
    return values * cosine + partner * sine


def head_only(values, head):
    lane = lax.broadcasted_iota(jnp.int32, values.shape, 1)
    return jnp.where(lane // HEAD_DIM == head, values, jnp.zeros_like(values))


def rows_at(step, size):
    return pl.ds(pl.multiple_of(step * size, size), size)


def remote(src, dst, send_sem, recv_sem, **device):
    return pltpu.make_async_remote_copy(
        src_ref=src,
        dst_ref=dst,
        send_sem=send_sem,
        recv_sem=recv_sem,
        device_id=device,
        device_id_type=MESH,
    )


class Refs:
    pass


def step_kernel(nt_dev, nd, *refs):
    names = (
        "tok", "cot", "gain", "bias", "wqkv_h", "bqkv", "wout_h", "bout", "win_h", "bin",
        "wdown_h", "bdown", "cos_h", "sin_h", "ox", "og", "ogain", "obias", "obqkv", "obout",
        "obin", "obdown", "oq", "oo", "oi", "od", "wqkv", "wout", "win", "wdown", "cosine",
        "sine", "x", "g", "xt", "ct", "h0", "h1", "qm", "kv", "kt", "vt", "ob", "ot", "lse",
        "u", "act", "mu", "rs", "part", "psend", "ra", "rb", "sa", "sb", "r2a", "r2b", "agbuf",
        "dz", "do", "dom", "delta", "dqt", "dkvo", "dkvi", "own", "dqkv", "du", "dact",
        "binacc", "dh0", "ge", "gl", "r1e", "r1l", "r2e", "r2l", "s3e", "s3l", "r3e", "r3l",
        "k3e", "k3l", "ln", "other", "ln1", "other1", "ln2", "other2", "lnc", "ln3", "lnall",
        "lnacc", "lsem", "kvs", "kvr", "dks", "dkr", "ars", "arr", "g1s", "g1r", "g2s", "g2r",
        "g3s", "g3r", "s1s", "s1r", "s2s", "s2r", "s3s", "s3r", "s4s", "s4r",
    )
    assert len(names) == len(refs)
    v = Refs()
    v.__dict__.update(zip(names, refs))
    rows, depth = v.x.shape
    group = SEQ // rows
    nx = nd // group
    chunk = rows // nt_dev
    grow = depth // nd
    width = v.wout.shape[1]
    ff = v.win.shape[2]

    me_t = lax.axis_index("tensor")
    me_d = lax.axis_index("dp")
    rank = lax.rem(me_d, group)
    core = lax.rem(me_d, 2)
    zlo = lax.rem(me_d // 2, 2)
    xc = me_d // group
    ny = nt_dev // 2
    hd = depth // 2
    yy = me_t // 2
    zh = lax.rem(me_t, 2)
    other_zh = me_t + 1 - 2 * zh
    other_core = me_d + 1 - 2 * core
    other_z = me_d + 2 - 4 * zlo

    barrier = pltpu.get_barrier_semaphore()
    for k in range(1, nt_dev):
        pl.semaphore_signal(
            barrier, inc=1, device_id={"tensor": lax.rem(me_t + k, nt_dev)}, device_id_type=MESH
        )
    for k in range(1, nd):
        pl.semaphore_signal(
            barrier, inc=1, device_id={"dp": lax.rem(me_d + k, nd)}, device_id_type=MESH
        )

    def load(src, dst, index):
        copy = pltpu.make_async_copy(src, dst, v.lsem.at[index])
        copy.start()
        return copy

    load_tok = load(v.tok, v.xt, 0)
    load_cos = load(v.cos_h.at[rows_at(rank, rows)], v.cosine, 1)
    load_sin = load(v.sin_h.at[rows_at(rank, rows)], v.sine, 2)
    load_qkv = []
    load_rest = []
    for l in range(LAYERS):
        load_qkv.append(
            [
                load(
                    v.wqkv_h.at[l, c],
                    v.wqkv.at[l, :, pl.ds(c * width, width)],
                    4 + 6 * l + c,
                )
                for c in range(3)
            ]
        )
        load_rest.append(
            [
                load(v.win_h.at[l], v.win.at[l], 4 + 6 * l + 3),
                load(v.wdown_h.at[l], v.wdown.at[l], 4 + 6 * l + 4),
                load(v.wout_h.at[l], v.wout.at[l], 4 + 6 * l + 5),
            ]
        )
    load_cot = load(v.cot, v.ct, 3)

    def norm_rows(l, at, x):
        mean = jnp.mean(x, axis=-1, keepdims=True)
        center = x - mean
        spread = jnp.mean(center * center, axis=-1, keepdims=True)
        r = lax.rsqrt(spread + EPS)
        xhat = center * r
        v.mu[l, at, :] = mean
        v.rs[l, at, :] = r
        v.h0[l, at, :] = (xhat * v.gain[l, 0:1, :] + v.bias[l, 0:1, :]).astype(BF16)
        v.h1[l, at, :] = (xhat * v.gain[l, 1:2, :] + v.bias[l, 1:2, :]).astype(BF16)

    def stream_rows(l, at):
        if l == 0:
            return v.xt[at, :].astype(F32)
        return v.x[at, :]

    def at_y(k):
        return lax.rem(yy + k, ny)

    def copy_of(s, src, dst, sem, to):
        return remote(src, dst, v.ars.at[s, sem], v.arr.at[s, sem], tensor=to)

    def a1(s, k):
        to = at_y(k)
        return copy_of(
            s, v.psend.at[s, 0, pl.ds(2 * to, 2)], v.ra.at[s, k - 1], k - 1, 2 * to + zh
        )

    def b1(s, m):
        to = at_y(m)
        return copy_of(
            s, v.psend.at[s, 1, 2 * to + 1 - zh], v.rb.at[s, to], ny - 2 + m, other_zh
        )

    def a2(s):
        return copy_of(s, v.sa.at[s], v.r2a.at[s], 2 * ny - 1, other_zh)

    def b2(s, k):
        return copy_of(
            s, v.sb.at[s, k - 1], v.r2b.at[s, k - 1], 2 * ny - 1 + k, 2 * at_y(k) + zh
        )

    def rs_pair(s, m):
        b1(s, m).start()

        @pl.when(m < ny)
        def _():
            a1(s, m).start()

    def rs_forward(s):
        for m in range(1, ny):
            b1(s, m).wait_recv()
            to = at_y(m)
            v.sb[s, m - 1] = (
                v.psend[s, 1, 2 * to + zh].astype(F32) + v.rb[s, to].astype(F32)
            ).astype(BF16)
            b2(s, m).start()
        for k in range(1, ny):
            a1(s, k).wait_recv()
        total = v.psend[s, 0, other_zh].astype(F32)
        for k in range(1, ny):
            total = total + v.ra[s, k - 1, 1 - zh].astype(F32)
        v.sa[s] = total.astype(BF16)
        a2(s).start()
        b1(s, ny).wait_recv()

    def rs_finish(s):
        a2(s).wait()
        for k in range(1, ny):
            b2(s, k).wait()
            a1(s, k).wait_send()
        for m in range(1, ny + 1):
            b1(s, m).wait_send()

    def rs_sum(s, at):
        first = v.psend[s, 0, me_t, at, :].astype(F32) + v.r2a[s, at, :].astype(F32)
        second = v.psend[s, 1, me_t, at, :].astype(F32) + v.rb[s, yy, at, :].astype(F32)
        for k in range(1, ny):
            first = first + v.ra[s, k - 1, zh, at, :].astype(F32)
            second = second + v.r2b[s, k - 1, at, :].astype(F32)
        return jnp.concatenate([first, second], axis=1)

    def ag_copy(s, half, chunk_at, sem, to):
        block = v.agbuf.at[s, half, chunk_at]
        return copy_of(s, block, block, sem, to)

    ag0 = 3 * ny - 1

    def gz(s):
        return ag_copy(s, 0, me_t, ag0, other_zh)

    def gy(s, k):
        return ag_copy(s, 0, me_t, ag0 + k, 2 * at_y(k) + zh)

    def fy(s, k):
        return ag_copy(s, 0, other_zh, ag0 + ny - 1 + k, 2 * at_y(k) + zh)

    def by(s, k):
        return ag_copy(s, 1, me_t, ag0 + 2 * ny - 2 + k, 2 * at_y(k) + zh)

    def bz(s, m):
        return ag_copy(s, 1, 2 * at_y(m) + zh, ag0 + 3 * ny - 2 + m, other_zh)

    def arrived(s, half, chunk_at, sem):
        ag_copy(s, half, chunk_at, sem, other_zh).wait_recv()

    def ag_put(s, at, value):
        v.agbuf[s, 0, me_t, at, :] = value[:, :hd].astype(BF16)
        v.agbuf[s, 1, me_t, at, :] = value[:, hd:].astype(BF16)

    def ag_start(s):
        gz(s).start()
        for k in range(1, ny):
            by(s, k).start()
        bz(s, 0).start()
        for k in range(1, ny):
            gy(s, k).start()

    def ag_forward(s):
        arrived(s, 0, other_zh, ag0)
        for k in range(1, ny):
            fy(s, k).start()
        for k in range(1, ny):
            arrived(s, 1, 2 * at_y(ny - k) + zh, ag0 + 2 * ny - 2 + k)
            bz(s, ny - k).start()

    def ag_pairs(s, first, last, use, after):
        def one(m, carry):
            pair = at_y(m)

            @pl.when(m > 0)
            def _():
                arrived(s, 0, 2 * pair + zh, ag0 + ny - m)
                arrived(s, 0, 2 * pair + 1 - zh, ag0 + 2 * ny - 1 - m)

            arrived(s, 1, 2 * pair + 1 - zh, ag0 + 3 * ny - 2 + m)
            for i in range(2):
                src = 2 * pair + i
                for j in range(chunk // ST):
                    at = slice(j * ST, (j + 1) * ST)
                    use(
                        pl.ds(pl.multiple_of(src * chunk + j * ST, ST), ST),
                        jnp.concatenate(
                            [v.agbuf[s, 0, src, at, :], v.agbuf[s, 1, src, at, :]], axis=1
                        ).astype(F32),
                    )
            after(rows_at(pair, 2 * chunk))
            return carry

        lax.fori_loop(first, last, one, 0)

    def ag_sent(s):
        gz(s).wait_send()
        bz(s, 0).wait_send()
        for k in range(1, ny):
            gy(s, k).wait_send()
            fy(s, k).wait_send()
            by(s, k).wait_send()
            bz(s, k).wait_send()

    def kv_copy(l, step):
        slot, to = [(rank, other_core), (rank, other_z), (rank - 2, other_core)][step]
        block = v.kv.at[l, slot]
        return remote(block, block, v.kvs.at[l, step], v.kvr.at[l, step], dp=to)

    def kv_in(l, step):
        slot = [rank - 1, rank - 2, rank - 1 - 2 * core][step]
        block = v.kv.at[l, slot]
        return remote(block, block, v.kvs.at[l, step], v.kvr.at[l, step], dp=other_core)

    def dkv_copy(l, step):
        return remote(
            v.dkvo.at[l, step],
            v.dkvi.at[l, step],
            v.dks.at[l, step],
            v.dkr.at[l, step],
            dp=other_z if step == 1 else other_core,
        )

    def transpose_block(l, b):
        block = v.kv[l, b].astype(F32)
        v.kt[l, b] = block[:, :width].T.astype(BF16)
        v.vt[l, b] = block[:, width:].T.astype(BF16)

    def qkv_rows(l, at, size):
        mixed = nn(v.h0[l, at, :], v.wqkv[l])
        cosine, sine = v.cosine[at, :], v.sine[at, :]
        q = rotate(mixed[:, :width] + v.bqkv[0, l : l + 1, :], cosine, sine).astype(BF16)
        k = rotate(mixed[:, width : 2 * width] + v.bqkv[1, l : l + 1, :], cosine, sine)
        val = mixed[:, 2 * width :] + v.bqkv[2, l : l + 1, :]
        scaled = (q.astype(F32) * 0.125).astype(BF16)
        v.qm[l, 0, at, :] = head_only(scaled, 0)
        v.qm[l, 1, at, :] = head_only(scaled, 1)
        v.kv[l, rank, at, :width] = k.astype(BF16)
        v.kv[l, rank, at, width:] = val.astype(BF16)

    def kv_send(l):
        @pl.when(zlo == 0)
        def _():
            kv_copy(l, 1).start()

        @pl.when(core == 0)
        def _():
            kv_copy(l, 0).start()

    def kv_relay(l):
        @pl.when(zlo == 1)
        def _():
            kv_in(l, 1).wait_recv()
            kv_copy(l, 2).start()

    def kv_finish(l):
        transpose_block(l, rank)

        @pl.when(core == 1)
        def _():
            kv_in(l, 0).wait_recv()
            transpose_block(l, rank - 1)

        @pl.when(zlo == 1)
        def _():
            transpose_block(l, rank - 2)
            kv_in(l, 2).wait_recv()
            transpose_block(l, rank - 1 - 2 * core)

    def feed_forward(l):
        for c in load_rest[l]:
            c.wait()

        def up(i, carry):
            at = rows_at(i, MT)
            v.u[l, at, :] = nn(v.h1[l, at, :], v.win[l]) + v.bin[l : l + 1, :]
            return carry

        lax.fori_loop(0, rows // MT, up, 0)

        def activate(i, carry):
            at = rows_at(i, ST)
            u = v.u[l, at, :]
            v.act[l, at, :] = (0.5 * u * (1.0 + lax.erf(u * np.float32(0.5**0.5)))).astype(BF16)
            return carry

        lax.fori_loop(0, rows // ST, activate, 0)

        def down(i, carry):
            at = rows_at(i, MT)
            v.part[at, :] = nn(v.act[l, at, :], v.wdown[l])
            return carry

        lax.fori_loop(0, rows // MT, down, 0)

    def attention(l, s):
        for qt in range(rows // QT):
            q_at = slice(qt * QT, (qt + 1) * QT)
            head_rows = [slice(h * HEAD_DIM, (h + 1) * HEAD_DIM) for h in range(2)]

            def block(b, carry, masked):
                keys = v.kv[l, b, :, :width]
                scores = [nt(keys, v.qm[l, h, q_at, :]) for h in range(2)]
                result = []
                for h in range(2):
                    top, total, out = carry[h]
                    sc = scores[h]
                    if masked:
                        key = lax.broadcasted_iota(jnp.int32, sc.shape, 0)
                        query = lax.broadcasted_iota(jnp.int32, sc.shape, 1) + qt * QT
                        sc = jnp.where(key <= query, sc, -1e30)
                    new = jnp.maximum(top, jnp.max(sc, axis=0, keepdims=True))
                    p = jnp.exp(sc - new)
                    fade = jnp.exp(top - new)
                    total = total * fade + jnp.sum(p, axis=0, keepdims=True)
                    out = out * fade + nn(v.vt[l, b, head_rows[h], :], p.astype(BF16))
                    result.append((new, total, out))
                return tuple(result)

            start = (
                jnp.full((1, QT), -1e30, F32),
                jnp.zeros((1, QT), F32),
                jnp.zeros((HEAD_DIM, QT), F32),
            )
            carry = lax.fori_loop(0, rank, functools.partial(block, masked=False), (start, start))
            carry = block(rank, carry, True)
            for h in range(2):
                top, total, out = carry[h]
                v.ot[l, head_rows[h], q_at] = out / total
                v.lse[l, h : h + 1, q_at] = top + jnp.log(total)
            v.ob[l, q_at, :] = v.ot[l, :, q_at].T.astype(BF16)
            both = nn(v.ob[l, q_at, :], v.wout[l]) + v.part[q_at, :]
            both = both.astype(BF16)
            first = qt * QT // chunk
            for half in range(2):
                v.psend[s, half, first : first + QT // chunk] = both[
                    :, half * hd : (half + 1) * hd
                ].reshape(QT // chunk, chunk, hd)
            for pair in range(first // 2, (first + QT // chunk) // 2):
                rs_pair(s, lax.rem(pair - yy - 1 + 2 * ny, ny) + 1)

    def branch_reduce(s):
        rs_finish(s)
        for i in range(chunk // 16):
            at = slice(i * 16, (i + 1) * 16)
            ag_put(s, at, rs_sum(s, at))
        ag_start(s)

    grads = {0: (v.ge, v.r1e, v.r2e, v.s3e, v.r3e, v.k3e), 1: (v.gl, v.r1l, v.r2l, v.s3l, v.r3l, v.k3l)}

    def core_copy(l, p):
        g, r1 = grads[p][:2]
        return remote(
            g.at[l, 1 - core], r1.at[l], v.g1s.at[l, p], v.g1r.at[l, p], dp=other_core
        )

    def x_copy(l, p, k):
        r1, r2 = grads[p][1:3]
        to = lax.rem(xc + k, nx)
        return remote(
            r1.at[l, pl.ds(2 * to, 2)],
            r2.at[l, k - 1],
            v.g2s.at[l, p, k - 1],
            v.g2r.at[l, p, k - 1],
            dp=to * group + zlo * 2 + core,
        )

    def z_copy(l, p):
        return remote(
            grads[p][3].at[l], grads[p][4].at[l], v.g3s.at[l, p], v.g3r.at[l, p], dp=other_z
        )

    def grad_core(l, p):
        core_copy(l, p).start()

    def grad_x(l, p):
        core_copy(l, p).wait()
        g, r1 = grads[p][:2]

        def one(i, carry):
            for j in range(grow // 16):
                at = slice(j * 16, (j + 1) * 16)
                r1[l, i, at, :] = (
                    r1[l, i, at, :].astype(F32) + g[l, core, i, at, :].astype(F32)
                ).astype(BF16)
            return carry

        lax.fori_loop(0, nd // 2, one, 0)
        for k in range(1, nx):
            x_copy(l, p, k).start()

    def grad_z(l, p):
        _, r1, r2, s3, r3, k3 = grads[p]
        for k in range(1, nx):
            x_copy(l, p, k).wait()

        def total(z, at):
            value = r1[l, 2 * xc + z, at, :].astype(F32)
            for k in range(1, nx):
                value = value + r2[l, k - 1, z, at, :].astype(F32)
            return value

        for j in range(grow // 16):
            at = slice(j * 16, (j + 1) * 16)
            s3[l, at, :] = total(1 - zlo, at).astype(BF16)
        z_copy(l, p).start()
        for j in range(grow // 16):
            at = slice(j * 16, (j + 1) * 16)
            k3[l, at, :] = total(zlo, at)

    def grad_end(l, p):
        z_copy(l, p).wait()
        _, _, _, _, r3, k3 = grads[p]
        for j in range(grow // 16):
            at = slice(j * 16, (j + 1) * 16)
            total = k3[l, at, :] + r3[l, at, :].astype(F32)
            if p == 0:
                v.oo[l, at, :] = total[:, :width]
                v.od[l, at, :] = total[:, width : width + ff]
                v.oi[l, at, :] = total[:, width + ff :]
            else:
                for c in range(3):
                    v.oq[l, c, at, :] = total[:, c * width : (c + 1) * width]

    def start_gradient(l, at, gradient):
        v.dz[at, :] = gradient.astype(BF16)

    def attention_back(l):
        do = v.do[...]
        product = do.astype(F32).T * v.ot[l]
        v.delta[0:1, :] = jnp.sum(product[:HEAD_DIM], axis=0, keepdims=True)
        v.delta[1:2, :] = jnp.sum(product[HEAD_DIM:], axis=0, keepdims=True)
        v.dqt[...] = jnp.zeros_like(v.dqt)

        def piece(b, i, masked):
            at = rows_at(i, KT)
            keys = v.kv[l, b, at, :width]
            values = v.kv[l, b, at, width:]
            dk = jnp.zeros((KT, width), F32)
            dv = jnp.zeros((KT, width), F32)
            for h in range(2):
                head_rows = slice(h * HEAD_DIM, (h + 1) * HEAD_DIM)
                sc = nt(keys, v.qm[l, h])
                if masked:
                    key = lax.broadcasted_iota(jnp.int32, sc.shape, 0) + i * KT
                    query = lax.broadcasted_iota(jnp.int32, sc.shape, 1)
                    sc = jnp.where(key <= query, sc, -1e30)
                p = jnp.exp(sc - v.lse[l, h : h + 1, :])
                dp = nt(values, v.dom[h])
                ds = (p * (dp - v.delta[h : h + 1, :])).astype(BF16)
                dv = dv + nn(p.astype(BF16), v.dom[h])
                dk = dk + nn(ds, v.qm[l, h])
                v.dqt[head_rows, :] += nn(v.kt[l, b, head_rows, at], ds)
            return dk, dv

        def far(b, slot, received):
            def inner(i, c):
                dk, dv = piece(b, i, False)
                at = rows_at(i, KT)
                if received:
                    dk = dk + v.dkvi[l, 0, at, :width].astype(F32)
                    dv = dv + v.dkvi[l, 0, at, width:].astype(F32)
                v.dkvo[l, slot, at, :width] = dk.astype(BF16)
                v.dkvo[l, slot, at, width:] = dv.astype(BF16)
                return c

            lax.fori_loop(0, rows // KT, inner, 0)
            dkv_copy(l, slot).start()

        @pl.when(zlo == 1)
        def _():
            far(1 - core, 0, False)
            dkv_copy(l, 0).wait_recv()
            far(core, 1, True)

        @pl.when(core == 1)
        def _():
            far(rank - 1, 2, False)

        def near(i, c):
            dk, dv = piece(rank, i, True)
            at = rows_at(i, KT)
            v.own[at, :width] = dk
            v.own[at, width:] = dv
            return c

        lax.fori_loop(0, rows // KT, near, 0)

    def back_rows(l, at, size):
        do = nt(v.dz[at, :], v.wout[l]).astype(BF16)
        v.do[at, :] = do
        v.dom[0, at, :] = head_only(do, 0)
        v.dom[1, at, :] = head_only(do, 1)
        v.dact[at, :] = nt(v.dz[at, :], v.wdown[l])
        start = at.start if isinstance(at, pl.Slice) else at

        def slope(i, acc):
            rows_now = pl.ds(pl.multiple_of(start + i * ST, ST), ST)
            u = v.u[l, rows_now, :]
            inner = 0.5 * (1.0 + lax.erf(u * np.float32(0.5**0.5)))
            inner = inner + u * jnp.exp(-0.5 * u * u) * np.float32((2.0 * np.pi) ** -0.5)
            du = (v.dact[rows_now, :] * inner).astype(BF16)
            v.du[rows_now, :] = du
            return acc + jnp.sum(du.astype(F32).reshape(ST // 8, 8, ff), axis=0)

        v.binacc[l] += lax.fori_loop(0, size // ST, slope, jnp.zeros((8, ff), F32))
        v.part[at, :] = nt(v.du[at, :], v.win[l])

    def early_grads(l):
        def one(i, carry):
            at = rows_at(i, 2 * grow)
            dzt = v.dz[:, at].astype(F32).T.astype(BF16)
            ht = v.h1[l, :, at].astype(F32).T.astype(BF16)
            wo = nn(dzt, v.ob[l]).astype(BF16)
            wd = nn(dzt, v.act[l]).astype(BF16)
            wi = nn(ht, v.du[...]).astype(BF16)
            for c in range(2):
                part = slice(c * grow, (c + 1) * grow)
                v.ge[l, c, i, :, :width] = wo[part]
                v.ge[l, c, i, :, width : width + ff] = wd[part]
                v.ge[l, c, i, :, width + ff :] = wi[part]
            return carry

        lax.fori_loop(0, depth // (2 * grow), one, 0)

    def late_grads(l):
        def one(i, carry):
            at = rows_at(i, 2 * grow)
            ht = v.h0[l, :, at].astype(F32).T.astype(BF16)
            wq = nn(ht, v.dqkv[...]).astype(BF16)
            for c in range(2):
                v.gl[l, c, i] = wq[c * grow : (c + 1) * grow]
            return carry

        lax.fori_loop(0, depth // (2 * grow), one, 0)

    def qkv_back(l):
        for step, here in ((2, core == 0), (1, zlo == 0)):

            @pl.when(here)
            def _():
                dkv_copy(l, step).wait_recv()
                v.own[...] += v.dkvi[l, step].astype(F32)

        cosine, sine = v.cosine[...], -v.sine[...]
        v.dqkv[:, :width] = rotate(v.dqt[...].T * 0.125, cosine, sine).astype(BF16)
        v.dqkv[:, width : 2 * width] = rotate(v.own[:, :width], cosine, sine).astype(BF16)
        v.dqkv[:, 2 * width : 3 * width] = v.own[:, width:].astype(BF16)
        v.other[4 * l + 3 : 4 * l + 4, : 3 * width] = jnp.sum(
            v.dqkv[...].astype(F32), axis=0, keepdims=True
        )

        def one(i, carry):
            at = rows_at(i, MT)
            v.dh0[at, :] = nt(v.dqkv[at, :], v.wqkv[l])
            return carry

        lax.fori_loop(0, rows // MT, one, 0)

        def send(m, carry):
            pair = at_y(m)
            for i in range(2 * chunk // ST):
                at = pl.ds(pl.multiple_of(pair * 2 * chunk + i * ST, ST), ST)
                both = v.dh0[at, :] * v.gain[l, 0:1, :] + v.part[at, :] * v.gain[l, 1:2, :]
                both = both.astype(BF16)
                part = slice(i * ST % chunk, i * ST % chunk + ST)
                for half in range(2):
                    v.psend[0, half, 2 * pair + i * ST // chunk, part, :] = both[
                        :, half * hd : (half + 1) * hd
                    ]
            rs_pair(0, m)
            return carry

        lax.fori_loop(1, ny + 1, send, 0)

    def norm_grads(l):
        v.lnacc[...] = jnp.zeros_like(v.lnacc)

        def fold(value):
            return jnp.sum(value.reshape(2, 8, depth), axis=0)

        def one(i, carry):
            at = rows_at(i, 16)
            xhat = (stream_rows(l, at) - v.mu[l, at, :]) * v.rs[l, at, :]
            first, second = v.dh0[at, :], v.part[at, :]
            v.lnacc[0] += fold(first * xhat)
            v.lnacc[1] += fold(second * xhat)
            v.lnacc[2] += fold(first)
            v.lnacc[3] += fold(second)
            v.lnacc[4] += fold(v.dz[at, :].astype(F32))
            return carry

        lax.fori_loop(0, rows // 16, one, 0)
        for i in range(4):
            v.ln[4 * l + i : 4 * l + i + 1, :] = jnp.sum(v.lnacc[i], axis=0, keepdims=True)
        column = jnp.sum(v.lnacc[4], axis=0, keepdims=True)
        v.other[4 * l : 4 * l + 1, :] = column[:, :ff]
        v.other[4 * l + 1 : 4 * l + 2, :] = column[:, ff:]
        v.other[4 * l + 2 : 4 * l + 3, :] = jnp.sum(v.binacc[l], axis=0, keepdims=True)

    def stream_reduce(l):
        rs_finish(0)
        for i in range(chunk // 16):
            at = pl.ds(pl.multiple_of(me_t * chunk + i * 16, 16), 16)
            gd = rs_sum(0, slice(i * 16, (i + 1) * 16))
            r = v.rs[l, at, :]
            xhat = (stream_rows(l, at) - v.mu[l, at, :]) * r
            mean = jnp.mean(gd, axis=-1, keepdims=True)
            along = jnp.mean(gd * xhat, axis=-1, keepdims=True)
            dx = r * (gd - mean - xhat * along)
            ag_put(0, slice(i * 16, (i + 1) * 16), dx)
        ag_start(0)

    def small_core(i):
        mine, theirs = [(v.ln, v.ln1), (v.other, v.other1)][i]
        return remote(mine, theirs, v.s1s.at[i], v.s1r.at[i], dp=other_core)

    def small_scatter(k):
        to = lax.rem(me_t + k, nt_dev)
        columns = pl.ds(pl.multiple_of(to * LANES, LANES), LANES)
        return remote(
            v.ln.at[:, columns], v.ln2.at[k - 1], v.s2s.at[k - 1], v.s2r.at[k - 1], tensor=to
        )

    def small_dp(k, i):
        to = lax.rem(me_d + 2 * k, nd)
        mine, theirs = [(v.lnc, v.ln3), (v.other, v.other2)][i]
        return remote(mine, theirs.at[k - 1], v.s3s.at[i, k - 1], v.s3r.at[i, k - 1], dp=to)

    def small_gather(k):
        to = lax.rem(me_t + k, nt_dev)
        block = v.lnall.at[me_t]
        return remote(block, block, v.s4s.at[k - 1], v.s4r.at[me_t], tensor=to)

    def small_start():
        for i in range(2):
            small_core(i).start()

    def small_second():
        for i in range(2):
            small_core(i).wait()
        v.ln[...] += v.ln1[...]
        v.other[...] += v.other1[...]
        for k in range(1, nt_dev):
            small_scatter(k).start()
        for k in range(1, nd // 2):
            small_dp(k, 1).start()

    def small_third():
        mine = pl.ds(pl.multiple_of(me_t * LANES, LANES), LANES)
        total = v.ln[:, mine]
        for k in range(1, nt_dev):
            small_scatter(k).wait()
            total = total + v.ln2[k - 1]
        v.lnc[...] = total
        for k in range(1, nd // 2):
            small_dp(k, 0).start()

    def small_fourth():
        total = v.lnc[...]
        for k in range(1, nd // 2):
            small_dp(k, 0).wait()
            total = total + v.ln3[k - 1]
        v.lnall[me_t] = total
        for k in range(1, nt_dev):
            small_gather(k).start()
        total = v.other[...]
        for k in range(1, nd // 2):
            small_dp(k, 1).wait()
            total = total + v.other2[k - 1]
        for l in range(LAYERS):
            for half in range(2):
                at = slice(half * ff, (half + 1) * ff)
                row = total[4 * l + half : 4 * l + half + 1, :]
                v.obout[l : l + 1, at] = row
                v.obdown[l : l + 1, at] = row
            v.obin[l : l + 1, :] = total[4 * l + 2 : 4 * l + 3, :]
            for c in range(3):
                at = slice(c * width, (c + 1) * width)
                v.obqkv[c, l : l + 1, :] = total[4 * l + 3 : 4 * l + 4, at]

    def small_end():
        for k in range(1, nt_dev):
            src = lax.rem(me_t + k, nt_dev)
            block = v.lnall.at[src]
            remote(block, block, v.s4s.at[k - 1], v.s4r.at[src], tensor=src).wait()
        for j in range(nt_dev):
            at = slice(j * LANES, (j + 1) * LANES)
            block = v.lnall[j]
            for l in range(LAYERS):
                v.ogain[l, :, at] = block[4 * l : 4 * l + 2, :]
                v.obias[l, :, at] = block[4 * l + 2 : 4 * l + 4, :]

    def nothing(at):
        pass

    with jax.named_scope("tok"):
        load_tok.wait()

    def first_norm(i, carry):
        at = rows_at(i, ST)
        norm_rows(0, at, v.xt[at, :].astype(F32))
        return carry

    with jax.named_scope("norm0"):
        lax.fori_loop(0, rows // ST, first_norm, 0, unroll=2)
    with jax.named_scope("qkv0"):
        for c in load_qkv[0]:
            c.wait()
        load_cos.wait()
        load_sin.wait()

        def first_qkv(i, carry):
            qkv_rows(0, rows_at(i, MT), MT)
            return carry

        lax.fori_loop(0, rows // MT, first_qkv, 0)
    with jax.named_scope("barrier"):
        pl.semaphore_wait(barrier, nt_dev - 1 + nd - 1)
    kv_send(0)
    v.ln[...] = jnp.zeros_like(v.ln)
    v.other[...] = jnp.zeros_like(v.other)
    v.binacc[...] = jnp.zeros_like(v.binacc)
    with jax.named_scope("ffn0"):
        feed_forward(0)
    with jax.named_scope("kv0"):
        kv_relay(0)
        kv_finish(0)
    with jax.named_scope("attn0"):
        attention(0, 0)
    with jax.named_scope("forward0"):
        rs_forward(0)
    with jax.named_scope("reduce0"):
        branch_reduce(0)

    def next_stream(at, z):
        x = v.xt[at, :].astype(F32) + (z + (v.bout[0:1, :] + v.bdown[0:1, :]))
        v.x[at, :] = x
        norm_rows(1, at, x)

    def next_qkv(at):
        qkv_rows(1, at, 2 * chunk)

    with jax.named_scope("gather0"):
        for c in load_qkv[1]:
            c.wait()
        ag_forward(0)
        ag_pairs(0, 0, ny, next_stream, next_qkv)
        kv_send(1)
        ag_sent(0)
    with jax.named_scope("ffn1"):
        feed_forward(1)
    with jax.named_scope("kv1"):
        kv_relay(1)
        kv_finish(1)
    with jax.named_scope("attn1"):
        attention(1, 1)

    with jax.named_scope("dz1"):
        load_cot.wait()

        def first_gradient(i, carry):
            at = rows_at(i, ST)
            v.dz[at, :] = v.ct[at, :]
            v.g[at, :] = v.ct[at, :].astype(F32)
            return carry

        lax.fori_loop(0, rows // ST, first_gradient, 0)

    with jax.named_scope("back1"):

        def first_back(i, carry):
            back_rows(1, rows_at(i, MT), MT)
            return carry

        lax.fori_loop(0, rows // MT, first_back, 0)
    with jax.named_scope("attn_grad1"):
        attention_back(1)

    def early(l, z):
        @pl.when(zlo == z)
        def _():
            early_grads(l)
            grad_core(l, 0)

    with jax.named_scope("forward1"):
        rs_forward(1)
    with jax.named_scope("early1"):
        early(1, 0)
    with jax.named_scope("qkv_grad1"):
        qkv_back(1)
    with jax.named_scope("early1b"):
        early(1, 1)
    with jax.named_scope("late1"):
        late_grads(1)
        grad_core(1, 1)
    with jax.named_scope("forward"):
        rs_forward(0)
    with jax.named_scope("norm_grad1"):
        norm_grads(1)
    with jax.named_scope("gx10"):
        grad_x(1, 0)
    with jax.named_scope("stream_reduce1"):
        stream_reduce(1)
    with jax.named_scope("gx11"):
        grad_x(1, 1)

    def next_gradient(at, dx):
        gradient = v.g[at, :] + dx
        v.g[at, :] = gradient
        v.dz[at, :] = gradient.astype(BF16)

    def next_back(at):
        back_rows(0, at, 2 * chunk)

    with jax.named_scope("gather2"):
        ag_forward(0)
        ag_pairs(0, 0, ny, next_gradient, next_back)
        ag_sent(0)
    with jax.named_scope("reduce1"):
        branch_reduce(1)
    with jax.named_scope("attn_grad0"):
        attention_back(0)
    with jax.named_scope("forward1b"):
        ag_forward(1)
    with jax.named_scope("gz1"):
        grad_z(1, 0)
        grad_z(1, 1)
    with jax.named_scope("early0"):
        early(0, 0)
    with jax.named_scope("qkv_grad0"):
        qkv_back(0)
    with jax.named_scope("early0b"):
        early(0, 1)
    with jax.named_scope("late0"):
        late_grads(0)
        grad_core(0, 1)
    with jax.named_scope("forward"):
        rs_forward(0)
    with jax.named_scope("norm_grad0"):
        norm_grads(0)
        small_start()
    with jax.named_scope("gx00"):
        grad_x(0, 0)

    def last_stream(at, z):
        v.x[at, :] = v.x[at, :] + (z + (v.bout[1:2, :] + v.bdown[1:2, :]))

    store_x = pltpu.make_async_copy(v.x, v.ox, v.lsem.at[0])
    store_g = pltpu.make_async_copy(v.g, v.og, v.lsem.at[1])
    with jax.named_scope("small_second"):
        small_second()
    with jax.named_scope("stream_reduce0"):
        stream_reduce(0)
    with jax.named_scope("gx01"):
        grad_x(0, 1)
    with jax.named_scope("small_third"):
        small_third()
    with jax.named_scope("gather1"):
        ag_pairs(1, 0, ny, last_stream, nothing)
        ag_sent(1)
        store_x.start()
    with jax.named_scope("gend1"):
        grad_end(1, 0)
        grad_end(1, 1)

    def last_gradient(at, dx):
        v.g[at, :] = v.g[at, :] + dx

    with jax.named_scope("gather3"):
        ag_forward(0)
        ag_pairs(0, 0, ny // 2, last_gradient, nothing)
    with jax.named_scope("small_fourth"):
        small_fourth()
    with jax.named_scope("gather3b"):
        ag_pairs(0, ny // 2, ny, last_gradient, nothing)
        store_g.start()
        ag_sent(0)
    with jax.named_scope("gz0"):
        grad_z(0, 0)
        grad_z(0, 1)
    with jax.named_scope("small_end"):
        small_end()
    with jax.named_scope("gend0"):
        grad_end(0, 0)
        grad_end(0, 1)
        store_x.wait()
        store_g.wait()
    for l in range(LAYERS):
        for step, here in ((0, core == 0), (1, zlo == 0), (2, zlo == 1)):

            @pl.when(here)
            def _():
                kv_copy(l, step).wait_send()

        for step, here in ((0, zlo == 1), (1, zlo == 1), (2, core == 1)):

            @pl.when(here)
            def _():
                dkv_copy(l, step).wait_send()


def store_kernel(count, *refs):
    given, kept = refs[:count], refs[count : 2 * count]
    held = refs[2 * count : 2 * count + 2]
    sems = refs[2 * count + 2]
    rows = held[0].shape[0] // PARTS
    parts = [(i, slice(j * rows, (j + 1) * rows), i * PARTS + j) for j in range(PARTS) for i in range(2)]
    loads = [
        pltpu.make_async_copy(given[i].at[at], held[i].at[at], sems.at[0, n]) for i, at, n in parts
    ]
    stores = [
        pltpu.make_async_copy(held[i].at[at], kept[i].at[at], sems.at[1, n]) for i, at, n in parts
    ]
    others = [
        pltpu.make_async_copy(given[i], kept[i], sems.at[2, i]) for i in range(2, count)
    ]
    for copy in loads + others:
        copy.start()
    for load, store in zip(loads, stores):
        load.wait()
        store.start()
    for copy in stores + others:
        copy.wait()


def on_device(nt_dev, nd, *args):
    tokens, cotangent, ln_gain, ln_bias, w_qkv, b_qkv, w_out, b_out, w_in, b_in, w_down, b_down = args
    rows, depth = tokens.shape
    width = w_out.shape[1]
    ff = w_in.shape[2]
    group = SEQ // rows
    chunk = rows // nt_dev
    grow = depth // nd
    half = nd // 2
    nx = nd // group
    early = width + 2 * ff
    late = 3 * width
    cosine, sine = rope_constants()
    vm = pltpu.VMEM
    dma = pltpu.SemaphoreType.DMA
    two = LAYERS
    scratch = [
        vm((two, depth, 3 * width), BF16),
        vm((two, width, depth), BF16),
        vm((two, depth, ff), BF16),
        vm((two, ff, depth), BF16),
        vm((rows, LANES), F32),
        vm((rows, LANES), F32),
        vm((rows, depth), F32),
        vm((rows, depth), F32),
        vm((rows, depth), BF16),
        vm((rows, depth), BF16),
        vm((two, rows, depth), BF16),
        vm((two, rows, depth), BF16),
        vm((two, 2, rows, width), BF16),
        vm((two, group, rows, 2 * width), BF16),
        vm((two, group, width, rows), BF16),
        vm((two, group, width, rows), BF16),
        vm((two, rows, width), BF16),
        vm((two, width, rows), F32),
        vm((two, 8, rows), F32),
        vm((two, rows, ff), F32),
        vm((two, rows, ff), BF16),
        vm((two, rows, 1), F32),
        vm((two, rows, 1), F32),
        vm((rows, depth), F32),
        vm((2, 2, nt_dev, chunk, depth // 2), BF16),
        vm((2, nt_dev // 2 - 1, 2, chunk, depth // 2), BF16),
        vm((2, nt_dev // 2, chunk, depth // 2), BF16),
        vm((2, chunk, depth // 2), BF16),
        vm((2, nt_dev // 2 - 1, chunk, depth // 2), BF16),
        vm((2, chunk, depth // 2), BF16),
        vm((2, nt_dev // 2 - 1, chunk, depth // 2), BF16),
        vm((2, 2, nt_dev, chunk, depth // 2), BF16),
        vm((rows, depth), BF16),
        vm((rows, width), BF16),
        vm((2, rows, width), BF16),
        vm((8, rows), F32),
        vm((width, rows), F32),
        vm((two, 3, rows, 2 * width), BF16),
        vm((two, 3, rows, 2 * width), BF16),
        vm((rows, 2 * width), F32),
        vm((rows, 3 * width), BF16),
        vm((rows, ff), BF16),
        vm((rows, ff), F32),
        vm((two, 8, ff), F32),
        vm((rows, depth), F32),
        vm((two, 2, half, grow, early), BF16),
        vm((two, 2, half, grow, late), BF16),
        vm((two, half, grow, early), BF16),
        vm((two, half, grow, late), BF16),
        vm((two, nx - 1, 2, grow, early), BF16),
        vm((two, nx - 1, 2, grow, late), BF16),
        vm((two, grow, early), BF16),
        vm((two, grow, late), BF16),
        vm((two, grow, early), BF16),
        vm((two, grow, late), BF16),
        vm((two, grow, early), F32),
        vm((two, grow, late), F32),
        vm((8, depth), F32),
        vm((8, ff), F32),
        vm((8, depth), F32),
        vm((8, ff), F32),
        vm((nt_dev - 1, 8, LANES), F32),
        vm((half - 1, 8, ff), F32),
        vm((8, LANES), F32),
        vm((half - 1, 8, LANES), F32),
        vm((nt_dev, 8, LANES), F32),
        vm((5, 8, depth), F32),
        dma((16,)),
        dma((two, 3)),
        dma((two, 3)),
        dma((two, 3)),
        dma((two, 3)),
        dma((2, 7 * (nt_dev // 2) - 3)),
        dma((2, 7 * (nt_dev // 2) - 3)),
        dma((two, 2)),
        dma((two, 2)),
        dma((two, 2, nx - 1)),
        dma((two, 2, nx - 1)),
        dma((two, 2)),
        dma((two, 2)),
        dma((2,)),
        dma((2,)),
        dma((nt_dev - 1,)),
        dma((nt_dev - 1,)),
        dma((2, half - 1)),
        dma((2, half - 1)),
        dma((nt_dev - 1,)),
        dma((nt_dev,)),
    ]
    here = pl.BlockSpec(memory_space=pltpu.VMEM)
    away = pl.BlockSpec(memory_space=pl.ANY)
    shapes = [
        (rows, depth),
        (rows, depth),
        (two, 2, depth),
        (two, 2, depth),
        (3, two, width),
        (two, depth),
        (two, ff),
        (two, depth),
        (two, 3, grow, width),
        (two, grow, width),
        (two, grow, ff),
        (two, grow, ff),
    ]
    out = pl.pallas_call(
        functools.partial(step_kernel, nt_dev, nd),
        out_shape=[jax.ShapeDtypeStruct(s, F32) for s in shapes],
        in_specs=[away, away, here, here, away, here, away, here, away, here, away, here, away, away],
        out_specs=[away] * 2 + [here] * (len(shapes) - 2),
        scratch_shapes=scratch,
        compiler_params=pltpu.CompilerParams(
            collective_id=0, has_side_effects=True, vmem_limit_bytes=64 * 1024 * 1024 - 65536
        ),
    )(
        tokens,
        cotangent,
        ln_gain,
        ln_bias,
        w_qkv.transpose(0, 2, 1, 3),
        b_qkv.transpose(1, 0, 2),
        w_out,
        b_out,
        w_in,
        b_in,
        w_down,
        b_down,
        jnp.asarray(cosine),
        jnp.asarray(sine),
    )
    out = pl.pallas_call(
        functools.partial(store_kernel, len(shapes)),
        out_shape=[jax.ShapeDtypeStruct(s, F32) for s in shapes],
        in_specs=[away] * 2 + [here] * (len(shapes) - 2),
        out_specs=[away] * len(shapes),
        scratch_shapes=[vm((rows, depth), F32), vm((rows, depth), F32), dma((3, 16))],
    )(*out)
    x, g, gain, bias, bqkv, bout, b_in_g, bdown, wq, wo, wi, wd = out
    return (
        x,
        g,
        gain,
        bias,
        wq.transpose(0, 2, 1, 3),
        bqkv.transpose(1, 0, 2),
        wo.transpose(0, 2, 1),
        bout,
        wi,
        b_in_g,
        wd.transpose(0, 2, 1),
        bdown,
    )


def solution(mesh):
    return jax.shard_map(
        functools.partial(on_device, mesh.shape["tensor"], mesh.shape["dp"]),
        mesh=mesh,
        in_specs=(
            P("dp", None),
            P("dp", None),
            P(),
            P(),
            P(None, None, None, "tensor"),
            P(None, None, "tensor"),
            P(None, "tensor", None),
            P(),
            P(None, None, "tensor"),
            P(None, "tensor"),
            P(None, "tensor", None),
            P(),
        ),
        out_specs=(
            P("dp", None),
            P("dp", None),
            P(),
            P(),
            P(None, "dp", None, "tensor"),
            P(None, None, "tensor"),
            P(None, "tensor", "dp"),
            P(),
            P(None, "dp", "tensor"),
            P(None, "tensor"),
            P(None, "tensor", "dp"),
            P(),
        ),
        check_vma=False,
    )
```

```python
import functools

import jax
import jax.numpy as jnp
import numpy as np
from jax import lax
from jax.experimental import pallas as pl
from jax.experimental.pallas import tpu as pltpu
from jax.sharding import PartitionSpec as P

HEAD_DIM = 64
ROT = 16
SEQ = 2048
LAYERS = 2
EPS = 1e-05
F32 = jnp.float32
BF16 = jnp.bfloat16
MESH = pl.DeviceIdType.MESH
LANES = 128
QT = 256
KT = 256
MT = 256
ST = 32
TP = 4
PARTS = 4


def nn(a, b):
    return jnp.dot(a, b, preferred_element_type=F32)


def nt(a, b):
    return lax.dot_general(a, b, (((1,), (1,)), ((), ())), preferred_element_type=F32)


def rope_constants():
    half = ROT // 2
    exponent = np.arange(0, ROT, 2).astype(np.float32) / np.float32(ROT)
    inverse = (np.float32(1.0) / np.float32(10000.0) ** exponent).astype(np.float32)
    angles = np.arange(SEQ).astype(np.float32)[:, None] * inverse[None, :]
    cosine = np.ones((SEQ, LANES), np.float32)
    sine = np.zeros((SEQ, LANES), np.float32)
    for start in range(0, LANES, HEAD_DIM):
        cosine[:, start : start + half] = np.cos(angles)
        cosine[:, start + half : start + ROT] = np.cos(angles)
        sine[:, start : start + half] = -np.sin(angles)
        sine[:, start + half : start + ROT] = np.sin(angles)
    return cosine, sine


def rotate(values, cosine, sine):
    half = ROT // 2
    lane = lax.broadcasted_iota(jnp.int32, values.shape, 1)
    partner = jnp.where(
        lane % HEAD_DIM < half,
        pltpu.roll(values, LANES - half, 1),
        pltpu.roll(values, half, 1),
    )
    return values * cosine + partner * sine


def head_only(values, head):
    lane = lax.broadcasted_iota(jnp.int32, values.shape, 1)
    return jnp.where(lane // HEAD_DIM == head, values, jnp.zeros_like(values))


def rows_at(step, size):
    return pl.ds(pl.multiple_of(step * size, size), size)


def remote(src, dst, send_sem, recv_sem, **device):
    return pltpu.make_async_remote_copy(
        src_ref=src,
        dst_ref=dst,
        send_sem=send_sem,
        recv_sem=recv_sem,
        device_id=device,
        device_id_type=MESH,
    )


class Refs:
    pass


def step_kernel(nt_dev, nd, *refs):
    names = (
        "tok", "cot", "gain", "bias", "wqkv_h", "bqkv", "wout_h", "bout", "win_h", "bin",
        "wdown_h", "bdown", "cos_h", "sin_h", "ox", "og", "ogain", "obias", "obqkv", "obout",
        "obin", "obdown", "oq", "oo", "oi", "od", "wqkv", "wout", "win", "wdown", "cosine",
        "sine", "x", "g", "xt", "ct", "h0", "h1", "qm", "kv", "kt", "vt", "ob", "ot", "top",
        "lse", "u", "act", "mu", "rs", "part", "psend", "ra", "rb", "sa", "sb", "r2a", "r2b",
        "agbuf", "dz", "do", "dom", "delta", "dqt", "dkvo", "dkvi", "own", "dqkv", "du", "dact",
        "binacc", "dh0", "dh1", "ge", "gl", "r1e", "r1l", "r2e", "r2l", "s3e", "s3l", "r3e",
        "r3l", "k3e", "k3l", "ln", "other", "ln1", "other1", "ln2", "other2", "lnsum", "ln3",
        "lnall", "lnacc", "lsem", "kvs", "kvr", "dks", "dkr", "ars", "arr", "g1s", "g1r", "g2s",
        "g2r", "g3s", "g3r", "s1s", "s1r", "s2s", "s2r", "s3s", "s3r", "s4s", "s4r",
    )
    assert len(names) == len(refs)
    v = Refs()
    v.__dict__.update(zip(names, refs))
    rows, depth = v.x.shape
    group = SEQ // rows
    nx = nd // group
    chunk = rows // nt_dev
    grow = depth // nd
    width = v.wout.shape[1]
    ff = v.win.shape[2]

    me_t = lax.axis_index("tensor")
    me_d = lax.axis_index("dp")
    rank = lax.rem(me_d, group)
    core = lax.rem(me_d, 2)
    zlo = lax.rem(me_d // 2, 2)
    xc = me_d // group
    ny = nt_dev // 2
    hd = depth // 2
    yy = me_t // 2
    zh = lax.rem(me_t, 2)
    other_zh = me_t + 1 - 2 * zh
    other_core = me_d + 1 - 2 * core
    other_z = me_d + 2 - 4 * zlo

    barrier = pltpu.get_barrier_semaphore()
    for k in range(1, nt_dev):
        pl.semaphore_signal(
            barrier, inc=1, device_id={"tensor": lax.rem(me_t + k, nt_dev)}, device_id_type=MESH
        )
    for k in range(1, nd):
        pl.semaphore_signal(
            barrier, inc=1, device_id={"dp": lax.rem(me_d + k, nd)}, device_id_type=MESH
        )

    parts = [slice(i * rows // TP, (i + 1) * rows // TP) for i in range(TP)]

    def load(src, dst, index):
        copy = pltpu.make_async_copy(src, dst, v.lsem.at[index])
        copy.start()
        return copy

    load_tok = [load(v.tok.at[at], v.xt.at[at], 16 + i) for i, at in enumerate(parts)]
    load_cos = load(v.cos_h.at[rows_at(rank, rows)], v.cosine, 1)
    load_sin = load(v.sin_h.at[rows_at(rank, rows)], v.sine, 2)
    load_qkv = []
    load_rest = []
    for l in range(LAYERS):
        load_qkv.append(
            [
                load(
                    v.wqkv_h.at[l, c],
                    v.wqkv.at[l, :, pl.ds(c * width, width)],
                    4 + 6 * l + c,
                )
                for c in range(3)
            ]
        )
        load_rest.append(
            [
                load(v.win_h.at[l], v.win.at[l], 4 + 6 * l + 3),
                load(v.wdown_h.at[l], v.wdown.at[l], 4 + 6 * l + 4),
                load(v.wout_h.at[l], v.wout.at[l], 4 + 6 * l + 5),
            ]
        )
    load_cot = load(v.cot, v.ct, 3)

    def norm_rows(l, at, x):
        mean = jnp.mean(x, axis=-1, keepdims=True)
        center = x - mean
        spread = jnp.mean(center * center, axis=-1, keepdims=True)
        r = lax.rsqrt(spread + EPS)
        xhat = center * r
        v.mu[l, at, :] = mean
        v.rs[l, at, :] = r
        v.h0[l, at, :] = (xhat * v.gain[l, 0:1, :] + v.bias[l, 0:1, :]).astype(BF16)
        v.h1[l, at, :] = (xhat * v.gain[l, 1:2, :] + v.bias[l, 1:2, :]).astype(BF16)

    def stream_rows(l, at):
        if l == 0:
            return v.xt[at, :].astype(F32)
        return v.x[at, :]

    def at_y(k):
        return lax.rem(yy + k, ny)

    def copy_of(s, src, dst, sem, to):
        return remote(src, dst, v.ars.at[s, sem], v.arr.at[s, sem], tensor=to)

    def a1(s, k):
        to = at_y(k)
        return copy_of(
            s, v.psend.at[s, 0, pl.ds(2 * to, 2)], v.ra.at[s, k - 1], k - 1, 2 * to + zh
        )

    def b1(s, m):
        to = at_y(m)
        return copy_of(
            s, v.psend.at[s, 1, 2 * to + 1 - zh], v.rb.at[s, to], ny - 2 + m, other_zh
        )

    def a2(s):
        return copy_of(s, v.sa.at[s], v.r2a.at[s], 2 * ny - 1, other_zh)

    def b2(s, k):
        return copy_of(
            s, v.sb.at[s, k - 1], v.r2b.at[s, k - 1], 2 * ny - 1 + k, 2 * at_y(k) + zh
        )

    def rs_pair(s, m):
        b1(s, m).start()

        @pl.when(m < ny)
        def _():
            a1(s, m).start()

    def rs_forward(s):
        for m in range(1, ny):
            b1(s, m).wait_recv()
            to = at_y(m)
            v.sb[s, m - 1] = (
                v.psend[s, 1, 2 * to + zh].astype(F32) + v.rb[s, to].astype(F32)
            ).astype(BF16)
            b2(s, m).start()
        for k in range(1, ny):
            a1(s, k).wait_recv()
        total = v.psend[s, 0, other_zh].astype(F32)
        for k in range(1, ny):
            total = total + v.ra[s, k - 1, 1 - zh].astype(F32)
        v.sa[s] = total.astype(BF16)
        a2(s).start()
        b1(s, ny).wait_recv()

    def rs_finish(s):
        a2(s).wait()
        for k in range(1, ny):
            b2(s, k).wait()
            a1(s, k).wait_send()
        for m in range(1, ny + 1):
            b1(s, m).wait_send()

    def rs_sum(s, at):
        first = v.psend[s, 0, me_t, at, :].astype(F32) + v.r2a[s, at, :].astype(F32)
        second = v.psend[s, 1, me_t, at, :].astype(F32) + v.rb[s, yy, at, :].astype(F32)
        for k in range(1, ny):
            first = first + v.ra[s, k - 1, zh, at, :].astype(F32)
            second = second + v.r2b[s, k - 1, at, :].astype(F32)
        return jnp.concatenate([first, second], axis=1)

    def ag_copy(s, half, chunk_at, sem, to):
        block = v.agbuf.at[s, half, chunk_at]
        return copy_of(s, block, block, sem, to)

    ag0 = 3 * ny - 1
    near_first = sorted(range(1, ny), key=lambda k: min(k, ny - k))

    def gz(s):
        return ag_copy(s, 0, me_t, ag0, other_zh)

    def gy(s, k):
        return ag_copy(s, 0, me_t, ag0 + k, 2 * at_y(k) + zh)

    def fy(s, k):
        return ag_copy(s, 0, other_zh, ag0 + ny - 1 + k, 2 * at_y(k) + zh)

    def by(s, k):
        return ag_copy(s, 1, me_t, ag0 + 2 * ny - 2 + k, 2 * at_y(k) + zh)

    def bz(s, m):
        return ag_copy(s, 1, 2 * at_y(m) + zh, ag0 + 3 * ny - 2 + m, other_zh)

    def place(step):
        return lax.rem((step + 1) // 2 * (2 * lax.rem(step, 2) - 1) + ny, ny)

    def arrived(s, half, chunk_at, sem):
        ag_copy(s, half, chunk_at, sem, other_zh).wait_recv()

    def ag_put(s, at, value):
        v.agbuf[s, 0, me_t, at, :] = value[:, :hd].astype(BF16)
        v.agbuf[s, 1, me_t, at, :] = value[:, hd:].astype(BF16)

    def ag_start(s):
        gz(s).start()
        for k in near_first:
            by(s, k).start()
        bz(s, 0).start()
        for k in near_first:
            gy(s, k).start()

    def ag_forward(s):
        arrived(s, 0, other_zh, ag0)
        for k in near_first:
            fy(s, k).start()
        for k in near_first:
            arrived(s, 1, 2 * at_y(ny - k) + zh, ag0 + 2 * ny - 2 + k)
            bz(s, ny - k).start()

    def ag_pairs(s, first, last, use, after):
        def one(step, carry):
            m = place(step)
            pair = at_y(m)

            @pl.when(m > 0)
            def _():
                arrived(s, 0, 2 * pair + zh, ag0 + ny - m)
                arrived(s, 0, 2 * pair + 1 - zh, ag0 + 2 * ny - 1 - m)

            arrived(s, 1, 2 * pair + 1 - zh, ag0 + 3 * ny - 2 + m)
            for i in range(2):
                src = 2 * pair + i
                for j in range(chunk // ST):
                    at = slice(j * ST, (j + 1) * ST)
                    use(
                        pl.ds(pl.multiple_of(src * chunk + j * ST, ST), ST),
                        jnp.concatenate(
                            [v.agbuf[s, 0, src, at, :], v.agbuf[s, 1, src, at, :]], axis=1
                        ).astype(F32),
                    )
            after(rows_at(pair, 2 * chunk))
            return carry

        lax.fori_loop(first, last, one, 0)

    def ag_sent(s):
        gz(s).wait_send()
        bz(s, 0).wait_send()
        for k in range(1, ny):
            gy(s, k).wait_send()
            fy(s, k).wait_send()
            by(s, k).wait_send()
            bz(s, k).wait_send()

    def kv_copy(l, step):
        slot, to = [(rank, other_core), (rank, other_z), (rank - 2, other_core)][step]
        block = v.kv.at[l, slot]
        return remote(block, block, v.kvs.at[l, step], v.kvr.at[l, step], dp=to)

    def kv_in(l, step):
        slot = [rank - 1, rank - 2, rank - 1 - 2 * core][step]
        block = v.kv.at[l, slot]
        return remote(block, block, v.kvs.at[l, step], v.kvr.at[l, step], dp=other_core)

    def dkv_copy(l, step):
        return remote(
            v.dkvo.at[l, step],
            v.dkvi.at[l, step],
            v.dks.at[l, step],
            v.dkr.at[l, step],
            dp=other_z if step == 1 else other_core,
        )

    def transpose_block(l, b):
        block = v.kv[l, b].astype(F32)
        v.kt[l, b] = block[:, :width].T.astype(BF16)
        v.vt[l, b] = block[:, width:].T.astype(BF16)

    def qkv_rows(l, at, size):
        mixed = nn(v.h0[l, at, :], v.wqkv[l])
        cosine, sine = v.cosine[at, :], v.sine[at, :]
        q = rotate(mixed[:, :width] + v.bqkv[0, l : l + 1, :], cosine, sine).astype(BF16)
        k = rotate(mixed[:, width : 2 * width] + v.bqkv[1, l : l + 1, :], cosine, sine)
        val = mixed[:, 2 * width :] + v.bqkv[2, l : l + 1, :]
        scaled = (q.astype(F32) * 0.125).astype(BF16)
        v.qm[l, 0, at, :] = head_only(scaled, 0)
        v.qm[l, 1, at, :] = head_only(scaled, 1)
        v.kv[l, rank, at, :width] = k.astype(BF16)
        v.kv[l, rank, at, width:] = val.astype(BF16)

    def kv_send(l):
        @pl.when(zlo == 0)
        def _():
            kv_copy(l, 1).start()

        @pl.when(core == 0)
        def _():
            kv_copy(l, 0).start()

    def kv_near(l):
        transpose_block(l, rank)

        @pl.when(core == 1)
        def _():
            kv_in(l, 0).wait_recv()
            transpose_block(l, rank - 1)

    def kv_far(l):
        @pl.when(zlo == 1)
        def _():
            kv_in(l, 1).wait_recv()
            kv_copy(l, 2).start()
            transpose_block(l, rank - 2)
            kv_in(l, 2).wait_recv()
            transpose_block(l, rank - 1 - 2 * core)

    def feed_forward(l, at, size):
        v.u[l, at, :] = nn(v.h1[l, at, :], v.win[l]) + v.bin[l : l + 1, :]

        def activate(i, carry):
            now = pl.ds(pl.multiple_of(at.start + i * ST, ST), ST)
            u = v.u[l, now, :]
            inner = 0.5 * (1.0 + lax.erf(u * np.float32(0.5**0.5)))
            v.act[l, now, :] = (u * inner).astype(BF16)
            v.u[l, now, :] = inner + u * jnp.exp(-0.5 * u * u) * np.float32((2.0 * np.pi) ** -0.5)
            return carry

        lax.fori_loop(0, size // ST, activate, 0)
        v.part[at, :] = nn(v.act[l, at, :], v.wdown[l])

    def attention(l, s, part):
        for qt in range(rows // QT):
            q_at = slice(qt * QT, (qt + 1) * QT)
            head_rows = [slice(h * HEAD_DIM, (h + 1) * HEAD_DIM) for h in range(2)]

            def block(b, carry, masked):
                keys = v.kv[l, b, :, :width]
                scores = [nt(keys, v.qm[l, h, q_at, :]) for h in range(2)]
                result = []
                for h in range(2):
                    top, total, out = carry[h]
                    sc = scores[h]
                    if masked:
                        key = lax.broadcasted_iota(jnp.int32, sc.shape, 0)
                        query = lax.broadcasted_iota(jnp.int32, sc.shape, 1) + qt * QT
                        sc = jnp.where(key <= query, sc, -1e30)
                    new = jnp.maximum(top, jnp.max(sc, axis=0, keepdims=True))
                    p = jnp.exp(sc - new)
                    fade = jnp.exp(top - new)
                    total = total * fade + jnp.sum(p, axis=0, keepdims=True)
                    out = out * fade + nn(v.vt[l, b, head_rows[h], :], p.astype(BF16))
                    result.append((new, total, out))
                return tuple(result)

            start = (
                jnp.full((1, QT), -1e30, F32),
                jnp.zeros((1, QT), F32),
                jnp.zeros((HEAD_DIM, QT), F32),
            )
            if part == 0:
                carry = block(rank, (start, start), True)
                carry = lax.fori_loop(
                    rank - core, rank, functools.partial(block, masked=False), carry
                )
                for h in range(2):
                    v.top[h : h + 1, q_at] = carry[h][0]
                    v.lse[l, h : h + 1, q_at] = carry[h][1]
                    v.ot[l, head_rows[h], q_at] = carry[h][2]
                continue
            carry = tuple(
                (
                    v.top[h : h + 1, q_at],
                    v.lse[l, h : h + 1, q_at],
                    v.ot[l, head_rows[h], q_at],
                )
                for h in range(2)
            )
            carry = lax.fori_loop(0, 2 * zlo, functools.partial(block, masked=False), carry)
            for h in range(2):
                top, total, out = carry[h]
                v.ot[l, head_rows[h], q_at] = out / total
                v.lse[l, h : h + 1, q_at] = top + jnp.log(total)
            v.ob[l, q_at, :] = v.ot[l, :, q_at].T.astype(BF16)
            both = nn(v.ob[l, q_at, :], v.wout[l]) + v.part[q_at, :]
            both = both.astype(BF16)
            first = qt * QT // chunk
            for half in range(2):
                v.psend[s, half, first : first + QT // chunk] = both[
                    :, half * hd : (half + 1) * hd
                ].reshape(QT // chunk, chunk, hd)
            for pair in range(first // 2, (first + QT // chunk) // 2):
                rs_pair(s, lax.rem(pair - yy - 1 + 2 * ny, ny) + 1)

    def branch_reduce(s):
        rs_finish(s)
        for i in range(chunk // 16):
            at = slice(i * 16, (i + 1) * 16)
            ag_put(s, at, rs_sum(s, at))
        ag_start(s)

    grads = {0: (v.ge, v.r1e, v.r2e, v.s3e, v.r3e, v.k3e), 1: (v.gl, v.r1l, v.r2l, v.s3l, v.r3l, v.k3l)}

    def core_copy(l, p):
        g, r1 = grads[p][:2]
        return remote(
            g.at[l, 1 - core], r1.at[l], v.g1s.at[l, p], v.g1r.at[l, p], dp=other_core
        )

    def x_copy(l, p, k):
        r1, r2 = grads[p][1:3]
        to = lax.rem(xc + k, nx)
        return remote(
            r1.at[l, pl.ds(2 * to, 2)],
            r2.at[l, k - 1],
            v.g2s.at[l, p, k - 1],
            v.g2r.at[l, p, k - 1],
            dp=to * group + zlo * 2 + core,
        )

    def z_copy(l, p):
        return remote(
            grads[p][3].at[l], grads[p][4].at[l], v.g3s.at[l, p], v.g3r.at[l, p], dp=other_z
        )

    def grad_core(l, p):
        core_copy(l, p).start()

    def grad_x(l, p):
        core_copy(l, p).wait()
        g, r1 = grads[p][:2]

        def one(i, carry):
            for j in range(grow // 16):
                at = slice(j * 16, (j + 1) * 16)
                r1[l, i, at, :] = (
                    r1[l, i, at, :].astype(F32) + g[l, core, i, at, :].astype(F32)
                ).astype(BF16)
            return carry

        lax.fori_loop(0, nd // 2, one, 0)
        for k in range(1, nx):
            x_copy(l, p, k).start()

    def grad_z(l, p):
        _, r1, r2, s3, r3, k3 = grads[p]
        for k in range(1, nx):
            x_copy(l, p, k).wait()

        def total(z, at):
            value = r1[l, 2 * xc + z, at, :].astype(F32)
            for k in range(1, nx):
                value = value + r2[l, k - 1, z, at, :].astype(F32)
            return value

        for j in range(grow // 16):
            at = slice(j * 16, (j + 1) * 16)
            s3[l, at, :] = total(1 - zlo, at).astype(BF16)
        z_copy(l, p).start()
        for j in range(grow // 16):
            at = slice(j * 16, (j + 1) * 16)
            k3[l, at, :] = total(zlo, at)

    def grad_end(l, p):
        z_copy(l, p).wait()
        _, _, _, _, r3, k3 = grads[p]
        for j in range(grow // 16):
            at = slice(j * 16, (j + 1) * 16)
            total = k3[l, at, :] + r3[l, at, :].astype(F32)
            if p == 0:
                v.oo[l, at, :] = total[:, :width]
                v.od[l, at, :] = total[:, width : width + ff]
                v.oi[l, at, :] = total[:, width + ff :]
            else:
                for c in range(3):
                    v.oq[l, c, at, :] = total[:, c * width : (c + 1) * width]

    def start_gradient(l, at, gradient):
        v.dz[at, :] = gradient.astype(BF16)

    def attention_back(l, first, second):
        do = v.do[...]
        product = do.astype(F32).T * v.ot[l]
        v.delta[0:1, :] = jnp.sum(product[:HEAD_DIM], axis=0, keepdims=True)
        v.delta[1:2, :] = jnp.sum(product[HEAD_DIM:], axis=0, keepdims=True)
        v.dqt[...] = jnp.zeros_like(v.dqt)

        def piece(b, i, masked):
            at = rows_at(i, KT)
            keys = v.kv[l, b, at, :width]
            values = v.kv[l, b, at, width:]
            dk = jnp.zeros((KT, width), F32)
            dv = jnp.zeros((KT, width), F32)
            for h in range(2):
                head_rows = slice(h * HEAD_DIM, (h + 1) * HEAD_DIM)
                sc = nt(keys, v.qm[l, h])
                if masked:
                    key = lax.broadcasted_iota(jnp.int32, sc.shape, 0) + i * KT
                    query = lax.broadcasted_iota(jnp.int32, sc.shape, 1)
                    sc = jnp.where(key <= query, sc, -1e30)
                p = jnp.exp(sc - v.lse[l, h : h + 1, :])
                dp = nt(values, v.dom[h])
                ds = (p * (dp - v.delta[h : h + 1, :])).astype(BF16)
                dv = dv + nn(p.astype(BF16), v.dom[h])
                dk = dk + nn(ds, v.qm[l, h])
                v.dqt[head_rows, :] += nn(v.kt[l, b, head_rows, at], ds)
            return dk, dv

        def far(b, slot, received):
            def inner(i, c):
                dk, dv = piece(b, i, False)
                at = rows_at(i, KT)
                if received:
                    dk = dk + v.dkvi[l, 0, at, :width].astype(F32)
                    dv = dv + v.dkvi[l, 0, at, width:].astype(F32)
                v.dkvo[l, slot, at, :width] = dk.astype(BF16)
                v.dkvo[l, slot, at, width:] = dv.astype(BF16)
                return c

            lax.fori_loop(0, rows // KT, inner, 0, unroll=True)
            dkv_copy(l, slot).start()

        @pl.when(zlo == 1)
        def _():
            far(1 - core, 0, False)
            first()
            dkv_copy(l, 0).wait_recv()
            far(core, 1, True)
            second()

        @pl.when(core == 1)
        def _():
            far(rank - 1, 2, False)

        def near(i, c):
            dk, dv = piece(rank, i, True)
            at = rows_at(i, KT)
            v.own[at, :width] = dk
            v.own[at, width:] = dv
            return c

        lax.fori_loop(0, rows // KT, near, 0, unroll=True)

    def do_rows(l, at):
        do = nt(v.dz[at, :], v.wout[l]).astype(BF16)
        v.do[at, :] = do
        v.dom[0, at, :] = head_only(do, 0)
        v.dom[1, at, :] = head_only(do, 1)

    def dact_rows(l, at):
        v.dact[at, :] = nt(v.dz[at, :], v.wdown[l])

    def back_rows(l, at, size):
        def slope(i, acc):
            now = pl.ds(pl.multiple_of(at.start + i * ST, ST), ST)
            du = (v.dact[now, :] * v.u[l, now, :]).astype(BF16)
            v.du[now, :] = du
            return acc + jnp.sum(du.astype(F32).reshape(ST // 8, 8, ff), axis=0)

        v.binacc[l] += lax.fori_loop(0, size // ST, slope, jnp.zeros((8, ff), F32))
        v.dh1[at, :] = nt(v.du[at, :], v.win[l])

    def early_grads(l):
        def one(i, carry):
            at = rows_at(i, 2 * grow)
            dzt = v.dz[:, at].astype(F32).T.astype(BF16)
            ht = v.h1[l, :, at].astype(F32).T.astype(BF16)
            wo = nn(dzt, v.ob[l]).astype(BF16)
            wd = nn(dzt, v.act[l]).astype(BF16)
            wi = nn(ht, v.du[...]).astype(BF16)
            for c in range(2):
                part = slice(c * grow, (c + 1) * grow)
                v.ge[l, c, i, :, :width] = wo[part]
                v.ge[l, c, i, :, width : width + ff] = wd[part]
                v.ge[l, c, i, :, width + ff :] = wi[part]
            return carry

        lax.fori_loop(0, depth // (2 * grow), one, 0)

    def late_grads(l):
        def one(i, carry):
            at = rows_at(i, 2 * grow)
            ht = v.h0[l, :, at].astype(F32).T.astype(BF16)
            wq = nn(ht, v.dqkv[...]).astype(BF16)
            for c in range(2):
                v.gl[l, c, i] = wq[c * grow : (c + 1) * grow]
            return carry

        lax.fori_loop(0, depth // (2 * grow), one, 0)

    def qkv_back(l):
        for step, here in ((2, core == 0), (1, zlo == 0)):

            @pl.when(here)
            def _():
                dkv_copy(l, step).wait_recv()
                v.own[...] += v.dkvi[l, step].astype(F32)

        cosine, sine = v.cosine[...], -v.sine[...]
        v.dqkv[:, :width] = rotate(v.dqt[...].T * 0.125, cosine, sine).astype(BF16)
        v.dqkv[:, width : 2 * width] = rotate(v.own[:, :width], cosine, sine).astype(BF16)
        v.dqkv[:, 2 * width : 3 * width] = v.own[:, width:].astype(BF16)
        v.other[4 * l + 3 : 4 * l + 4, : 3 * width] = jnp.sum(
            v.dqkv[...].astype(F32), axis=0, keepdims=True
        )

        def one(i, carry):
            at = rows_at(i, MT)
            v.dh0[at, :] = nt(v.dqkv[at, :], v.wqkv[l])
            return carry

        lax.fori_loop(0, rows // MT, one, 0)

        def send(m, carry):
            pair = at_y(m)
            for i in range(2 * chunk // ST):
                at = pl.ds(pl.multiple_of(pair * 2 * chunk + i * ST, ST), ST)
                both = v.dh0[at, :] * v.gain[l, 0:1, :] + v.dh1[at, :] * v.gain[l, 1:2, :]
                both = both.astype(BF16)
                part = slice(i * ST % chunk, i * ST % chunk + ST)
                for half in range(2):
                    v.psend[0, half, 2 * pair + i * ST // chunk, part, :] = both[
                        :, half * hd : (half + 1) * hd
                    ]
            rs_pair(0, m)
            return carry

        lax.fori_loop(1, ny + 1, send, 0)

    def norm_grads(l):
        v.lnacc[...] = jnp.zeros_like(v.lnacc)

        def fold(value):
            return jnp.sum(value.reshape(2, 8, depth), axis=0)

        def one(i, carry):
            at = rows_at(i, 16)
            xhat = (stream_rows(l, at) - v.mu[l, at, :]) * v.rs[l, at, :]
            first, second = v.dh0[at, :], v.dh1[at, :]
            v.lnacc[0] += fold(first * xhat)
            v.lnacc[1] += fold(second * xhat)
            v.lnacc[2] += fold(first)
            v.lnacc[3] += fold(second)
            v.lnacc[4] += fold(v.dz[at, :].astype(F32))
            return carry

        lax.fori_loop(0, rows // 16, one, 0)
        for i in range(4):
            v.ln[4 * l + i : 4 * l + i + 1, :] = jnp.sum(v.lnacc[i], axis=0, keepdims=True)
        column = jnp.sum(v.lnacc[4], axis=0, keepdims=True)
        v.other[4 * l : 4 * l + 1, :] = column[:, :ff]
        v.other[4 * l + 1 : 4 * l + 2, :] = column[:, ff:]
        v.other[4 * l + 2 : 4 * l + 3, :] = jnp.sum(v.binacc[l], axis=0, keepdims=True)

    def stream_reduce(l):
        rs_finish(0)
        for i in range(chunk // 16):
            at = pl.ds(pl.multiple_of(me_t * chunk + i * 16, 16), 16)
            gd = rs_sum(0, slice(i * 16, (i + 1) * 16))
            r = v.rs[l, at, :]
            xhat = (stream_rows(l, at) - v.mu[l, at, :]) * r
            mean = jnp.mean(gd, axis=-1, keepdims=True)
            along = jnp.mean(gd * xhat, axis=-1, keepdims=True)
            dx = r * (gd - mean - xhat * along)
            ag_put(0, slice(i * 16, (i + 1) * 16), dx)
        ag_start(0)

    def small_core(i):
        mine, theirs = [(v.ln, v.ln1), (v.other, v.other1)][i]
        return remote(mine, theirs, v.s1s.at[i], v.s1r.at[i], dp=other_core)

    def small_dp(k, i):
        to = lax.rem(me_d + 2 * k, nd)
        mine, theirs = [(v.ln, v.ln3), (v.other, v.other2)][i]
        return remote(mine, theirs.at[k - 1], v.s3s.at[i, k - 1], v.s3r.at[i, k - 1], dp=to)

    def small_scatter(k):
        to = lax.rem(me_t + k, nt_dev)
        columns = pl.ds(pl.multiple_of(to * LANES, LANES), LANES)
        return remote(
            v.lnsum.at[:, columns], v.ln2.at[k - 1], v.s2s.at[k - 1], v.s2r.at[k - 1], tensor=to
        )

    def small_gather(k):
        to = lax.rem(me_t + k, nt_dev)
        block = v.lnall.at[me_t]
        return remote(block, block, v.s4s.at[k - 1], v.s4r.at[me_t], tensor=to)

    def small_start():
        for i in range(2):
            small_core(i).start()

    def small_second():
        for i in range(2):
            small_core(i).wait()
        v.ln[...] += v.ln1[...]
        v.other[...] += v.other1[...]
        for k in range(1, nd // 2):
            for i in range(2):
                small_dp(k, i).start()

    def small_third():
        total = v.ln[...]
        for k in range(1, nd // 2):
            small_dp(k, 0).wait()
            total = total + v.ln3[k - 1]
        v.lnsum[...] = total
        for k in range(1, nt_dev):
            small_scatter(k).start()
        total = v.other[...]
        for k in range(1, nd // 2):
            small_dp(k, 1).wait()
            total = total + v.other2[k - 1]
        for l in range(LAYERS):
            for half in range(2):
                at = slice(half * ff, (half + 1) * ff)
                row = total[4 * l + half : 4 * l + half + 1, :]
                v.obout[l : l + 1, at] = row
                v.obdown[l : l + 1, at] = row
            v.obin[l : l + 1, :] = total[4 * l + 2 : 4 * l + 3, :]
            for c in range(3):
                at = slice(c * width, (c + 1) * width)
                v.obqkv[c, l : l + 1, :] = total[4 * l + 3 : 4 * l + 4, at]

    def small_fourth():
        mine = pl.ds(pl.multiple_of(me_t * LANES, LANES), LANES)
        total = v.lnsum[:, mine]
        for k in range(1, nt_dev):
            small_scatter(k).wait()
            total = total + v.ln2[k - 1]
        v.lnall[me_t] = total
        for k in range(1, nt_dev):
            small_gather(k).start()

    def small_end():
        for k in range(1, nt_dev):
            src = lax.rem(me_t + k, nt_dev)
            block = v.lnall.at[src]
            remote(block, block, v.s4s.at[k - 1], v.s4r.at[src], tensor=src).wait()
        for j in range(nt_dev):
            at = slice(j * LANES, (j + 1) * LANES)
            block = v.lnall[j]
            for l in range(LAYERS):
                v.ogain[l, :, at] = block[4 * l : 4 * l + 2, :]
                v.obias[l, :, at] = block[4 * l + 2 : 4 * l + 4, :]

    def nothing(at):
        pass

    def first_norm(i, carry):
        at = rows_at(i, ST)
        norm_rows(0, at, v.xt[at, :].astype(F32))
        return carry

    with jax.named_scope("norm0"):
        for i in range(TP):
            load_tok[i].wait()
            lax.fori_loop(i * rows // TP // ST, (i + 1) * rows // TP // ST, first_norm, 0, unroll=2)
    with jax.named_scope("qkv0"):
        for c in load_qkv[0]:
            c.wait()
        load_cos.wait()
        load_sin.wait()

        def first_qkv(i, carry):
            qkv_rows(0, rows_at(i, MT), MT)
            return carry

        lax.fori_loop(0, rows // MT, first_qkv, 0)
    with jax.named_scope("barrier"):
        pl.semaphore_wait(barrier, nt_dev - 1 + nd - 1)
    kv_send(0)
    v.ln[...] = jnp.zeros_like(v.ln)
    v.other[...] = jnp.zeros_like(v.other)
    v.binacc[...] = jnp.zeros_like(v.binacc)
    with jax.named_scope("ffn0"):
        for c in load_rest[0]:
            c.wait()

        def first_ffn(i, carry):
            feed_forward(0, rows_at(i, MT), MT)
            return carry

        lax.fori_loop(0, rows // MT, first_ffn, 0)
    with jax.named_scope("near0"):
        kv_near(0)
        attention(0, 0, 0)
    def first_gradients(z):
        @pl.when(zlo == z)
        def _():
            load_cot.wait()
            for c in load_rest[1]:
                c.wait()

            def copy_rows(i, carry):
                at = rows_at(i, ST)
                v.dz[at, :] = v.ct[at, :]
                v.g[at, :] = v.ct[at, :].astype(F32)
                return carry

            def rows_back(i, carry):
                at = rows_at(i, MT)
                do_rows(1, at)
                dact_rows(1, at)
                return carry

            lax.fori_loop(0, rows // ST, copy_rows, 0)
            lax.fori_loop(0, rows // MT, rows_back, 0)

    with jax.named_scope("dz1"):
        first_gradients(1)
    with jax.named_scope("kv0"):
        kv_far(0)
    with jax.named_scope("attn0"):
        attention(0, 0, 1)
    with jax.named_scope("dz1b"):
        first_gradients(0)
    with jax.named_scope("forward0"):
        rs_forward(0)
    with jax.named_scope("reduce0"):
        branch_reduce(0)

    def next_stream(at, z):
        x = v.xt[at, :].astype(F32) + (z + (v.bout[0:1, :] + v.bdown[0:1, :]))
        v.x[at, :] = x
        norm_rows(1, at, x)

    def next_qkv(at):
        qkv_rows(1, at, 2 * chunk)

    def next_ffn(at):
        feed_forward(1, at, 2 * chunk)
        back_rows(1, at, 2 * chunk)

    def next_both(at):
        next_qkv(at)
        next_ffn(at)

    with jax.named_scope("gather0"):
        for c in load_qkv[1]:
            c.wait()
        ag_forward(0)
        ag_pairs(0, 0, ny - 1, next_stream, next_both)
        ag_pairs(0, ny - 1, ny, next_stream, next_qkv)
        kv_send(1)
        ag_sent(0)
    with jax.named_scope("ffn1"):
        next_ffn(rows_at(at_y(place(jnp.int32(ny - 1))), 2 * chunk))
    with jax.named_scope("near1"):
        kv_near(1)
        attention(1, 1, 0)
    with jax.named_scope("kv1"):
        kv_far(1)
    with jax.named_scope("attn1"):
        attention(1, 1, 1)

    with jax.named_scope("attn_grad1"):
        attention_back(1, lambda: None, lambda: rs_forward(1))

    def early(l, z):
        @pl.when(zlo == z)
        def _():
            early_grads(l)
            grad_core(l, 0)

    with jax.named_scope("forward1"):

        @pl.when(zlo == 0)
        def _():
            rs_forward(1)

    with jax.named_scope("early1"):
        early(1, 0)
    with jax.named_scope("qkv_grad1"):
        qkv_back(1)
    with jax.named_scope("early1b"):
        early(1, 1)
    with jax.named_scope("late1"):
        late_grads(1)
        grad_core(1, 1)
    with jax.named_scope("forward"):
        rs_forward(0)
    with jax.named_scope("norm_grad1"):
        norm_grads(1)
    with jax.named_scope("gx10"):
        grad_x(1, 0)
    with jax.named_scope("stream_reduce1"):
        stream_reduce(1)
    with jax.named_scope("gx11"):
        grad_x(1, 1)

    def next_gradient(at, dx):
        gradient = v.g[at, :] + dx
        v.g[at, :] = gradient
        v.dz[at, :] = gradient.astype(BF16)

    def next_back(at):
        do_rows(0, at)
        dact_rows(0, at)
        back_rows(0, at, 2 * chunk)

    with jax.named_scope("gather2"):
        ag_forward(0)
        ag_pairs(0, 0, ny, next_gradient, next_back)
        ag_sent(0)
    with jax.named_scope("reduce1"):
        branch_reduce(1)
    with jax.named_scope("attn_grad0"):
        attention_back(0, lambda: ag_forward(1), lambda: None)
    with jax.named_scope("forward1b"):

        @pl.when(zlo == 0)
        def _():
            ag_forward(1)

    with jax.named_scope("gz1"):
        grad_z(1, 0)
        grad_z(1, 1)
    with jax.named_scope("early0"):
        early(0, 0)
    with jax.named_scope("qkv_grad0"):
        qkv_back(0)
    with jax.named_scope("early0b"):
        early(0, 1)
    with jax.named_scope("norm_grad0"):
        norm_grads(0)
        small_start()
    with jax.named_scope("late0"):
        late_grads(0)
        grad_core(0, 1)
    with jax.named_scope("small_second"):
        small_second()
    with jax.named_scope("gx00"):
        grad_x(0, 0)
    with jax.named_scope("forward"):
        rs_forward(0)

    def last_stream(at, z):
        v.x[at, :] = v.x[at, :] + (z + (v.bout[1:2, :] + v.bdown[1:2, :]))

    store_x = pltpu.make_async_copy(v.x, v.ox, v.lsem.at[0])
    store_g = pltpu.make_async_copy(v.g, v.og, v.lsem.at[1])
    with jax.named_scope("stream_reduce0"):
        stream_reduce(0)
    with jax.named_scope("gx01"):
        grad_x(0, 1)
    with jax.named_scope("forward0c"):
        ag_forward(0)
    with jax.named_scope("small_third"):
        small_third()
    with jax.named_scope("gather1"):
        ag_pairs(1, 0, ny, last_stream, nothing)
        ag_sent(1)
        store_x.start()
    with jax.named_scope("gend1"):
        grad_end(1, 0)
        grad_end(1, 1)

    def last_gradient(at, dx):
        v.g[at, :] = v.g[at, :] + dx

    with jax.named_scope("gather3"):
        ag_pairs(0, 0, ny // 2, last_gradient, nothing)
    with jax.named_scope("small_fourth"):
        small_fourth()
    with jax.named_scope("gather3b"):
        ag_pairs(0, ny // 2, ny, last_gradient, nothing)
        store_g.start()
        ag_sent(0)
    with jax.named_scope("gz0"):
        grad_z(0, 0)
        grad_z(0, 1)
    with jax.named_scope("small_end"):
        small_end()
    with jax.named_scope("gend0"):
        grad_end(0, 0)
        grad_end(0, 1)
        store_x.wait()
        store_g.wait()
    for l in range(LAYERS):
        for step, here in ((0, core == 0), (1, zlo == 0), (2, zlo == 1)):

            @pl.when(here)
            def _():
                kv_copy(l, step).wait_send()

        for step, here in ((0, zlo == 1), (1, zlo == 1), (2, core == 1)):

            @pl.when(here)
            def _():
                dkv_copy(l, step).wait_send()


def store_kernel(count, *refs):
    given, kept, held = refs[:count], refs[count : 2 * count], refs[2 * count : 3 * count]
    sems = refs[3 * count]
    parts = []
    for i in range(count):
        pieces = PARTS if i < 2 else 1
        rows = held[i].shape[0] // pieces
        parts += [(i, slice(j * rows, (j + 1) * rows)) for j in range(pieces)]
    loads = [
        pltpu.make_async_copy(given[i].at[at], held[i].at[at], sems.at[0, n])
        for n, (i, at) in enumerate(parts)
    ]
    stores = [
        pltpu.make_async_copy(held[i].at[at], kept[i].at[at], sems.at[1, n])
        for n, (i, at) in enumerate(parts)
    ]
    for copy in loads:
        copy.start()
    for load, store in zip(loads, stores):
        load.wait()
        store.start()
    for copy in stores:
        copy.wait()


def on_device(nt_dev, nd, *args):
    tokens, cotangent, ln_gain, ln_bias, w_qkv, b_qkv, w_out, b_out, w_in, b_in, w_down, b_down = args
    rows, depth = tokens.shape
    width = w_out.shape[1]
    ff = w_in.shape[2]
    group = SEQ // rows
    chunk = rows // nt_dev
    grow = depth // nd
    half = nd // 2
    nx = nd // group
    early = width + 2 * ff
    late = 3 * width
    cosine, sine = rope_constants()
    vm = pltpu.VMEM
    dma = pltpu.SemaphoreType.DMA
    two = LAYERS
    scratch = [
        vm((two, depth, 3 * width), BF16),
        vm((two, width, depth), BF16),
        vm((two, depth, ff), BF16),
        vm((two, ff, depth), BF16),
        vm((rows, LANES), F32),
        vm((rows, LANES), F32),
        vm((rows, depth), F32),
        vm((rows, depth), F32),
        vm((rows, depth), BF16),
        vm((rows, depth), BF16),
        vm((two, rows, depth), BF16),
        vm((two, rows, depth), BF16),
        vm((two, 2, rows, width), BF16),
        vm((two, group, rows, 2 * width), BF16),
        vm((two, group, width, rows), BF16),
        vm((two, group, width, rows), BF16),
        vm((two, rows, width), BF16),
        vm((two, width, rows), F32),
        vm((8, rows), F32),
        vm((two, 8, rows), F32),
        vm((two, rows, ff), F32),
        vm((two, rows, ff), BF16),
        vm((two, rows, 1), F32),
        vm((two, rows, 1), F32),
        vm((rows, depth), F32),
        vm((2, 2, nt_dev, chunk, depth // 2), BF16),
        vm((2, nt_dev // 2 - 1, 2, chunk, depth // 2), BF16),
        vm((2, nt_dev // 2, chunk, depth // 2), BF16),
        vm((2, chunk, depth // 2), BF16),
        vm((2, nt_dev // 2 - 1, chunk, depth // 2), BF16),
        vm((2, chunk, depth // 2), BF16),
        vm((2, nt_dev // 2 - 1, chunk, depth // 2), BF16),
        vm((2, 2, nt_dev, chunk, depth // 2), BF16),
        vm((rows, depth), BF16),
        vm((rows, width), BF16),
        vm((2, rows, width), BF16),
        vm((8, rows), F32),
        vm((width, rows), F32),
        vm((two, 3, rows, 2 * width), BF16),
        vm((two, 3, rows, 2 * width), BF16),
        vm((rows, 2 * width), F32),
        vm((rows, 3 * width), BF16),
        vm((rows, ff), BF16),
        vm((rows, ff), F32),
        vm((two, 8, ff), F32),
        vm((rows, depth), F32),
        vm((rows, depth), F32),
        vm((two, 2, half, grow, early), BF16),
        vm((two, 2, half, grow, late), BF16),
        vm((two, half, grow, early), BF16),
        vm((two, half, grow, late), BF16),
        vm((two, nx - 1, 2, grow, early), BF16),
        vm((two, nx - 1, 2, grow, late), BF16),
        vm((two, grow, early), BF16),
        vm((two, grow, late), BF16),
        vm((two, grow, early), BF16),
        vm((two, grow, late), BF16),
        vm((two, grow, early), F32),
        vm((two, grow, late), F32),
        vm((8, depth), F32),
        vm((8, ff), F32),
        vm((8, depth), F32),
        vm((8, ff), F32),
        vm((nt_dev - 1, 8, LANES), F32),
        vm((half - 1, 8, ff), F32),
        vm((8, depth), F32),
        vm((half - 1, 8, depth), F32),
        vm((nt_dev, 8, LANES), F32),
        vm((5, 8, depth), F32),
        dma((16 + TP,)),
        dma((two, 3)),
        dma((two, 3)),
        dma((two, 3)),
        dma((two, 3)),
        dma((2, 7 * (nt_dev // 2) - 3)),
        dma((2, 7 * (nt_dev // 2) - 3)),
        dma((two, 2)),
        dma((two, 2)),
        dma((two, 2, nx - 1)),
        dma((two, 2, nx - 1)),
        dma((two, 2)),
        dma((two, 2)),
        dma((2,)),
        dma((2,)),
        dma((nt_dev - 1,)),
        dma((nt_dev - 1,)),
        dma((2, half - 1)),
        dma((2, half - 1)),
        dma((nt_dev - 1,)),
        dma((nt_dev,)),
    ]
    here = pl.BlockSpec(memory_space=pltpu.VMEM)
    away = pl.BlockSpec(memory_space=pl.ANY)
    shapes = [
        (rows, depth),
        (rows, depth),
        (two, 2, depth),
        (two, 2, depth),
        (3, two, width),
        (two, depth),
        (two, ff),
        (two, depth),
        (two, 3, grow, width),
        (two, grow, width),
        (two, grow, ff),
        (two, grow, ff),
    ]
    out = pl.pallas_call(
        functools.partial(step_kernel, nt_dev, nd),
        out_shape=[jax.ShapeDtypeStruct(s, F32) for s in shapes],
        in_specs=[away, away, here, here, away, here, away, here, away, here, away, here, away, away],
        out_specs=[away] * 2 + [here] * (len(shapes) - 2),
        scratch_shapes=scratch,
        compiler_params=pltpu.CompilerParams(
            collective_id=0, has_side_effects=True, vmem_limit_bytes=64 * 1024 * 1024 - 65536
        ),
    )(
        tokens,
        cotangent,
        ln_gain,
        ln_bias,
        w_qkv.transpose(0, 2, 1, 3),
        b_qkv.transpose(1, 0, 2),
        w_out,
        b_out,
        w_in,
        b_in,
        w_down,
        b_down,
        jnp.asarray(cosine),
        jnp.asarray(sine),
    )
    out = pl.pallas_call(
        functools.partial(store_kernel, len(shapes)),
        out_shape=[jax.ShapeDtypeStruct(s, F32) for s in shapes],
        in_specs=[away] * len(shapes),
        out_specs=[away] * len(shapes),
        scratch_shapes=[vm(s, F32) for s in shapes] + [dma((2, 2 * PARTS + len(shapes)))],
    )(*out)
    x, g, gain, bias, bqkv, bout, b_in_g, bdown, wq, wo, wi, wd = out
    return (
        x,
        g,
        gain,
        bias,
        wq.transpose(0, 2, 1, 3),
        bqkv.transpose(1, 0, 2),
        wo.transpose(0, 2, 1),
        bout,
        wi,
        b_in_g,
        wd.transpose(0, 2, 1),
        bdown,
    )


def solution(mesh):
    return jax.shard_map(
        functools.partial(on_device, mesh.shape["tensor"], mesh.shape["dp"]),
        mesh=mesh,
        in_specs=(
            P("dp", None),
            P("dp", None),
            P(),
            P(),
            P(None, None, None, "tensor"),
            P(None, None, "tensor"),
            P(None, "tensor", None),
            P(),
            P(None, None, "tensor"),
            P(None, "tensor"),
            P(None, "tensor", None),
            P(),
        ),
        out_specs=(
            P("dp", None),
            P("dp", None),
            P(),
            P(),
            P(None, "dp", None, "tensor"),
            P(None, None, "tensor"),
            P(None, "tensor", "dp"),
            P(),
            P(None, "dp", "tensor"),
            P(None, "tensor"),
            P(None, "tensor", "dp"),
            P(),
        ),
        check_vma=False,
    )
```

```python
import functools

import jax
import jax.numpy as jnp
import numpy as np
from jax import lax
from jax.experimental import pallas as pl
from jax.experimental.pallas import tpu as pltpu
from jax.sharding import PartitionSpec as P

HEAD_DIM = 64
ROT = 16
SEQ = 2048
LAYERS = 2
EPS = 1e-05
F32 = jnp.float32
BF16 = jnp.bfloat16
MESH = pl.DeviceIdType.MESH
LANES = 128
QT = 256
KT = 256
MT = 256
ST = 32
TP = 4
PARTS = 4


def nn(a, b):
    return jnp.dot(a, b, preferred_element_type=F32)


def nt(a, b):
    return lax.dot_general(a, b, (((1,), (1,)), ((), ())), preferred_element_type=F32)


def rope_constants():
    half = ROT // 2
    exponent = np.arange(0, ROT, 2).astype(np.float32) / np.float32(ROT)
    inverse = (np.float32(1.0) / np.float32(10000.0) ** exponent).astype(np.float32)
    angles = np.arange(SEQ).astype(np.float32)[:, None] * inverse[None, :]
    cosine = np.ones((SEQ, LANES), np.float32)
    sine = np.zeros((SEQ, LANES), np.float32)
    for start in range(0, LANES, HEAD_DIM):
        cosine[:, start : start + half] = np.cos(angles)
        cosine[:, start + half : start + ROT] = np.cos(angles)
        sine[:, start : start + half] = -np.sin(angles)
        sine[:, start + half : start + ROT] = np.sin(angles)
    return cosine, sine


def rotate(values, cosine, sine):
    half = ROT // 2
    lane = lax.broadcasted_iota(jnp.int32, values.shape, 1)
    partner = jnp.where(
        lane % HEAD_DIM < half,
        pltpu.roll(values, LANES - half, 1),
        pltpu.roll(values, half, 1),
    )
    return values * cosine + partner * sine


def head_only(values, head):
    lane = lax.broadcasted_iota(jnp.int32, values.shape, 1)
    return jnp.where(lane // HEAD_DIM == head, values, jnp.zeros_like(values))


def rows_at(step, size):
    return pl.ds(pl.multiple_of(step * size, size), size)


def remote(src, dst, send_sem, recv_sem, **device):
    return pltpu.make_async_remote_copy(
        src_ref=src,
        dst_ref=dst,
        send_sem=send_sem,
        recv_sem=recv_sem,
        device_id=device,
        device_id_type=MESH,
    )


class Refs:
    pass


def step_kernel(nt_dev, nd, *refs):
    names = (
        "tok", "cot", "gain", "bias", "wqkv_h", "bqkv", "wout_h", "bout", "win_h", "bin",
        "wdown_h", "bdown", "cos_h", "sin_h", "ox", "og", "ogain", "obias", "obqkv", "obout",
        "obin", "obdown", "oq", "oo", "oi", "od", "wqkv", "wout", "win", "wdown", "cosine",
        "sine", "x", "g", "xt", "ct", "h0", "h1", "qm", "kv", "kt", "vt", "ob", "ot", "top",
        "lse", "u", "act", "mu", "rs", "part", "psend", "ra", "rb", "sa", "sb", "r2a", "r2b",
        "agbuf", "dz", "do", "dom", "delta", "dqt", "dkvo", "dkvi", "own", "dqkv", "du", "dact",
        "binacc", "dh0", "dh1", "ge", "gl", "r1e", "r1l", "r2e", "r2l", "s3e", "s3l", "r3e",
        "r3l", "k3e", "k3l", "ln", "other", "ln1", "other1", "ln2", "other2", "lnsum", "ln3",
        "lnall", "lnacc", "lsem", "kvs", "kvr", "dks", "dkr", "ars", "arr", "g1s", "g1r", "g2s",
        "g2r", "g3s", "g3r", "s1s", "s1r", "s2s", "s2r", "s3s", "s3r", "s4s", "s4r",
    )
    assert len(names) == len(refs)
    v = Refs()
    v.__dict__.update(zip(names, refs))
    rows, depth = v.x.shape
    group = SEQ // rows
    nx = nd // group
    chunk = rows // nt_dev
    grow = depth // nd
    width = v.wout.shape[1]
    ff = v.win.shape[2]

    me_t = lax.axis_index("tensor")
    me_d = lax.axis_index("dp")
    rank = lax.rem(me_d, group)
    core = lax.rem(me_d, 2)
    zlo = lax.rem(me_d // 2, 2)
    xc = me_d // group
    ny = nt_dev // 2
    hd = depth // 2
    yy = me_t // 2
    zh = lax.rem(me_t, 2)
    other_zh = me_t + 1 - 2 * zh
    other_core = me_d + 1 - 2 * core
    other_z = me_d + 2 - 4 * zlo

    barrier = pltpu.get_barrier_semaphore()
    for k in range(1, nt_dev):
        pl.semaphore_signal(
            barrier, inc=1, device_id={"tensor": lax.rem(me_t + k, nt_dev)}, device_id_type=MESH
        )
    for k in range(1, nd):
        pl.semaphore_signal(
            barrier, inc=1, device_id={"dp": lax.rem(me_d + k, nd)}, device_id_type=MESH
        )

    parts = [slice(i * rows // TP, (i + 1) * rows // TP) for i in range(TP)]

    def load(src, dst, index):
        copy = pltpu.make_async_copy(src, dst, v.lsem.at[index])
        copy.start()
        return copy

    load_tok = [load(v.tok.at[at], v.xt.at[at], 16 + i) for i, at in enumerate(parts)]
    load_cos = load(v.cos_h.at[rows_at(rank, rows)], v.cosine, 1)
    load_sin = load(v.sin_h.at[rows_at(rank, rows)], v.sine, 2)
    load_qkv = []
    load_rest = []
    for l in range(LAYERS):
        load_qkv.append(
            [
                load(
                    v.wqkv_h.at[l, c],
                    v.wqkv.at[l, :, pl.ds(c * width, width)],
                    4 + 6 * l + c,
                )
                for c in range(3)
            ]
        )
        load_rest.append(
            [
                load(v.win_h.at[l], v.win.at[l], 4 + 6 * l + 3),
                load(v.wdown_h.at[l], v.wdown.at[l], 4 + 6 * l + 4),
                load(v.wout_h.at[l], v.wout.at[l], 4 + 6 * l + 5),
            ]
        )
    load_cot = load(v.cot, v.ct, 3)

    def norm_rows(l, at, x):
        mean = jnp.mean(x, axis=-1, keepdims=True)
        center = x - mean
        spread = jnp.mean(center * center, axis=-1, keepdims=True)
        r = lax.rsqrt(spread + EPS)
        xhat = center * r
        v.mu[l, at, :] = mean
        v.rs[l, at, :] = r
        v.h0[l, at, :] = (xhat * v.gain[l, 0:1, :] + v.bias[l, 0:1, :]).astype(BF16)
        v.h1[l, at, :] = (xhat * v.gain[l, 1:2, :] + v.bias[l, 1:2, :]).astype(BF16)

    def stream_rows(l, at):
        if l == 0:
            return v.xt[at, :].astype(F32)
        return v.x[at, :]

    def at_y(k):
        return lax.rem(yy + k, ny)

    def copy_of(s, src, dst, sem, to):
        return remote(src, dst, v.ars.at[s, sem], v.arr.at[s, sem], tensor=to)

    def a1(s, k):
        to = at_y(k)
        return copy_of(
            s, v.psend.at[s, 0, pl.ds(2 * to, 2)], v.ra.at[s, k - 1], k - 1, 2 * to + zh
        )

    def b1(s, m):
        to = at_y(m)
        return copy_of(
            s, v.psend.at[s, 1, 2 * to + 1 - zh], v.rb.at[s, to], ny - 2 + m, other_zh
        )

    def a2(s):
        return copy_of(s, v.sa.at[s], v.r2a.at[s], 2 * ny - 1, other_zh)

    def b2(s, k):
        return copy_of(
            s, v.sb.at[s, k - 1], v.r2b.at[s, k - 1], 2 * ny - 1 + k, 2 * at_y(k) + zh
        )

    def rs_pair(s, m):
        b1(s, m).start()

        @pl.when(m < ny)
        def _():
            a1(s, m).start()

    def rs_forward(s):
        for m in range(1, ny):
            b1(s, m).wait_recv()
            to = at_y(m)
            v.sb[s, m - 1] = (
                v.psend[s, 1, 2 * to + zh].astype(F32) + v.rb[s, to].astype(F32)
            ).astype(BF16)
            b2(s, m).start()
        for k in range(1, ny):
            a1(s, k).wait_recv()
        total = v.psend[s, 0, other_zh].astype(F32)
        for k in range(1, ny):
            total = total + v.ra[s, k - 1, 1 - zh].astype(F32)
        v.sa[s] = total.astype(BF16)
        a2(s).start()
        b1(s, ny).wait_recv()

    def rs_finish(s):
        a2(s).wait()
        for k in range(1, ny):
            b2(s, k).wait()
            a1(s, k).wait_send()
        for m in range(1, ny + 1):
            b1(s, m).wait_send()

    def rs_sum(s, at):
        first = v.psend[s, 0, me_t, at, :].astype(F32) + v.r2a[s, at, :].astype(F32)
        second = v.psend[s, 1, me_t, at, :].astype(F32) + v.rb[s, yy, at, :].astype(F32)
        for k in range(1, ny):
            first = first + v.ra[s, k - 1, zh, at, :].astype(F32)
            second = second + v.r2b[s, k - 1, at, :].astype(F32)
        return jnp.concatenate([first, second], axis=1)

    def ag_copy(s, half, chunk_at, sem, to):
        block = v.agbuf.at[s, :, chunk_at] if s == 1 else v.agbuf.at[s, half, chunk_at]
        return copy_of(s, block, block, sem, to)

    ag0 = 3 * ny - 1
    near_first = sorted(range(1, ny), key=lambda k: min(k, ny - k))

    def gz(s):
        return ag_copy(s, 0, me_t, ag0, other_zh)

    def gy(s, k):
        return ag_copy(s, 0, me_t, ag0 + k, 2 * at_y(k) + zh)

    def fy(s, k):
        return ag_copy(s, 0, other_zh, ag0 + ny - 1 + k, 2 * at_y(k) + zh)

    def by(s, k):
        return ag_copy(s, 1, me_t, ag0 + 2 * ny - 2 + k, 2 * at_y(k) + zh)

    def bz(s, m):
        return ag_copy(s, 1, 2 * at_y(m) + zh, ag0 + 3 * ny - 2 + m, other_zh)

    def place(step):
        return ((step + 1) // 2 * (2 * (step % 2) - 1) + ny) % ny

    def arrived(s, half, chunk_at, sem):
        ag_copy(s, half, chunk_at, sem, other_zh).wait_recv()

    def ag_put(s, at, value):
        v.agbuf[s, 0, me_t, at, :] = value[:, :hd].astype(BF16)
        v.agbuf[s, 1, me_t, at, :] = value[:, hd:].astype(BF16)

    def ag_start(s):
        gz(s).start()
        if s == 0:
            for k in near_first:
                by(s, k).start()
            bz(s, 0).start()
        for k in near_first:
            gy(s, k).start()

    def ag_forward(s):
        arrived(s, 0, other_zh, ag0)
        for k in near_first:
            fy(s, k).start()
        if s == 0:
            for k in near_first:
                arrived(s, 1, 2 * at_y(ny - k) + zh, ag0 + 2 * ny - 2 + k)
                bz(s, ny - k).start()

    def ag_pairs(s, first, last, use, after):
        def one(step, carry):
            m = place(step)
            pair = at_y(m)

            @pl.when(m > 0)
            def _():
                arrived(s, 0, 2 * pair + zh, ag0 + ny - m)
                arrived(s, 0, 2 * pair + 1 - zh, ag0 + 2 * ny - 1 - m)

            if s == 0:
                arrived(s, 1, 2 * pair + 1 - zh, ag0 + 3 * ny - 2 + m)
            for i in range(2):
                src = 2 * pair + i
                for j in range(chunk // ST):
                    at = slice(j * ST, (j + 1) * ST)
                    use(
                        pl.ds(pl.multiple_of(src * chunk + j * ST, ST), ST),
                        jnp.concatenate(
                            [v.agbuf[s, 0, src, at, :], v.agbuf[s, 1, src, at, :]], axis=1
                        ).astype(F32),
                    )
            after(rows_at(pair, 2 * chunk))
            return carry

        lax.fori_loop(first, last, one, 0)

    def ag_sent(s):
        gz(s).wait_send()
        for k in range(1, ny):
            gy(s, k).wait_send()
            fy(s, k).wait_send()
        if s == 0:
            bz(s, 0).wait_send()
            for k in range(1, ny):
                by(s, k).wait_send()
                bz(s, k).wait_send()

    def kv_copy(l, step):
        slot, to = [(rank, other_core), (rank, other_z), (rank - 2, other_core)][step]
        block = v.kv.at[l, slot]
        return remote(block, block, v.kvs.at[l, step], v.kvr.at[l, step], dp=to)

    def kv_in(l, step):
        slot = [rank - 1, rank - 2, rank - 1 - 2 * core][step]
        block = v.kv.at[l, slot]
        return remote(block, block, v.kvs.at[l, step], v.kvr.at[l, step], dp=other_core)

    def dkv_copy(l, step, i):
        at = slice(i * KT, (i + 1) * KT)
        return remote(
            v.dkvo.at[l, step, at],
            v.dkvi.at[l, step, at],
            v.dks.at[l, step, i],
            v.dkr.at[l, step, i],
            dp=other_z if step == 1 else other_core,
        )

    def transpose_block(l, b):
        block = v.kv[l, b].astype(F32)
        v.kt[l, b] = block[:, :width].T.astype(BF16)
        v.vt[l, b] = block[:, width:].T.astype(BF16)

    def qkv_rows(l, at, size):
        mixed = nn(v.h0[l, at, :], v.wqkv[l])
        cosine, sine = v.cosine[at, :], v.sine[at, :]
        q = rotate(mixed[:, :width] + v.bqkv[0, l : l + 1, :], cosine, sine).astype(BF16)
        k = rotate(mixed[:, width : 2 * width] + v.bqkv[1, l : l + 1, :], cosine, sine)
        val = mixed[:, 2 * width :] + v.bqkv[2, l : l + 1, :]
        scaled = (q.astype(F32) * 0.125).astype(BF16)
        v.qm[l, 0, at, :] = head_only(scaled, 0)
        v.qm[l, 1, at, :] = head_only(scaled, 1)
        v.kv[l, rank, at, :width] = k.astype(BF16)
        v.kv[l, rank, at, width:] = val.astype(BF16)

    def kv_send(l):
        @pl.when(zlo == 0)
        def _():
            kv_copy(l, 1).start()

        @pl.when(core == 0)
        def _():
            kv_copy(l, 0).start()

    def kv_near(l):
        transpose_block(l, rank)

        @pl.when(core == 1)
        def _():
            kv_in(l, 0).wait_recv()
            transpose_block(l, rank - 1)

    def kv_far(l):
        @pl.when(zlo == 1)
        def _():
            kv_in(l, 1).wait_recv()
            kv_copy(l, 2).start()
            transpose_block(l, rank - 2)
            kv_in(l, 2).wait_recv()
            transpose_block(l, rank - 1 - 2 * core)

    def feed_forward(l, at, size):
        v.u[l, at, :] = nn(v.h1[l, at, :], v.win[l]) + v.bin[l : l + 1, :]

        def activate(i, carry):
            now = pl.ds(pl.multiple_of(at.start + i * ST, ST), ST)
            u = v.u[l, now, :]
            inner = 0.5 * (1.0 + lax.erf(u * np.float32(0.5**0.5)))
            v.act[l, now, :] = (u * inner).astype(BF16)
            v.u[l, now, :] = inner + u * jnp.exp(-0.5 * u * u) * np.float32((2.0 * np.pi) ** -0.5)
            return carry

        lax.fori_loop(0, size // ST, activate, 0)
        v.part[at, :] = nn(v.act[l, at, :], v.wdown[l])

    def attention(l, s, part):
        for qt in range(rows // QT):
            q_at = slice(qt * QT, (qt + 1) * QT)
            head_rows = [slice(h * HEAD_DIM, (h + 1) * HEAD_DIM) for h in range(2)]

            def block(b, carry, masked):
                keys = v.kv[l, b, :, :width]
                scores = [nt(keys, v.qm[l, h, q_at, :]) for h in range(2)]
                result = []
                for h in range(2):
                    top, total, out = carry[h]
                    sc = scores[h]
                    if masked:
                        key = lax.broadcasted_iota(jnp.int32, sc.shape, 0)
                        query = lax.broadcasted_iota(jnp.int32, sc.shape, 1) + qt * QT
                        sc = jnp.where(key <= query, sc, -1e30)
                    new = jnp.maximum(top, jnp.max(sc, axis=0, keepdims=True))
                    p = jnp.exp(sc - new)
                    fade = jnp.exp(top - new)
                    total = total * fade + jnp.sum(p, axis=0, keepdims=True)
                    out = out * fade + nn(v.vt[l, b, head_rows[h], :], p.astype(BF16))
                    result.append((new, total, out))
                return tuple(result)

            start = (
                jnp.full((1, QT), -1e30, F32),
                jnp.zeros((1, QT), F32),
                jnp.zeros((HEAD_DIM, QT), F32),
            )
            if part == 0:
                carry = block(rank, (start, start), True)
                carry = lax.fori_loop(
                    rank - core, rank, functools.partial(block, masked=False), carry
                )
                for h in range(2):
                    v.top[h : h + 1, q_at] = carry[h][0]
                    v.lse[l, h : h + 1, q_at] = carry[h][1]
                    v.ot[l, head_rows[h], q_at] = carry[h][2]
                continue
            carry = tuple(
                (
                    v.top[h : h + 1, q_at],
                    v.lse[l, h : h + 1, q_at],
                    v.ot[l, head_rows[h], q_at],
                )
                for h in range(2)
            )
            carry = lax.fori_loop(0, 2 * zlo, functools.partial(block, masked=False), carry)
            for h in range(2):
                top, total, out = carry[h]
                v.ot[l, head_rows[h], q_at] = out / total
                v.lse[l, h : h + 1, q_at] = top + jnp.log(total)
            v.ob[l, q_at, :] = v.ot[l, :, q_at].T.astype(BF16)
            both = nn(v.ob[l, q_at, :], v.wout[l]) + v.part[q_at, :]
            both = both.astype(BF16)
            first = qt * QT // chunk
            for half in range(2):
                v.psend[s, half, first : first + QT // chunk] = both[
                    :, half * hd : (half + 1) * hd
                ].reshape(QT // chunk, chunk, hd)
            for pair in range(first // 2, (first + QT // chunk) // 2):
                rs_pair(s, lax.rem(pair - yy - 1 + 2 * ny, ny) + 1)

    def branch_reduce(s):
        rs_finish(s)
        for i in range(chunk // 16):
            at = slice(i * 16, (i + 1) * 16)
            ag_put(s, at, rs_sum(s, at))
        ag_start(s)

    grads = {0: (v.ge, v.r1e, v.r2e, v.s3e, v.r3e, v.k3e), 1: (v.gl, v.r1l, v.r2l, v.s3l, v.r3l, v.k3l)}

    def core_copy(l, p):
        g, r1 = grads[p][:2]
        return remote(
            g.at[l, 1 - core], r1.at[l], v.g1s.at[l, p], v.g1r.at[l, p], dp=other_core
        )

    def x_copy(l, p, k):
        r1, r2 = grads[p][1:3]
        to = lax.rem(xc + k, nx)
        return remote(
            r1.at[l, pl.ds(2 * to, 2)],
            r2.at[l, k - 1],
            v.g2s.at[l, p, k - 1],
            v.g2r.at[l, p, k - 1],
            dp=to * group + zlo * 2 + core,
        )

    def z_copy(l, p):
        return remote(
            grads[p][3].at[l], grads[p][4].at[l], v.g3s.at[l, p], v.g3r.at[l, p], dp=other_z
        )

    def grad_core(l, p):
        core_copy(l, p).start()

    def grad_x(l, p):
        core_copy(l, p).wait()
        g, r1 = grads[p][:2]

        def one(i, carry):
            for j in range(grow // 16):
                at = slice(j * 16, (j + 1) * 16)
                r1[l, i, at, :] = (
                    r1[l, i, at, :].astype(F32) + g[l, core, i, at, :].astype(F32)
                ).astype(BF16)
            return carry

        lax.fori_loop(0, nd // 2, one, 0)
        for k in range(1, nx):
            x_copy(l, p, k).start()

    def grad_z(l, p):
        _, r1, r2, s3, r3, k3 = grads[p]
        for k in range(1, nx):
            x_copy(l, p, k).wait()

        def total(z, at):
            value = r1[l, 2 * xc + z, at, :].astype(F32)
            for k in range(1, nx):
                value = value + r2[l, k - 1, z, at, :].astype(F32)
            return value

        for j in range(grow // 16):
            at = slice(j * 16, (j + 1) * 16)
            s3[l, at, :] = total(1 - zlo, at).astype(BF16)
        z_copy(l, p).start()
        for j in range(grow // 16):
            at = slice(j * 16, (j + 1) * 16)
            k3[l, at, :] = total(zlo, at)

    def grad_end(l, p):
        z_copy(l, p).wait()
        _, _, _, _, r3, k3 = grads[p]
        for j in range(grow // 16):
            at = slice(j * 16, (j + 1) * 16)
            total = k3[l, at, :] + r3[l, at, :].astype(F32)
            if p == 0:
                v.oo[l, at, :] = total[:, :width]
                v.od[l, at, :] = total[:, width : width + ff]
                v.oi[l, at, :] = total[:, width + ff :]
            else:
                for c in range(3):
                    v.oq[l, c, at, :] = total[:, c * width : (c + 1) * width]

    def start_gradient(l, at, gradient):
        v.dz[at, :] = gradient.astype(BF16)

    def attention_back(l, first, second):
        do = v.do[...]
        product = do.astype(F32).T * v.ot[l]
        v.delta[0:1, :] = jnp.sum(product[:HEAD_DIM], axis=0, keepdims=True)
        v.delta[1:2, :] = jnp.sum(product[HEAD_DIM:], axis=0, keepdims=True)
        v.dqt[...] = jnp.zeros_like(v.dqt)

        def piece(b, i, masked):
            at = slice(i * KT, (i + 1) * KT)
            keys = v.kv[l, b, at, :width]
            values = v.kv[l, b, at, width:]
            dk = jnp.zeros((KT, width), F32)
            dv = jnp.zeros((KT, width), F32)
            for h in range(2):
                head_rows = slice(h * HEAD_DIM, (h + 1) * HEAD_DIM)
                sc = nt(keys, v.qm[l, h])
                if masked:
                    key = lax.broadcasted_iota(jnp.int32, sc.shape, 0) + i * KT
                    query = lax.broadcasted_iota(jnp.int32, sc.shape, 1)
                    sc = jnp.where(key <= query, sc, -1e30)
                p = jnp.exp(sc - v.lse[l, h : h + 1, :])
                dp = nt(values, v.dom[h])
                ds = (p * (dp - v.delta[h : h + 1, :])).astype(BF16)
                dv = dv + nn(p.astype(BF16), v.dom[h])
                dk = dk + nn(ds, v.qm[l, h])
                v.dqt[head_rows, :] += nn(v.kt[l, b, head_rows, at], ds)
            return dk, dv

        def far(b, slot, received):
            for i in range(rows // KT):
                dk, dv = piece(b, i, False)
                at = slice(i * KT, (i + 1) * KT)
                if received:
                    dkv_copy(l, 0, i).wait_recv()
                    dk = dk + v.dkvi[l, 0, at, :width].astype(F32)
                    dv = dv + v.dkvi[l, 0, at, width:].astype(F32)
                v.dkvo[l, slot, at, :width] = dk.astype(BF16)
                v.dkvo[l, slot, at, width:] = dv.astype(BF16)
                dkv_copy(l, slot, i).start()

        @pl.when(zlo == 1)
        def _():
            far(1 - core, 0, False)
            first()
            far(core, 1, True)

        @pl.when(core == 1)
        def _():
            far(rank - 1, 2, False)

        @pl.when(rank == group - 1)
        def _():
            second()

        for i in range(rows // KT):
            dk, dv = piece(rank, i, True)
            at = slice(i * KT, (i + 1) * KT)
            v.own[at, :width] = dk
            v.own[at, width:] = dv

    def do_rows(l, at):
        do = nt(v.dz[at, :], v.wout[l]).astype(BF16)
        v.do[at, :] = do
        v.dom[0, at, :] = head_only(do, 0)
        v.dom[1, at, :] = head_only(do, 1)

    def dact_rows(l, at):
        v.dact[at, :] = nt(v.dz[at, :], v.wdown[l])

    def back_rows(l, at, size):
        def slope(i, acc):
            now = pl.ds(pl.multiple_of(at.start + i * ST, ST), ST)
            du = (v.dact[now, :] * v.u[l, now, :]).astype(BF16)
            v.du[now, :] = du
            return acc + jnp.sum(du.astype(F32).reshape(ST // 8, 8, ff), axis=0)

        v.binacc[l] += lax.fori_loop(0, size // ST, slope, jnp.zeros((8, ff), F32))
        v.dh1[at, :] = nt(v.du[at, :], v.win[l])

    def early_grads(l):
        def one(i, carry):
            at = rows_at(i, 2 * grow)
            dzt = v.dz[:, at].astype(F32).T.astype(BF16)
            ht = v.h1[l, :, at].astype(F32).T.astype(BF16)
            wo = nn(dzt, v.ob[l]).astype(BF16)
            wd = nn(dzt, v.act[l]).astype(BF16)
            wi = nn(ht, v.du[...]).astype(BF16)
            for c in range(2):
                part = slice(c * grow, (c + 1) * grow)
                v.ge[l, c, i, :, :width] = wo[part]
                v.ge[l, c, i, :, width : width + ff] = wd[part]
                v.ge[l, c, i, :, width + ff :] = wi[part]
            return carry

        lax.fori_loop(0, depth // (2 * grow), one, 0)

    def late_grads(l):
        def one(i, carry):
            at = rows_at(i, 2 * grow)
            ht = v.h0[l, :, at].astype(F32).T.astype(BF16)
            wq = nn(ht, v.dqkv[...]).astype(BF16)
            for c in range(2):
                v.gl[l, c, i] = wq[c * grow : (c + 1) * grow]
            return carry

        lax.fori_loop(0, depth // (2 * grow), one, 0)

    def qkv_back(l):
        @pl.when(zlo == 0)
        def _():
            grad_x(l, 0)

        for step, here in ((2, core == 0), (1, zlo == 0)):

            @pl.when(here)
            def _():
                for i in range(rows // KT):
                    dkv_copy(l, step, i).wait_recv()
                v.own[...] += v.dkvi[l, step].astype(F32)

        cosine, sine = v.cosine[...], -v.sine[...]
        v.dqkv[:, :width] = rotate(v.dqt[...].T * 0.125, cosine, sine).astype(BF16)
        v.dqkv[:, width : 2 * width] = rotate(v.own[:, :width], cosine, sine).astype(BF16)
        v.dqkv[:, 2 * width : 3 * width] = v.own[:, width:].astype(BF16)
        v.other[4 * l + 3 : 4 * l + 4, : 3 * width] = jnp.sum(
            v.dqkv[...].astype(F32), axis=0, keepdims=True
        )

        def one(i, carry):
            at = rows_at(i, MT)
            v.dh0[at, :] = nt(v.dqkv[at, :], v.wqkv[l])
            return carry

        lax.fori_loop(0, rows // MT, one, 0)

        def send(m, carry):
            pair = at_y(m)
            for i in range(2 * chunk // ST):
                at = pl.ds(pl.multiple_of(pair * 2 * chunk + i * ST, ST), ST)
                both = v.dh0[at, :] * v.gain[l, 0:1, :] + v.dh1[at, :] * v.gain[l, 1:2, :]
                both = both.astype(BF16)
                part = slice(i * ST % chunk, i * ST % chunk + ST)
                for half in range(2):
                    v.psend[0, half, 2 * pair + i * ST // chunk, part, :] = both[
                        :, half * hd : (half + 1) * hd
                    ]
            rs_pair(0, m)
            return carry

        lax.fori_loop(1, ny + 1, send, 0)

    def norm_grads(l):
        v.lnacc[...] = jnp.zeros_like(v.lnacc)

        def fold(value):
            return jnp.sum(value.reshape(2, 8, depth), axis=0)

        def one(i, carry):
            at = rows_at(i, 16)
            xhat = (stream_rows(l, at) - v.mu[l, at, :]) * v.rs[l, at, :]
            first, second = v.dh0[at, :], v.dh1[at, :]
            v.lnacc[0] += fold(first * xhat)
            v.lnacc[1] += fold(second * xhat)
            v.lnacc[2] += fold(first)
            v.lnacc[3] += fold(second)
            v.lnacc[4] += fold(v.dz[at, :].astype(F32))
            return carry

        lax.fori_loop(0, rows // 16, one, 0)
        for i in range(4):
            v.ln[4 * l + i : 4 * l + i + 1, :] = jnp.sum(v.lnacc[i], axis=0, keepdims=True)
        column = jnp.sum(v.lnacc[4], axis=0, keepdims=True)
        v.other[4 * l : 4 * l + 1, :] = column[:, :ff]
        v.other[4 * l + 1 : 4 * l + 2, :] = column[:, ff:]
        v.other[4 * l + 2 : 4 * l + 3, :] = jnp.sum(v.binacc[l], axis=0, keepdims=True)

    def stream_reduce(l):
        rs_finish(0)
        for i in range(chunk // 16):
            at = pl.ds(pl.multiple_of(me_t * chunk + i * 16, 16), 16)
            gd = rs_sum(0, slice(i * 16, (i + 1) * 16))
            r = v.rs[l, at, :]
            xhat = (stream_rows(l, at) - v.mu[l, at, :]) * r
            mean = jnp.mean(gd, axis=-1, keepdims=True)
            along = jnp.mean(gd * xhat, axis=-1, keepdims=True)
            dx = r * (gd - mean - xhat * along)
            ag_put(0, slice(i * 16, (i + 1) * 16), dx)
        ag_start(0)

    def small_core(i):
        mine, theirs = [(v.ln, v.ln1), (v.other, v.other1)][i]
        return remote(mine, theirs, v.s1s.at[i], v.s1r.at[i], dp=other_core)

    def small_dp(k, i):
        to = lax.rem(me_d + 2 * k, nd)
        mine, theirs = [(v.lnsum, v.ln3), (v.other, v.other2)][i]
        return remote(mine, theirs.at[k - 1], v.s3s.at[i, k - 1], v.s3r.at[i, k - 1], dp=to)

    def small_scatter(k):
        to = lax.rem(me_t + k, nt_dev)
        columns = pl.ds(pl.multiple_of(to * LANES, LANES), LANES)
        return remote(
            v.ln.at[:, columns], v.ln2.at[k - 1], v.s2s.at[k - 1], v.s2r.at[k - 1], tensor=to
        )

    def small_gather(k):
        to = lax.rem(me_t + k, nt_dev)
        block = v.lnall.at[me_t]
        return remote(block, block, v.s4s.at[k - 1], v.s4r.at[me_t], tensor=to)

    def small_start():
        for i in range(2):
            small_core(i).start()

    def small_second():
        for i in range(2):
            small_core(i).wait()
        v.ln[...] += v.ln1[...]
        v.other[...] += v.other1[...]
        for k in range(1, nt_dev):
            small_scatter(k).start()
        for k in range(1, nd // 2):
            small_dp(k, 1).start()

    def small_third():
        mine = pl.ds(pl.multiple_of(me_t * LANES, LANES), LANES)
        total = v.ln[:, mine]
        for k in range(1, nt_dev):
            small_scatter(k).wait()
            total = total + v.ln2[k - 1]
        v.lnsum[...] = total
        for k in range(1, nd // 2):
            small_dp(k, 0).start()

    def small_fourth():
        total = v.lnsum[...]
        for k in range(1, nd // 2):
            small_dp(k, 0).wait()
            total = total + v.ln3[k - 1]
        v.lnall[me_t] = total
        for k in range(1, nt_dev):
            small_gather(k).start()
        total = v.other[...]
        for k in range(1, nd // 2):
            small_dp(k, 1).wait()
            total = total + v.other2[k - 1]
        for l in range(LAYERS):
            for half in range(2):
                at = slice(half * ff, (half + 1) * ff)
                row = total[4 * l + half : 4 * l + half + 1, :]
                v.obout[l : l + 1, at] = row
                v.obdown[l : l + 1, at] = row
            v.obin[l : l + 1, :] = total[4 * l + 2 : 4 * l + 3, :]
            for c in range(3):
                at = slice(c * width, (c + 1) * width)
                v.obqkv[c, l : l + 1, :] = total[4 * l + 3 : 4 * l + 4, at]

    def small_end():
        for k in range(1, nt_dev):
            src = lax.rem(me_t + k, nt_dev)
            block = v.lnall.at[src]
            remote(block, block, v.s4s.at[k - 1], v.s4r.at[src], tensor=src).wait()
        for j in range(nt_dev):
            at = slice(j * LANES, (j + 1) * LANES)
            block = v.lnall[j]
            for l in range(LAYERS):
                v.ogain[l, :, at] = block[4 * l : 4 * l + 2, :]
                v.obias[l, :, at] = block[4 * l + 2 : 4 * l + 4, :]

    def nothing(at):
        pass

    def first_norm(i, carry):
        at = rows_at(i, ST)
        norm_rows(0, at, v.xt[at, :].astype(F32))
        return carry

    with jax.named_scope("norm0"):
        for i in range(TP):
            load_tok[i].wait()
            lax.fori_loop(i * rows // TP // ST, (i + 1) * rows // TP // ST, first_norm, 0, unroll=2)
    with jax.named_scope("qkv0"):
        for c in load_qkv[0]:
            c.wait()
        load_cos.wait()
        load_sin.wait()

        def first_qkv(i, carry):
            qkv_rows(0, rows_at(i, MT), MT)
            return carry

        lax.fori_loop(0, rows // MT, first_qkv, 0)
    with jax.named_scope("barrier"):
        pl.semaphore_wait(barrier, nt_dev - 1 + nd - 1)
    kv_send(0)
    v.ln[...] = jnp.zeros_like(v.ln)
    v.other[...] = jnp.zeros_like(v.other)
    v.binacc[...] = jnp.zeros_like(v.binacc)
    with jax.named_scope("ffn0"):
        for c in load_rest[0]:
            c.wait()

        def first_ffn(i, carry):
            feed_forward(0, rows_at(i, MT), MT)
            return carry

        lax.fori_loop(0, rows // MT, first_ffn, 0)
    with jax.named_scope("near0"):
        kv_near(0)
        attention(0, 0, 0)
    def first_gradients(z):
        @pl.when(zlo == z)
        def _():
            load_cot.wait()
            for c in load_rest[1]:
                c.wait()

            def copy_rows(i, carry):
                at = rows_at(i, ST)
                v.dz[at, :] = v.ct[at, :]
                v.g[at, :] = v.ct[at, :].astype(F32)
                return carry

            def rows_back(i, carry):
                at = rows_at(i, MT)
                do_rows(1, at)
                dact_rows(1, at)
                return carry

            lax.fori_loop(0, rows // ST, copy_rows, 0)
            lax.fori_loop(0, rows // MT, rows_back, 0)

    with jax.named_scope("dz1"):
        first_gradients(1)
    with jax.named_scope("kv0"):
        kv_far(0)
    with jax.named_scope("attn0"):
        attention(0, 0, 1)
    with jax.named_scope("dz1b"):
        first_gradients(0)
    with jax.named_scope("forward0"):
        rs_forward(0)
    with jax.named_scope("reduce0"):
        branch_reduce(0)

    def next_stream(at, z):
        x = v.xt[at, :].astype(F32) + (z + (v.bout[0:1, :] + v.bdown[0:1, :]))
        v.x[at, :] = x
        norm_rows(1, at, x)

    def next_qkv(at):
        qkv_rows(1, at, 2 * chunk)

    def next_ffn(at):
        feed_forward(1, at, 2 * chunk)
        back_rows(1, at, 2 * chunk)

    def next_both(at):
        next_qkv(at)
        next_ffn(at)

    with jax.named_scope("gather0"):
        for c in load_qkv[1]:
            c.wait()
        ag_forward(0)
        ag_pairs(0, 0, ny - 1, next_stream, next_both)
        ag_pairs(0, ny - 1, ny, next_stream, next_qkv)
        kv_send(1)
        ag_sent(0)
    with jax.named_scope("ffn1"):
        next_ffn(rows_at(at_y(place(ny - 1)), 2 * chunk))
    with jax.named_scope("near1"):
        kv_near(1)
        attention(1, 1, 0)
    with jax.named_scope("kv1"):
        kv_far(1)
    with jax.named_scope("attn1"):
        attention(1, 1, 1)

    with jax.named_scope("attn_grad1"):
        attention_back(1, lambda: None, lambda: rs_forward(1))

        @pl.when(rank != group - 1)
        def _():
            rs_forward(1)


    def forward_at(z):
        @pl.when(zlo == z)
        def _():
            rs_forward(0)

    def late_x(l):
        @pl.when(zlo == 1)
        def _():
            grad_x(l, 0)

    def early(l, z):
        @pl.when(zlo == z)
        def _():
            early_grads(l)
            grad_core(l, 0)

    with jax.named_scope("early1"):
        early(1, 0)
    with jax.named_scope("qkv_grad1"):
        qkv_back(1)
    with jax.named_scope("early1b"):
        early(1, 1)
    with jax.named_scope("norm_grad1"):
        norm_grads(1)
    with jax.named_scope("forward"):
        forward_at(1)
    with jax.named_scope("gx10"):
        late_x(1)
    with jax.named_scope("late1"):
        late_grads(1)
        grad_core(1, 1)
    with jax.named_scope("forward"):
        forward_at(0)
    with jax.named_scope("gx11"):
        grad_x(1, 1)
    with jax.named_scope("stream_reduce1"):
        stream_reduce(1)

    def next_gradient(at, dx):
        gradient = v.g[at, :] + dx
        v.g[at, :] = gradient
        v.dz[at, :] = gradient.astype(BF16)

    def next_back(at):
        do_rows(0, at)
        dact_rows(0, at)
        back_rows(0, at, 2 * chunk)

    with jax.named_scope("gather2"):
        ag_forward(0)
        branch_reduce(1)
        ag_pairs(0, 0, ny, next_gradient, next_back)
        ag_sent(0)
    with jax.named_scope("attn_grad0"):
        attention_back(0, lambda: ag_forward(1), lambda: None)
    with jax.named_scope("forward1b"):

        @pl.when(zlo == 0)
        def _():
            ag_forward(1)

    with jax.named_scope("early0"):
        early(0, 0)
    with jax.named_scope("qkv_grad0"):
        qkv_back(0)
    with jax.named_scope("early0b"):
        early(0, 1)
    with jax.named_scope("norm_grad0"):
        norm_grads(0)
        small_start()
    with jax.named_scope("gx00"):
        late_x(0)
    with jax.named_scope("forward"):
        forward_at(1)
    with jax.named_scope("small_second"):
        small_second()
    with jax.named_scope("late0"):
        late_grads(0)
        grad_core(0, 1)
    with jax.named_scope("forward"):
        forward_at(0)
    with jax.named_scope("gx01"):
        grad_x(0, 1)
    with jax.named_scope("gz1"):
        grad_z(1, 0)
        grad_z(1, 1)

    def last_stream(at, z):
        v.x[at, :] = v.x[at, :] + (z + (v.bout[1:2, :] + v.bdown[1:2, :]))

    store_x = pltpu.make_async_copy(v.x, v.ox, v.lsem.at[0])
    store_g = pltpu.make_async_copy(v.g, v.og, v.lsem.at[1])
    with jax.named_scope("stream_reduce0"):
        stream_reduce(0)
    with jax.named_scope("forward0c"):
        ag_forward(0)
    with jax.named_scope("small_third"):
        small_third()
    with jax.named_scope("gather1"):
        ag_pairs(1, 0, ny, last_stream, nothing)
        ag_sent(1)
        store_x.start()
    with jax.named_scope("gend1"):
        grad_end(1, 0)
        grad_end(1, 1)

    def last_gradient(at, dx):
        v.g[at, :] = v.g[at, :] + dx

    with jax.named_scope("gather3"):
        ag_pairs(0, 0, ny - 1, last_gradient, nothing)
    with jax.named_scope("small_fourth"):
        small_fourth()
    with jax.named_scope("gz0"):
        grad_z(0, 0)
        grad_z(0, 1)
    with jax.named_scope("gather3b"):
        ag_pairs(0, ny - 1, ny, last_gradient, nothing)
        store_g.start()
        ag_sent(0)
    with jax.named_scope("small_end"):
        small_end()
    with jax.named_scope("gend0"):
        grad_end(0, 0)
        grad_end(0, 1)
        store_x.wait()
        store_g.wait()
    for l in range(LAYERS):
        for step, here in ((0, core == 0), (1, zlo == 0), (2, zlo == 1)):

            @pl.when(here)
            def _():
                kv_copy(l, step).wait_send()

        for step, here in ((0, zlo == 1), (1, zlo == 1), (2, core == 1)):

            @pl.when(here)
            def _():
                for i in range(rows // KT):
                    dkv_copy(l, step, i).wait_send()


def store_kernel(count, *refs):
    given, kept, held = refs[:count], refs[count : 2 * count], refs[2 * count : 3 * count]
    sems = refs[3 * count]
    parts = []
    for i in range(count):
        pieces = PARTS if i < 2 else 1
        rows = held[i].shape[0] // pieces
        parts += [(i, slice(j * rows, (j + 1) * rows)) for j in range(pieces)]
    loads = [
        pltpu.make_async_copy(given[i].at[at], held[i].at[at], sems.at[0, n])
        for n, (i, at) in enumerate(parts)
    ]
    stores = [
        pltpu.make_async_copy(held[i].at[at], kept[i].at[at], sems.at[1, n])
        for n, (i, at) in enumerate(parts)
    ]
    for copy in loads:
        copy.start()
    for load, store in zip(loads, stores):
        load.wait()
        store.start()
    for copy in stores:
        copy.wait()


def on_device(nt_dev, nd, *args):
    tokens, cotangent, ln_gain, ln_bias, w_qkv, b_qkv, w_out, b_out, w_in, b_in, w_down, b_down = args
    rows, depth = tokens.shape
    width = w_out.shape[1]
    ff = w_in.shape[2]
    group = SEQ // rows
    chunk = rows // nt_dev
    grow = depth // nd
    half = nd // 2
    nx = nd // group
    early = width + 2 * ff
    late = 3 * width
    cosine, sine = rope_constants()
    vm = pltpu.VMEM
    dma = pltpu.SemaphoreType.DMA
    two = LAYERS
    scratch = [
        vm((two, depth, 3 * width), BF16),
        vm((two, width, depth), BF16),
        vm((two, depth, ff), BF16),
        vm((two, ff, depth), BF16),
        vm((rows, LANES), F32),
        vm((rows, LANES), F32),
        vm((rows, depth), F32),
        vm((rows, depth), F32),
        vm((rows, depth), BF16),
        vm((rows, depth), BF16),
        vm((two, rows, depth), BF16),
        vm((two, rows, depth), BF16),
        vm((two, 2, rows, width), BF16),
        vm((two, group, rows, 2 * width), BF16),
        vm((two, group, width, rows), BF16),
        vm((two, group, width, rows), BF16),
        vm((two, rows, width), BF16),
        vm((two, width, rows), F32),
        vm((8, rows), F32),
        vm((two, 8, rows), F32),
        vm((two, rows, ff), F32),
        vm((two, rows, ff), BF16),
        vm((two, rows, 1), F32),
        vm((two, rows, 1), F32),
        vm((rows, depth), F32),
        vm((2, 2, nt_dev, chunk, depth // 2), BF16),
        vm((2, nt_dev // 2 - 1, 2, chunk, depth // 2), BF16),
        vm((2, nt_dev // 2, chunk, depth // 2), BF16),
        vm((2, chunk, depth // 2), BF16),
        vm((2, nt_dev // 2 - 1, chunk, depth // 2), BF16),
        vm((2, chunk, depth // 2), BF16),
        vm((2, nt_dev // 2 - 1, chunk, depth // 2), BF16),
        vm((2, 2, nt_dev, chunk, depth // 2), BF16),
        vm((rows, depth), BF16),
        vm((rows, width), BF16),
        vm((2, rows, width), BF16),
        vm((8, rows), F32),
        vm((width, rows), F32),
        vm((two, 3, rows, 2 * width), BF16),
        vm((two, 3, rows, 2 * width), BF16),
        vm((rows, 2 * width), F32),
        vm((rows, 3 * width), BF16),
        vm((rows, ff), BF16),
        vm((rows, ff), F32),
        vm((two, 8, ff), F32),
        vm((rows, depth), F32),
        vm((rows, depth), F32),
        vm((two, 2, half, grow, early), BF16),
        vm((two, 2, half, grow, late), BF16),
        vm((two, half, grow, early), BF16),
        vm((two, half, grow, late), BF16),
        vm((two, nx - 1, 2, grow, early), BF16),
        vm((two, nx - 1, 2, grow, late), BF16),
        vm((two, grow, early), BF16),
        vm((two, grow, late), BF16),
        vm((two, grow, early), BF16),
        vm((two, grow, late), BF16),
        vm((two, grow, early), F32),
        vm((two, grow, late), F32),
        vm((8, depth), F32),
        vm((8, ff), F32),
        vm((8, depth), F32),
        vm((8, ff), F32),
        vm((nt_dev - 1, 8, LANES), F32),
        vm((half - 1, 8, ff), F32),
        vm((8, LANES), F32),
        vm((half - 1, 8, LANES), F32),
        vm((nt_dev, 8, LANES), F32),
        vm((5, 8, depth), F32),
        dma((16 + TP,)),
        dma((two, 3)),
        dma((two, 3)),
        dma((two, 3, rows // KT)),
        dma((two, 3, rows // KT)),
        dma((2, 7 * (nt_dev // 2) - 3)),
        dma((2, 7 * (nt_dev // 2) - 3)),
        dma((two, 2)),
        dma((two, 2)),
        dma((two, 2, nx - 1)),
        dma((two, 2, nx - 1)),
        dma((two, 2)),
        dma((two, 2)),
        dma((2,)),
        dma((2,)),
        dma((nt_dev - 1,)),
        dma((nt_dev - 1,)),
        dma((2, half - 1)),
        dma((2, half - 1)),
        dma((nt_dev - 1,)),
        dma((nt_dev,)),
    ]
    here = pl.BlockSpec(memory_space=pltpu.VMEM)
    away = pl.BlockSpec(memory_space=pl.ANY)
    shapes = [
        (rows, depth),
        (rows, depth),
        (two, 2, depth),
        (two, 2, depth),
        (3, two, width),
        (two, depth),
        (two, ff),
        (two, depth),
        (two, 3, grow, width),
        (two, grow, width),
        (two, grow, ff),
        (two, grow, ff),
    ]
    out = pl.pallas_call(
        functools.partial(step_kernel, nt_dev, nd),
        out_shape=[jax.ShapeDtypeStruct(s, F32) for s in shapes],
        in_specs=[away, away, here, here, away, here, away, here, away, here, away, here, away, away],
        out_specs=[away] * 2 + [here] * (len(shapes) - 2),
        scratch_shapes=scratch,
        compiler_params=pltpu.CompilerParams(
            collective_id=0, has_side_effects=True, vmem_limit_bytes=64 * 1024 * 1024 - 65536
        ),
    )(
        tokens,
        cotangent,
        ln_gain,
        ln_bias,
        w_qkv.transpose(0, 2, 1, 3),
        b_qkv.transpose(1, 0, 2),
        w_out,
        b_out,
        w_in,
        b_in,
        w_down,
        b_down,
        jnp.asarray(cosine),
        jnp.asarray(sine),
    )
    out = pl.pallas_call(
        functools.partial(store_kernel, len(shapes)),
        out_shape=[jax.ShapeDtypeStruct(s, F32) for s in shapes],
        in_specs=[away] * len(shapes),
        out_specs=[away] * len(shapes),
        scratch_shapes=[vm(s, F32) for s in shapes] + [dma((2, 2 * PARTS + len(shapes)))],
    )(*out)
    x, g, gain, bias, bqkv, bout, b_in_g, bdown, wq, wo, wi, wd = out
    return (
        x,
        g,
        gain,
        bias,
        wq.transpose(0, 2, 1, 3),
        bqkv.transpose(1, 0, 2),
        wo.transpose(0, 2, 1),
        bout,
        wi,
        b_in_g,
        wd.transpose(0, 2, 1),
        bdown,
    )


def solution(mesh):
    return jax.shard_map(
        functools.partial(on_device, mesh.shape["tensor"], mesh.shape["dp"]),
        mesh=mesh,
        in_specs=(
            P("dp", None),
            P("dp", None),
            P(),
            P(),
            P(None, None, None, "tensor"),
            P(None, None, "tensor"),
            P(None, "tensor", None),
            P(),
            P(None, None, "tensor"),
            P(None, "tensor"),
            P(None, "tensor", None),
            P(),
        ),
        out_specs=(
            P("dp", None),
            P("dp", None),
            P(),
            P(),
            P(None, "dp", None, "tensor"),
            P(None, None, "tensor"),
            P(None, "tensor", "dp"),
            P(),
            P(None, "dp", "tensor"),
            P(None, "tensor"),
            P(None, "tensor", "dp"),
            P(),
        ),
        check_vma=False,
    )
```

```python
import functools

import jax
import jax.numpy as jnp
import numpy as np
from jax import lax
from jax.experimental import pallas as pl
from jax.experimental.pallas import tpu as pltpu
from jax.sharding import PartitionSpec as P

HEAD_DIM = 64
ROT = 16
SEQ = 2048
LAYERS = 2
EPS = 1e-05
F32 = jnp.float32
BF16 = jnp.bfloat16
MESH = pl.DeviceIdType.MESH
LANES = 128
QT = 256
KT = 256
MT = 256
ST = 32
TP = 4
PARTS = 4


def nn(a, b):
    return jnp.dot(a, b, preferred_element_type=F32)


def nt(a, b):
    return lax.dot_general(a, b, (((1,), (1,)), ((), ())), preferred_element_type=F32)


def rope_constants():
    half = ROT // 2
    exponent = np.arange(0, ROT, 2).astype(np.float32) / np.float32(ROT)
    inverse = (np.float32(1.0) / np.float32(10000.0) ** exponent).astype(np.float32)
    angles = np.arange(SEQ).astype(np.float32)[:, None] * inverse[None, :]
    cosine = np.ones((SEQ, LANES), np.float32)
    sine = np.zeros((SEQ, LANES), np.float32)
    for start in range(0, LANES, HEAD_DIM):
        cosine[:, start : start + half] = np.cos(angles)
        cosine[:, start + half : start + ROT] = np.cos(angles)
        sine[:, start : start + half] = -np.sin(angles)
        sine[:, start + half : start + ROT] = np.sin(angles)
    return cosine, sine


def rotate(values, cosine, sine):
    half = ROT // 2
    lane = lax.broadcasted_iota(jnp.int32, values.shape, 1)
    partner = jnp.where(
        lane % HEAD_DIM < half,
        pltpu.roll(values, LANES - half, 1),
        pltpu.roll(values, half, 1),
    )
    return values * cosine + partner * sine


def head_only(values, head):
    lane = lax.broadcasted_iota(jnp.int32, values.shape, 1)
    return jnp.where(lane // HEAD_DIM == head, values, jnp.zeros_like(values))


def rows_at(step, size):
    return pl.ds(pl.multiple_of(step * size, size), size)


def remote(src, dst, send_sem, recv_sem, **device):
    return pltpu.make_async_remote_copy(
        src_ref=src,
        dst_ref=dst,
        send_sem=send_sem,
        recv_sem=recv_sem,
        device_id=device,
        device_id_type=MESH,
    )


class Refs:
    pass


def step_kernel(nt_dev, nd, *refs):
    names = (
        "tok", "cot", "gain", "bias", "wqkv_h", "bqkv", "wout_h", "bout", "win_h", "bin",
        "wdown_h", "bdown", "cos_h", "sin_h", "ox", "og", "ogain", "obias", "obqkv", "obout",
        "obin", "obdown", "oq", "oo", "oi", "od", "wqkv", "wout", "win", "wdown", "cosine",
        "sine", "x", "g", "xt", "ct", "h0", "h1", "qm", "kv", "kt", "vt", "ob", "ot", "top",
        "lse", "u", "act", "mu", "rs", "part", "psend", "ra", "rb", "sa", "sb", "r2a", "r2b",
        "agbuf", "dz", "do", "dom", "delta", "dqt", "dkvo", "dkvi", "own", "dqkv", "du", "dact",
        "binacc", "dh0", "dh1", "ge", "gl", "r1e", "r1l", "r2e", "r2l", "s3e", "s3l", "r3e",
        "r3l", "k3e", "k3l", "ln", "other", "ln1", "other1", "ln2", "other2", "lnsum", "ln3",
        "lnall", "lnacc", "lsem", "kvs", "kvr", "dks", "dkr", "ars", "arr", "g1s", "g1r", "g2s",
        "g2r", "g3s", "g3r", "s1s", "s1r", "s2s", "s2r", "s3s", "s3r", "s4s", "s4r",
    )
    assert len(names) == len(refs)
    v = Refs()
    v.__dict__.update(zip(names, refs))
    rows, depth = v.x.shape
    group = SEQ // rows
    nx = nd // group
    chunk = rows // nt_dev
    grow = depth // nd
    width = v.wout.shape[1]
    ff = v.win.shape[2]

    me_t = lax.axis_index("tensor")
    me_d = lax.axis_index("dp")
    rank = lax.rem(me_d, group)
    core = lax.rem(me_d, 2)
    zlo = lax.rem(me_d // 2, 2)
    xc = me_d // group
    ny = nt_dev // 2
    hd = depth // 2
    yy = me_t // 2
    zh = lax.rem(me_t, 2)
    other_zh = me_t + 1 - 2 * zh
    other_core = me_d + 1 - 2 * core
    other_z = me_d + 2 - 4 * zlo

    barrier = pltpu.get_barrier_semaphore()
    for k in range(1, nt_dev):
        pl.semaphore_signal(
            barrier, inc=1, device_id={"tensor": lax.rem(me_t + k, nt_dev)}, device_id_type=MESH
        )
    for k in range(1, nd):
        pl.semaphore_signal(
            barrier, inc=1, device_id={"dp": lax.rem(me_d + k, nd)}, device_id_type=MESH
        )

    parts = [slice(i * rows // TP, (i + 1) * rows // TP) for i in range(TP)]

    def load(src, dst, index):
        copy = pltpu.make_async_copy(src, dst, v.lsem.at[index])
        copy.start()
        return copy

    load_tok = [load(v.tok.at[at], v.xt.at[at], 16 + i) for i, at in enumerate(parts)]
    load_cos = load(v.cos_h.at[rows_at(rank, rows)], v.cosine, 1)
    load_sin = load(v.sin_h.at[rows_at(rank, rows)], v.sine, 2)
    load_qkv = []
    load_rest = []
    for l in range(LAYERS):
        load_qkv.append(
            [
                load(
                    v.wqkv_h.at[l, c],
                    v.wqkv.at[l, :, pl.ds(c * width, width)],
                    4 + 6 * l + c,
                )
                for c in range(3)
            ]
        )
        load_rest.append(
            [
                load(v.win_h.at[l], v.win.at[l], 4 + 6 * l + 3),
                load(v.wdown_h.at[l], v.wdown.at[l], 4 + 6 * l + 4),
                load(v.wout_h.at[l], v.wout.at[l], 4 + 6 * l + 5),
            ]
        )
    load_cot = load(v.cot, v.ct, 3)

    def norm_rows(l, at, x):
        mean = jnp.mean(x, axis=-1, keepdims=True)
        center = x - mean
        spread = jnp.mean(center * center, axis=-1, keepdims=True)
        r = lax.rsqrt(spread + EPS)
        xhat = center * r
        v.mu[l, at, :] = mean
        v.rs[l, at, :] = r
        v.h0[l, at, :] = (xhat * v.gain[l, 0:1, :] + v.bias[l, 0:1, :]).astype(BF16)
        v.h1[l, at, :] = (xhat * v.gain[l, 1:2, :] + v.bias[l, 1:2, :]).astype(BF16)

    def stream_rows(l, at):
        if l == 0:
            return v.xt[at, :].astype(F32)
        return v.x[at, :]

    def at_y(k):
        return lax.rem(yy + k, ny)

    def copy_of(s, src, dst, sem, to):
        return remote(src, dst, v.ars.at[s, sem], v.arr.at[s, sem], tensor=to)

    def a1(s, k):
        to = at_y(k)
        return copy_of(
            s, v.psend.at[s, 0, pl.ds(2 * to, 2)], v.ra.at[s, k - 1], k - 1, 2 * to + zh
        )

    def b1(s, m):
        to = at_y(m)
        return copy_of(
            s, v.psend.at[s, 1, 2 * to + 1 - zh], v.rb.at[s, to], ny - 2 + m, other_zh
        )

    def a2(s):
        return copy_of(s, v.sa.at[s], v.r2a.at[s], 2 * ny - 1, other_zh)

    def b2(s, k):
        return copy_of(
            s, v.sb.at[s, k - 1], v.r2b.at[s, k - 1], 2 * ny - 1 + k, 2 * at_y(k) + zh
        )

    def rs_pair(s, m):
        b1(s, m).start()

        @pl.when(m < ny)
        def _():
            a1(s, m).start()

    def rs_forward(s):
        for m in range(1, ny):
            b1(s, m).wait_recv()
            to = at_y(m)
            v.sb[s, m - 1] = (
                v.psend[s, 1, 2 * to + zh].astype(F32) + v.rb[s, to].astype(F32)
            ).astype(BF16)
            b2(s, m).start()
        for k in range(1, ny):
            a1(s, k).wait_recv()
        total = v.psend[s, 0, other_zh].astype(F32)
        for k in range(1, ny):
            total = total + v.ra[s, k - 1, 1 - zh].astype(F32)
        v.sa[s] = total.astype(BF16)
        a2(s).start()
        b1(s, ny).wait_recv()

    def rs_finish(s):
        a2(s).wait()
        for k in range(1, ny):
            b2(s, k).wait()
            a1(s, k).wait_send()
        for m in range(1, ny + 1):
            b1(s, m).wait_send()

    def rs_sum(s, at):
        first = v.psend[s, 0, me_t, at, :].astype(F32) + v.r2a[s, at, :].astype(F32)
        second = v.psend[s, 1, me_t, at, :].astype(F32) + v.rb[s, yy, at, :].astype(F32)
        for k in range(1, ny):
            first = first + v.ra[s, k - 1, zh, at, :].astype(F32)
            second = second + v.r2b[s, k - 1, at, :].astype(F32)
        return jnp.concatenate([first, second], axis=1)

    def ag_copy(s, half, chunk_at, sem, to):
        block = v.agbuf.at[s, :, chunk_at] if s == 1 else v.agbuf.at[s, half, chunk_at]
        return copy_of(s, block, block, sem, to)

    ag0 = 3 * ny - 1
    near_first = sorted(range(1, ny), key=lambda k: min(k, ny - k))

    def gz(s):
        return ag_copy(s, 0, me_t, ag0, other_zh)

    def gy(s, k):
        return ag_copy(s, 0, me_t, ag0 + k, 2 * at_y(k) + zh)

    def fy(s, k):
        return ag_copy(s, 0, other_zh, ag0 + ny - 1 + k, 2 * at_y(k) + zh)

    def by(s, k):
        return ag_copy(s, 1, me_t, ag0 + 2 * ny - 2 + k, 2 * at_y(k) + zh)

    def bz(s, m):
        return ag_copy(s, 1, 2 * at_y(m) + zh, ag0 + 3 * ny - 2 + m, other_zh)

    def place(step):
        return ((step + 1) // 2 * (2 * (step % 2) - 1) + ny) % ny

    def arrived(s, half, chunk_at, sem):
        ag_copy(s, half, chunk_at, sem, other_zh).wait_recv()

    def ag_put(s, at, value):
        v.agbuf[s, 0, me_t, at, :] = value[:, :hd].astype(BF16)
        v.agbuf[s, 1, me_t, at, :] = value[:, hd:].astype(BF16)

    def ag_start(s):
        gz(s).start()
        if s == 0:
            for k in near_first:
                by(s, k).start()
            bz(s, 0).start()
        for k in near_first:
            gy(s, k).start()

    def ag_forward(s):
        arrived(s, 0, other_zh, ag0)
        for k in near_first:
            fy(s, k).start()
        if s == 0:
            for k in near_first:
                arrived(s, 1, 2 * at_y(ny - k) + zh, ag0 + 2 * ny - 2 + k)
                bz(s, ny - k).start()

    def ag_pairs(s, first, last, use, after):
        def one(step, carry):
            m = place(step)
            pair = at_y(m)

            @pl.when(m > 0)
            def _():
                arrived(s, 0, 2 * pair + zh, ag0 + ny - m)
                arrived(s, 0, 2 * pair + 1 - zh, ag0 + 2 * ny - 1 - m)

            if s == 0:
                arrived(s, 1, 2 * pair + 1 - zh, ag0 + 3 * ny - 2 + m)
            for i in range(2):
                src = 2 * pair + i
                for j in range(chunk // ST):
                    at = slice(j * ST, (j + 1) * ST)
                    use(
                        pl.ds(pl.multiple_of(src * chunk + j * ST, ST), ST),
                        jnp.concatenate(
                            [v.agbuf[s, 0, src, at, :], v.agbuf[s, 1, src, at, :]], axis=1
                        ).astype(F32),
                    )
            after(rows_at(pair, 2 * chunk))
            return carry

        lax.fori_loop(first, last, one, 0)

    def ag_sent(s):
        gz(s).wait_send()
        for k in range(1, ny):
            gy(s, k).wait_send()
            fy(s, k).wait_send()
        if s == 0:
            bz(s, 0).wait_send()
            for k in range(1, ny):
                by(s, k).wait_send()
                bz(s, k).wait_send()

    def kv_copy(l, step):
        slot, to = [(rank, other_core), (rank, other_z), (rank - 2, other_core)][step]
        block = v.kv.at[l, slot]
        return remote(block, block, v.kvs.at[l, step], v.kvr.at[l, step], dp=to)

    def kv_in(l, step):
        slot = [rank - 1, rank - 2, rank - 1 - 2 * core][step]
        block = v.kv.at[l, slot]
        return remote(block, block, v.kvs.at[l, step], v.kvr.at[l, step], dp=other_core)

    def dkv_copy(l, step, i):
        at = slice(i * KT, (i + 1) * KT)
        return remote(
            v.dkvo.at[l, step, at],
            v.dkvi.at[l, step, at],
            v.dks.at[l, step, i],
            v.dkr.at[l, step, i],
            dp=other_z if step == 1 else other_core,
        )

    def transpose_block(l, b):
        block = v.kv[l, b].astype(F32)
        v.kt[l, b] = block[:, :width].T.astype(BF16)
        v.vt[l, b] = block[:, width:].T.astype(BF16)

    def qkv_rows(l, at, size):
        mixed = nn(v.h0[l, at, :], v.wqkv[l])
        cosine, sine = v.cosine[at, :], v.sine[at, :]
        q = rotate(mixed[:, :width] + v.bqkv[0, l : l + 1, :], cosine, sine).astype(BF16)
        k = rotate(mixed[:, width : 2 * width] + v.bqkv[1, l : l + 1, :], cosine, sine)
        val = mixed[:, 2 * width :] + v.bqkv[2, l : l + 1, :]
        scaled = (q.astype(F32) * 0.125).astype(BF16)
        v.qm[l, 0, at, :] = head_only(scaled, 0)
        v.qm[l, 1, at, :] = head_only(scaled, 1)
        v.kv[l, rank, at, :width] = k.astype(BF16)
        v.kv[l, rank, at, width:] = val.astype(BF16)

    def kv_send(l):
        @pl.when(zlo == 0)
        def _():
            kv_copy(l, 1).start()

        @pl.when(core == 0)
        def _():
            kv_copy(l, 0).start()

    def kv_near(l):
        transpose_block(l, rank)

        @pl.when(core == 1)
        def _():
            kv_in(l, 0).wait_recv()
            transpose_block(l, rank - 1)

    def kv_far(l):
        @pl.when(zlo == 1)
        def _():
            kv_in(l, 1).wait_recv()
            kv_copy(l, 2).start()
            transpose_block(l, rank - 2)
            kv_in(l, 2).wait_recv()
            transpose_block(l, rank - 1 - 2 * core)

    def feed_forward(l, at, size):
        v.u[l, at, :] = nn(v.h1[l, at, :], v.win[l]) + v.bin[l : l + 1, :]

        def activate(i, carry):
            now = pl.ds(pl.multiple_of(at.start + i * ST, ST), ST)
            u = v.u[l, now, :]
            inner = 0.5 * (1.0 + lax.erf(u * np.float32(0.5**0.5)))
            v.act[l, now, :] = (u * inner).astype(BF16)
            v.u[l, now, :] = inner + u * jnp.exp(-0.5 * u * u) * np.float32((2.0 * np.pi) ** -0.5)
            return carry

        lax.fori_loop(0, size // ST, activate, 0)
        v.part[at, :] = nn(v.act[l, at, :], v.wdown[l])

    def attention(l, s, part):
        for qt in range(rows // QT):
            q_at = slice(qt * QT, (qt + 1) * QT)
            head_rows = [slice(h * HEAD_DIM, (h + 1) * HEAD_DIM) for h in range(2)]

            def block(b, carry, masked):
                keys = v.kv[l, b, :, :width]
                scores = [nt(keys, v.qm[l, h, q_at, :]) for h in range(2)]
                result = []
                for h in range(2):
                    top, total, out = carry[h]
                    sc = scores[h]
                    if masked:
                        key = lax.broadcasted_iota(jnp.int32, sc.shape, 0)
                        query = lax.broadcasted_iota(jnp.int32, sc.shape, 1) + qt * QT
                        sc = jnp.where(key <= query, sc, -1e30)
                    new = jnp.maximum(top, jnp.max(sc, axis=0, keepdims=True))
                    p = jnp.exp(sc - new)
                    fade = jnp.exp(top - new)
                    total = total * fade + jnp.sum(p, axis=0, keepdims=True)
                    out = out * fade + nn(v.vt[l, b, head_rows[h], :], p.astype(BF16))
                    result.append((new, total, out))
                return tuple(result)

            start = (
                jnp.full((1, QT), -1e30, F32),
                jnp.zeros((1, QT), F32),
                jnp.zeros((HEAD_DIM, QT), F32),
            )
            if part == 0:
                carry = block(rank, (start, start), True)
                carry = lax.fori_loop(
                    rank - core, rank, functools.partial(block, masked=False), carry
                )
                for h in range(2):
                    v.top[h : h + 1, q_at] = carry[h][0]
                    v.lse[l, h : h + 1, q_at] = carry[h][1]
                    v.ot[l, head_rows[h], q_at] = carry[h][2]
                continue
            carry = tuple(
                (
                    v.top[h : h + 1, q_at],
                    v.lse[l, h : h + 1, q_at],
                    v.ot[l, head_rows[h], q_at],
                )
                for h in range(2)
            )
            carry = lax.fori_loop(0, 2 * zlo, functools.partial(block, masked=False), carry)
            for h in range(2):
                top, total, out = carry[h]
                v.ot[l, head_rows[h], q_at] = out / total
                v.lse[l, h : h + 1, q_at] = top + jnp.log(total)
            v.ob[l, q_at, :] = v.ot[l, :, q_at].T.astype(BF16)
            both = nn(v.ob[l, q_at, :], v.wout[l]) + v.part[q_at, :]
            both = both.astype(BF16)
            first = qt * QT // chunk
            for half in range(2):
                v.psend[s, half, first : first + QT // chunk] = both[
                    :, half * hd : (half + 1) * hd
                ].reshape(QT // chunk, chunk, hd)
            for pair in range(first // 2, (first + QT // chunk) // 2):
                rs_pair(s, lax.rem(pair - yy - 1 + 2 * ny, ny) + 1)

    def branch_reduce(s):
        rs_finish(s)
        for i in range(chunk // 16):
            at = slice(i * 16, (i + 1) * 16)
            ag_put(s, at, rs_sum(s, at))
        ag_start(s)

    grads = {0: (v.ge, v.r1e, v.r2e, v.s3e, v.r3e, v.k3e), 1: (v.gl, v.r1l, v.r2l, v.s3l, v.r3l, v.k3l)}

    def core_copy(l, p):
        g, r1 = grads[p][:2]
        return remote(
            g.at[l, 1 - core], r1.at[l], v.g1s.at[l, p], v.g1r.at[l, p], dp=other_core
        )

    def x_copy(l, p, k):
        r1, r2 = grads[p][1:3]
        to = lax.rem(xc + k, nx)
        return remote(
            r1.at[l, pl.ds(2 * to, 2)],
            r2.at[l, k - 1],
            v.g2s.at[l, p, k - 1],
            v.g2r.at[l, p, k - 1],
            dp=to * group + zlo * 2 + core,
        )

    def z_copy(l, p):
        return remote(
            grads[p][3].at[l], grads[p][4].at[l], v.g3s.at[l, p], v.g3r.at[l, p], dp=other_z
        )

    def grad_core(l, p):
        core_copy(l, p).start()

    def grad_x(l, p):
        core_copy(l, p).wait()
        g, r1 = grads[p][:2]

        def one(i, carry):
            for j in range(grow // 16):
                at = slice(j * 16, (j + 1) * 16)
                r1[l, i, at, :] = (
                    r1[l, i, at, :].astype(F32) + g[l, core, i, at, :].astype(F32)
                ).astype(BF16)
            return carry

        lax.fori_loop(0, nd // 2, one, 0)
        for k in range(1, nx):
            x_copy(l, p, k).start()

    def grad_z(l, p):
        _, r1, r2, s3, r3, k3 = grads[p]
        for k in range(1, nx):
            x_copy(l, p, k).wait()

        def total(z, at):
            value = r1[l, 2 * xc + z, at, :].astype(F32)
            for k in range(1, nx):
                value = value + r2[l, k - 1, z, at, :].astype(F32)
            return value

        for j in range(grow // 16):
            at = slice(j * 16, (j + 1) * 16)
            s3[l, at, :] = total(1 - zlo, at).astype(BF16)
        z_copy(l, p).start()
        for j in range(grow // 16):
            at = slice(j * 16, (j + 1) * 16)
            k3[l, at, :] = total(zlo, at)

    def grad_end(l, p):
        z_copy(l, p).wait()
        _, _, _, _, r3, k3 = grads[p]
        for j in range(grow // 16):
            at = slice(j * 16, (j + 1) * 16)
            total = k3[l, at, :] + r3[l, at, :].astype(F32)
            if p == 0:
                v.oo[l, at, :] = total[:, :width]
                v.od[l, at, :] = total[:, width : width + ff]
                v.oi[l, at, :] = total[:, width + ff :]
            else:
                for c in range(3):
                    v.oq[l, c, at, :] = total[:, c * width : (c + 1) * width]

    def start_gradient(l, at, gradient):
        v.dz[at, :] = gradient.astype(BF16)

    def attention_back(l, first, second):
        do = v.do[...]
        product = do.astype(F32).T * v.ot[l]
        v.delta[0:1, :] = jnp.sum(product[:HEAD_DIM], axis=0, keepdims=True)
        v.delta[1:2, :] = jnp.sum(product[HEAD_DIM:], axis=0, keepdims=True)
        v.dqt[...] = jnp.zeros_like(v.dqt)

        def piece(b, i, masked):
            at = slice(i * KT, (i + 1) * KT)
            keys = v.kv[l, b, at, :width]
            values = v.kv[l, b, at, width:]
            dk = jnp.zeros((KT, width), F32)
            dv = jnp.zeros((KT, width), F32)
            for h in range(2):
                head_rows = slice(h * HEAD_DIM, (h + 1) * HEAD_DIM)
                sc = nt(keys, v.qm[l, h])
                if masked:
                    key = lax.broadcasted_iota(jnp.int32, sc.shape, 0) + i * KT
                    query = lax.broadcasted_iota(jnp.int32, sc.shape, 1)
                    sc = jnp.where(key <= query, sc, -1e30)
                p = jnp.exp(sc - v.lse[l, h : h + 1, :])
                dp = nt(values, v.dom[h])
                ds = (p * (dp - v.delta[h : h + 1, :])).astype(BF16)
                dv = dv + nn(p.astype(BF16), v.dom[h])
                dk = dk + nn(ds, v.qm[l, h])
                v.dqt[head_rows, :] += nn(v.kt[l, b, head_rows, at], ds)
            return dk, dv

        def far(b, slot, received):
            for i in range(rows // KT):
                dk, dv = piece(b, i, False)
                at = slice(i * KT, (i + 1) * KT)
                if received:
                    dkv_copy(l, 0, i).wait_recv()
                    dk = dk + v.dkvi[l, 0, at, :width].astype(F32)
                    dv = dv + v.dkvi[l, 0, at, width:].astype(F32)
                v.dkvo[l, slot, at, :width] = dk.astype(BF16)
                v.dkvo[l, slot, at, width:] = dv.astype(BF16)
                dkv_copy(l, slot, i).start()

        @pl.when(zlo == 1)
        def _():
            far(1 - core, 0, False)
            first()
            far(core, 1, True)

        @pl.when(core == 1)
        def _():
            far(rank - 1, 2, False)

        @pl.when(rank == group - 1)
        def _():
            second()

        for i in range(rows // KT):
            dk, dv = piece(rank, i, True)
            at = slice(i * KT, (i + 1) * KT)
            v.own[at, :width] = dk
            v.own[at, width:] = dv

    def do_rows(l, at):
        do = nt(v.dz[at, :], v.wout[l]).astype(BF16)
        v.do[at, :] = do
        v.dom[0, at, :] = head_only(do, 0)
        v.dom[1, at, :] = head_only(do, 1)

    def dact_rows(l, at):
        v.dact[at, :] = nt(v.dz[at, :], v.wdown[l])

    def back_rows(l, at, size):
        def slope(i, acc):
            now = pl.ds(pl.multiple_of(at.start + i * ST, ST), ST)
            du = (v.dact[now, :] * v.u[l, now, :]).astype(BF16)
            v.du[now, :] = du
            return acc + jnp.sum(du.astype(F32).reshape(ST // 8, 8, ff), axis=0)

        v.binacc[l] += lax.fori_loop(0, size // ST, slope, jnp.zeros((8, ff), F32))
        v.dh1[at, :] = nt(v.du[at, :], v.win[l])

    def early_grads(l):
        def one(i, carry):
            at = rows_at(i, 2 * grow)
            dzt = v.dz[:, at].astype(F32).T.astype(BF16)
            ht = v.h1[l, :, at].astype(F32).T.astype(BF16)
            wo = nn(dzt, v.ob[l]).astype(BF16)
            wd = nn(dzt, v.act[l]).astype(BF16)
            wi = nn(ht, v.du[...]).astype(BF16)
            for c in range(2):
                part = slice(c * grow, (c + 1) * grow)
                v.ge[l, c, i, :, :width] = wo[part]
                v.ge[l, c, i, :, width : width + ff] = wd[part]
                v.ge[l, c, i, :, width + ff :] = wi[part]
            return carry

        lax.fori_loop(0, depth // (2 * grow), one, 0)

    def late_grads(l):
        def one(i, carry):
            at = rows_at(i, 2 * grow)
            ht = v.h0[l, :, at].astype(F32).T.astype(BF16)
            wq = nn(ht, v.dqkv[...]).astype(BF16)
            for c in range(2):
                v.gl[l, c, i] = wq[c * grow : (c + 1) * grow]
            return carry

        lax.fori_loop(0, depth // (2 * grow), one, 0)

    def qkv_back(l):
        @pl.when(zlo == 0)
        def _():
            grad_x(l, 0)

        for step, here in ((2, core == 0), (1, zlo == 0)):

            @pl.when(here)
            def _():
                for i in range(rows // KT):
                    dkv_copy(l, step, i).wait_recv()
                v.own[...] += v.dkvi[l, step].astype(F32)

        cosine, sine = v.cosine[...], -v.sine[...]
        v.dqkv[:, :width] = rotate(v.dqt[...].T * 0.125, cosine, sine).astype(BF16)
        v.dqkv[:, width : 2 * width] = rotate(v.own[:, :width], cosine, sine).astype(BF16)
        v.dqkv[:, 2 * width : 3 * width] = v.own[:, width:].astype(BF16)
        v.other[4 * l + 3 : 4 * l + 4, : 3 * width] = jnp.sum(
            v.dqkv[...].astype(F32), axis=0, keepdims=True
        )

        def one(i, carry):
            at = rows_at(i, MT)
            v.dh0[at, :] = nt(v.dqkv[at, :], v.wqkv[l])
            return carry

        lax.fori_loop(0, rows // MT, one, 0)

        def send(m, carry):
            pair = at_y(m)
            for i in range(2 * chunk // ST):
                at = pl.ds(pl.multiple_of(pair * 2 * chunk + i * ST, ST), ST)
                both = v.dh0[at, :] * v.gain[l, 0:1, :] + v.dh1[at, :] * v.gain[l, 1:2, :]
                both = both.astype(BF16)
                part = slice(i * ST % chunk, i * ST % chunk + ST)
                for half in range(2):
                    v.psend[0, half, 2 * pair + i * ST // chunk, part, :] = both[
                        :, half * hd : (half + 1) * hd
                    ]
            rs_pair(0, m)
            return carry

        lax.fori_loop(1, ny + 1, send, 0)

    def norm_grads(l):
        v.lnacc[...] = jnp.zeros_like(v.lnacc)

        def fold(value):
            return jnp.sum(value.reshape(2, 8, depth), axis=0)

        def one(i, carry):
            at = rows_at(i, 16)
            xhat = (stream_rows(l, at) - v.mu[l, at, :]) * v.rs[l, at, :]
            first, second = v.dh0[at, :], v.dh1[at, :]
            v.lnacc[0] += fold(first * xhat)
            v.lnacc[1] += fold(second * xhat)
            v.lnacc[2] += fold(first)
            v.lnacc[3] += fold(second)
            v.lnacc[4] += fold(v.dz[at, :].astype(F32))
            return carry

        lax.fori_loop(0, rows // 16, one, 0)
        for i in range(4):
            v.ln[4 * l + i : 4 * l + i + 1, :] = jnp.sum(v.lnacc[i], axis=0, keepdims=True)
        column = jnp.sum(v.lnacc[4], axis=0, keepdims=True)
        v.other[4 * l : 4 * l + 1, :] = column[:, :ff]
        v.other[4 * l + 1 : 4 * l + 2, :] = column[:, ff:]
        v.other[4 * l + 2 : 4 * l + 3, :] = jnp.sum(v.binacc[l], axis=0, keepdims=True)

    def stream_reduce(l):
        rs_finish(0)
        for i in range(chunk // 16):
            at = pl.ds(pl.multiple_of(me_t * chunk + i * 16, 16), 16)
            gd = rs_sum(0, slice(i * 16, (i + 1) * 16))
            r = v.rs[l, at, :]
            xhat = (stream_rows(l, at) - v.mu[l, at, :]) * r
            mean = jnp.mean(gd, axis=-1, keepdims=True)
            along = jnp.mean(gd * xhat, axis=-1, keepdims=True)
            dx = r * (gd - mean - xhat * along)
            ag_put(0, slice(i * 16, (i + 1) * 16), dx)
        ag_start(0)

    def small_core(i):
        mine, theirs = [(v.ln, v.ln1), (v.other, v.other1)][i]
        return remote(mine, theirs, v.s1s.at[i], v.s1r.at[i], dp=other_core)

    def small_dp(k, i):
        to = lax.rem(me_d + 2 * k, nd)
        mine, theirs = [(v.lnsum, v.ln3), (v.other, v.other2)][i]
        return remote(mine, theirs.at[k - 1], v.s3s.at[i, k - 1], v.s3r.at[i, k - 1], dp=to)

    def small_scatter(k):
        to = lax.rem(me_t + k, nt_dev)
        columns = pl.ds(pl.multiple_of(to * LANES, LANES), LANES)
        return remote(
            v.ln.at[:, columns], v.ln2.at[k - 1], v.s2s.at[k - 1], v.s2r.at[k - 1], tensor=to
        )

    def small_gather(k):
        to = lax.rem(me_t + k, nt_dev)
        block = v.lnall.at[me_t]
        return remote(block, block, v.s4s.at[k - 1], v.s4r.at[me_t], tensor=to)

    def small_start():
        for i in range(2):
            small_core(i).start()

    def small_second():
        for i in range(2):
            small_core(i).wait()
        v.ln[...] += v.ln1[...]
        v.other[...] += v.other1[...]
        for k in range(1, nt_dev):
            small_scatter(k).start()
        for k in range(1, nd // 2):
            small_dp(k, 1).start()

    def small_third():
        mine = pl.ds(pl.multiple_of(me_t * LANES, LANES), LANES)
        total = v.ln[:, mine]
        for k in range(1, nt_dev):
            small_scatter(k).wait()
            total = total + v.ln2[k - 1]
        v.lnsum[...] = total
        for k in range(1, nd // 2):
            small_dp(k, 0).start()

    def small_fourth():
        total = v.lnsum[...]
        for k in range(1, nd // 2):
            small_dp(k, 0).wait()
            total = total + v.ln3[k - 1]
        v.lnall[me_t] = total
        for k in range(1, nt_dev):
            small_gather(k).start()
        total = v.other[...]
        for k in range(1, nd // 2):
            small_dp(k, 1).wait()
            total = total + v.other2[k - 1]
        for l in range(LAYERS):
            for half in range(2):
                at = slice(half * ff, (half + 1) * ff)
                row = total[4 * l + half : 4 * l + half + 1, :]
                v.obout[l : l + 1, at] = row
                v.obdown[l : l + 1, at] = row
            v.obin[l : l + 1, :] = total[4 * l + 2 : 4 * l + 3, :]
            for c in range(3):
                at = slice(c * width, (c + 1) * width)
                v.obqkv[c, l : l + 1, :] = total[4 * l + 3 : 4 * l + 4, at]

    def small_end():
        for k in range(1, nt_dev):
            src = lax.rem(me_t + k, nt_dev)
            block = v.lnall.at[src]
            remote(block, block, v.s4s.at[k - 1], v.s4r.at[src], tensor=src).wait()
        for j in range(nt_dev):
            at = slice(j * LANES, (j + 1) * LANES)
            block = v.lnall[j]
            for l in range(LAYERS):
                v.ogain[l, :, at] = block[4 * l : 4 * l + 2, :]
                v.obias[l, :, at] = block[4 * l + 2 : 4 * l + 4, :]

    def nothing(at):
        pass

    def first_norm(i, carry):
        at = rows_at(i, ST)
        norm_rows(0, at, v.xt[at, :].astype(F32))
        return carry

    with jax.named_scope("norm0"):
        for i in range(TP):
            load_tok[i].wait()
            lax.fori_loop(i * rows // TP // ST, (i + 1) * rows // TP // ST, first_norm, 0, unroll=2)
    with jax.named_scope("qkv0"):
        for c in load_qkv[0]:
            c.wait()
        load_cos.wait()
        load_sin.wait()

        def first_qkv(i, carry):
            qkv_rows(0, rows_at(i, MT), MT)
            return carry

        lax.fori_loop(0, rows // MT, first_qkv, 0)
    with jax.named_scope("barrier"):
        pl.semaphore_wait(barrier, nt_dev - 1 + nd - 1)
    kv_send(0)
    v.ln[...] = jnp.zeros_like(v.ln)
    v.other[...] = jnp.zeros_like(v.other)
    v.binacc[...] = jnp.zeros_like(v.binacc)
    with jax.named_scope("ffn0"):
        for c in load_rest[0]:
            c.wait()

        def first_ffn(i, carry):
            feed_forward(0, rows_at(i, MT), MT)
            return carry

        lax.fori_loop(0, rows // MT, first_ffn, 0)
    with jax.named_scope("near0"):
        kv_near(0)
        attention(0, 0, 0)
    def first_gradients(z):
        @pl.when(zlo == z)
        def _():
            load_cot.wait()
            for c in load_rest[1]:
                c.wait()

            def copy_rows(i, carry):
                at = rows_at(i, ST)
                v.dz[at, :] = v.ct[at, :]
                v.g[at, :] = v.ct[at, :].astype(F32)
                return carry

            def rows_back(i, carry):
                at = rows_at(i, MT)
                do_rows(1, at)
                dact_rows(1, at)
                return carry

            lax.fori_loop(0, rows // ST, copy_rows, 0)
            lax.fori_loop(0, rows // MT, rows_back, 0)

    with jax.named_scope("dz1"):
        first_gradients(1)
    with jax.named_scope("kv0"):
        kv_far(0)
    with jax.named_scope("attn0"):
        attention(0, 0, 1)
    with jax.named_scope("dz1b"):
        first_gradients(0)
    with jax.named_scope("forward0"):
        rs_forward(0)
    with jax.named_scope("reduce0"):
        branch_reduce(0)

    def next_stream(at, z):
        x = v.xt[at, :].astype(F32) + (z + (v.bout[0:1, :] + v.bdown[0:1, :]))
        v.x[at, :] = x
        norm_rows(1, at, x)

    def next_qkv(at):
        qkv_rows(1, at, 2 * chunk)

    def next_ffn(at):
        feed_forward(1, at, 2 * chunk)
        back_rows(1, at, 2 * chunk)

    def next_both(at):
        next_qkv(at)
        next_ffn(at)

    with jax.named_scope("gather0"):
        for c in load_qkv[1]:
            c.wait()
        ag_forward(0)
        ag_pairs(0, 0, ny - 1, next_stream, next_both)
        ag_pairs(0, ny - 1, ny, next_stream, next_qkv)
        kv_send(1)
        ag_sent(0)
    with jax.named_scope("ffn1"):
        next_ffn(rows_at(at_y(place(ny - 1)), 2 * chunk))
    with jax.named_scope("near1"):
        kv_near(1)
        attention(1, 1, 0)
    with jax.named_scope("kv1"):
        kv_far(1)
    with jax.named_scope("attn1"):
        attention(1, 1, 1)

    with jax.named_scope("attn_grad1"):
        attention_back(1, lambda: None, lambda: rs_forward(1))

        @pl.when(rank != group - 1)
        def _():
            rs_forward(1)


    def forward_at(z):
        @pl.when(zlo == z)
        def _():
            rs_forward(0)

    def late_x(l):
        @pl.when(zlo == 1)
        def _():
            grad_x(l, 0)

    def early(l, z):
        @pl.when(zlo == z)
        def _():
            early_grads(l)
            grad_core(l, 0)

    with jax.named_scope("early1"):
        early(1, 0)
    with jax.named_scope("qkv_grad1"):
        qkv_back(1)
    with jax.named_scope("early1b"):
        early(1, 1)
    with jax.named_scope("norm_grad1"):
        norm_grads(1)
    with jax.named_scope("forward"):
        forward_at(1)
    with jax.named_scope("gx10"):
        late_x(1)
    with jax.named_scope("late1"):
        late_grads(1)
        grad_core(1, 1)
    with jax.named_scope("forward"):
        forward_at(0)
    with jax.named_scope("gx11"):
        grad_x(1, 1)
    with jax.named_scope("stream_reduce1"):
        stream_reduce(1)

    def next_gradient(at, dx):
        gradient = v.g[at, :] + dx
        v.g[at, :] = gradient
        v.dz[at, :] = gradient.astype(BF16)

    def next_back(at):
        do_rows(0, at)
        dact_rows(0, at)
        back_rows(0, at, 2 * chunk)

    with jax.named_scope("gather2"):
        ag_forward(0)
        branch_reduce(1)
        ag_pairs(0, 0, ny, next_gradient, next_back)
        ag_sent(0)
    with jax.named_scope("attn_grad0"):
        attention_back(0, lambda: ag_forward(1), lambda: None)
    with jax.named_scope("forward1b"):

        @pl.when(zlo == 0)
        def _():
            ag_forward(1)

    with jax.named_scope("early0"):
        early(0, 0)
    with jax.named_scope("qkv_grad0"):
        qkv_back(0)
    with jax.named_scope("early0b"):
        early(0, 1)
    with jax.named_scope("norm_grad0"):
        norm_grads(0)
        small_start()
    with jax.named_scope("gx00"):
        late_x(0)
    with jax.named_scope("small_second"):
        small_second()
    with jax.named_scope("forward"):
        forward_at(1)
    with jax.named_scope("late0"):
        late_grads(0)
        grad_core(0, 1)
    with jax.named_scope("forward"):
        forward_at(0)
    with jax.named_scope("small_third"):
        small_third()
    with jax.named_scope("gx01"):
        grad_x(0, 1)

    def last_stream(at, z):
        v.x[at, :] = v.x[at, :] + (z + (v.bout[1:2, :] + v.bdown[1:2, :]))

    store_x = pltpu.make_async_copy(v.x, v.ox, v.lsem.at[0])
    store_g = pltpu.make_async_copy(v.g, v.og, v.lsem.at[1])
    with jax.named_scope("stream_reduce0"):
        stream_reduce(0)
    with jax.named_scope("forward0c"):
        ag_forward(0)
    with jax.named_scope("gz1"):
        grad_z(1, 0)
        grad_z(1, 1)
    with jax.named_scope("gather1"):
        ag_pairs(1, 0, ny, last_stream, nothing)
        ag_sent(1)
        store_x.start()

    def last_gradient(at, dx):
        v.g[at, :] = v.g[at, :] + dx

    with jax.named_scope("gather3"):
        ag_pairs(0, 0, ny // 2, last_gradient, nothing)
    with jax.named_scope("small_fourth"):
        small_fourth()
    with jax.named_scope("gz00"):
        grad_z(0, 0)
    with jax.named_scope("gather3a"):
        ag_pairs(0, ny // 2, ny - 1, last_gradient, nothing)
    with jax.named_scope("gz01"):
        grad_z(0, 1)
    with jax.named_scope("gather3b"):
        ag_pairs(0, ny - 1, ny, last_gradient, nothing)
        store_g.start()
        ag_sent(0)
    with jax.named_scope("gend1"):
        grad_end(1, 0)
        grad_end(1, 1)
    with jax.named_scope("small_end"):
        small_end()
    with jax.named_scope("gend0"):
        grad_end(0, 0)
        grad_end(0, 1)
        store_x.wait()
        store_g.wait()
    for l in range(LAYERS):
        for step, here in ((0, core == 0), (1, zlo == 0), (2, zlo == 1)):

            @pl.when(here)
            def _():
                kv_copy(l, step).wait_send()

        for step, here in ((0, zlo == 1), (1, zlo == 1), (2, core == 1)):

            @pl.when(here)
            def _():
                for i in range(rows // KT):
                    dkv_copy(l, step, i).wait_send()


def store_kernel(count, *refs):
    given, kept, held = refs[:count], refs[count : 2 * count], refs[2 * count : 3 * count]
    sems = refs[3 * count]
    parts = []
    for i in range(count):
        pieces = PARTS if i < 2 else 1
        rows = held[i].shape[0] // pieces
        parts += [(i, slice(j * rows, (j + 1) * rows)) for j in range(pieces)]
    loads = [
        pltpu.make_async_copy(given[i].at[at], held[i].at[at], sems.at[0, n])
        for n, (i, at) in enumerate(parts)
    ]
    stores = [
        pltpu.make_async_copy(held[i].at[at], kept[i].at[at], sems.at[1, n])
        for n, (i, at) in enumerate(parts)
    ]
    for copy in loads:
        copy.start()
    for load, store in zip(loads, stores):
        load.wait()
        store.start()
    for copy in stores:
        copy.wait()


def on_device(nt_dev, nd, *args):
    tokens, cotangent, ln_gain, ln_bias, w_qkv, b_qkv, w_out, b_out, w_in, b_in, w_down, b_down = args
    rows, depth = tokens.shape
    width = w_out.shape[1]
    ff = w_in.shape[2]
    group = SEQ // rows
    chunk = rows // nt_dev
    grow = depth // nd
    half = nd // 2
    nx = nd // group
    early = width + 2 * ff
    late = 3 * width
    cosine, sine = rope_constants()
    vm = pltpu.VMEM
    dma = pltpu.SemaphoreType.DMA
    two = LAYERS
    scratch = [
        vm((two, depth, 3 * width), BF16),
        vm((two, width, depth), BF16),
        vm((two, depth, ff), BF16),
        vm((two, ff, depth), BF16),
        vm((rows, LANES), F32),
        vm((rows, LANES), F32),
        vm((rows, depth), F32),
        vm((rows, depth), F32),
        vm((rows, depth), BF16),
        vm((rows, depth), BF16),
        vm((two, rows, depth), BF16),
        vm((two, rows, depth), BF16),
        vm((two, 2, rows, width), BF16),
        vm((two, group, rows, 2 * width), BF16),
        vm((two, group, width, rows), BF16),
        vm((two, group, width, rows), BF16),
        vm((two, rows, width), BF16),
        vm((two, width, rows), F32),
        vm((8, rows), F32),
        vm((two, 8, rows), F32),
        vm((two, rows, ff), F32),
        vm((two, rows, ff), BF16),
        vm((two, rows, 1), F32),
        vm((two, rows, 1), F32),
        vm((rows, depth), F32),
        vm((2, 2, nt_dev, chunk, depth // 2), BF16),
        vm((2, nt_dev // 2 - 1, 2, chunk, depth // 2), BF16),
        vm((2, nt_dev // 2, chunk, depth // 2), BF16),
        vm((2, chunk, depth // 2), BF16),
        vm((2, nt_dev // 2 - 1, chunk, depth // 2), BF16),
        vm((2, chunk, depth // 2), BF16),
        vm((2, nt_dev // 2 - 1, chunk, depth // 2), BF16),
        vm((2, 2, nt_dev, chunk, depth // 2), BF16),
        vm((rows, depth), BF16),
        vm((rows, width), BF16),
        vm((2, rows, width), BF16),
        vm((8, rows), F32),
        vm((width, rows), F32),
        vm((two, 3, rows, 2 * width), BF16),
        vm((two, 3, rows, 2 * width), BF16),
        vm((rows, 2 * width), F32),
        vm((rows, 3 * width), BF16),
        vm((rows, ff), BF16),
        vm((rows, ff), F32),
        vm((two, 8, ff), F32),
        vm((rows, depth), F32),
        vm((rows, depth), F32),
        vm((two, 2, half, grow, early), BF16),
        vm((two, 2, half, grow, late), BF16),
        vm((two, half, grow, early), BF16),
        vm((two, half, grow, late), BF16),
        vm((two, nx - 1, 2, grow, early), BF16),
        vm((two, nx - 1, 2, grow, late), BF16),
        vm((two, grow, early), BF16),
        vm((two, grow, late), BF16),
        vm((two, grow, early), BF16),
        vm((two, grow, late), BF16),
        vm((two, grow, early), F32),
        vm((two, grow, late), F32),
        vm((8, depth), F32),
        vm((8, ff), F32),
        vm((8, depth), F32),
        vm((8, ff), F32),
        vm((nt_dev - 1, 8, LANES), F32),
        vm((half - 1, 8, ff), F32),
        vm((8, LANES), F32),
        vm((half - 1, 8, LANES), F32),
        vm((nt_dev, 8, LANES), F32),
        vm((5, 8, depth), F32),
        dma((16 + TP,)),
        dma((two, 3)),
        dma((two, 3)),
        dma((two, 3, rows // KT)),
        dma((two, 3, rows // KT)),
        dma((2, 7 * (nt_dev // 2) - 3)),
        dma((2, 7 * (nt_dev // 2) - 3)),
        dma((two, 2)),
        dma((two, 2)),
        dma((two, 2, nx - 1)),
        dma((two, 2, nx - 1)),
        dma((two, 2)),
        dma((two, 2)),
        dma((2,)),
        dma((2,)),
        dma((nt_dev - 1,)),
        dma((nt_dev - 1,)),
        dma((2, half - 1)),
        dma((2, half - 1)),
        dma((nt_dev - 1,)),
        dma((nt_dev,)),
    ]
    here = pl.BlockSpec(memory_space=pltpu.VMEM)
    away = pl.BlockSpec(memory_space=pl.ANY)
    shapes = [
        (rows, depth),
        (rows, depth),
        (two, 2, depth),
        (two, 2, depth),
        (3, two, width),
        (two, depth),
        (two, ff),
        (two, depth),
        (two, 3, grow, width),
        (two, grow, width),
        (two, grow, ff),
        (two, grow, ff),
    ]
    out = pl.pallas_call(
        functools.partial(step_kernel, nt_dev, nd),
        out_shape=[jax.ShapeDtypeStruct(s, F32) for s in shapes],
        in_specs=[away, away, here, here, away, here, away, here, away, here, away, here, away, away],
        out_specs=[away] * 2 + [here] * (len(shapes) - 2),
        scratch_shapes=scratch,
        compiler_params=pltpu.CompilerParams(
            collective_id=0, has_side_effects=True, vmem_limit_bytes=64 * 1024 * 1024 - 65536
        ),
    )(
        tokens,
        cotangent,
        ln_gain,
        ln_bias,
        w_qkv.transpose(0, 2, 1, 3),
        b_qkv.transpose(1, 0, 2),
        w_out,
        b_out,
        w_in,
        b_in,
        w_down,
        b_down,
        jnp.asarray(cosine),
        jnp.asarray(sine),
    )
    out = pl.pallas_call(
        functools.partial(store_kernel, len(shapes)),
        out_shape=[jax.ShapeDtypeStruct(s, F32) for s in shapes],
        in_specs=[away] * len(shapes),
        out_specs=[away] * len(shapes),
        scratch_shapes=[vm(s, F32) for s in shapes] + [dma((2, 2 * PARTS + len(shapes)))],
    )(*out)
    x, g, gain, bias, bqkv, bout, b_in_g, bdown, wq, wo, wi, wd = out
    return (
        x,
        g,
        gain,
        bias,
        wq.transpose(0, 2, 1, 3),
        bqkv.transpose(1, 0, 2),
        wo.transpose(0, 2, 1),
        bout,
        wi,
        b_in_g,
        wd.transpose(0, 2, 1),
        bdown,
    )


def solution(mesh):
    return jax.shard_map(
        functools.partial(on_device, mesh.shape["tensor"], mesh.shape["dp"]),
        mesh=mesh,
        in_specs=(
            P("dp", None),
            P("dp", None),
            P(),
            P(),
            P(None, None, None, "tensor"),
            P(None, None, "tensor"),
            P(None, "tensor", None),
            P(),
            P(None, None, "tensor"),
            P(None, "tensor"),
            P(None, "tensor", None),
            P(),
        ),
        out_specs=(
            P("dp", None),
            P("dp", None),
            P(),
            P(),
            P(None, "dp", None, "tensor"),
            P(None, None, "tensor"),
            P(None, "tensor", "dp"),
            P(),
            P(None, "dp", "tensor"),
            P(None, "tensor"),
            P(None, "tensor", "dp"),
            P(),
        ),
        check_vma=False,
    )
```

```python
import functools

import jax
import jax.numpy as jnp
import numpy as np
from jax import lax
from jax.experimental import pallas as pl
from jax.experimental.pallas import tpu as pltpu
from jax.sharding import PartitionSpec as P

HEAD_DIM = 64
ROT = 16
SEQ = 2048
LAYERS = 2
EPS = 1e-05
F32 = jnp.float32
BF16 = jnp.bfloat16
MESH = pl.DeviceIdType.MESH
LANES = 128
QT = 256
KT = 256
MT = 256
ST = 32
TP = 4
PARTS = 2


def nn(a, b):
    return jnp.dot(a, b, preferred_element_type=F32)


def nt(a, b):
    return lax.dot_general(a, b, (((1,), (1,)), ((), ())), preferred_element_type=F32)


def rope_constants():
    half = ROT // 2
    exponent = np.arange(0, ROT, 2).astype(np.float32) / np.float32(ROT)
    inverse = (np.float32(1.0) / np.float32(10000.0) ** exponent).astype(np.float32)
    angles = np.arange(SEQ).astype(np.float32)[:, None] * inverse[None, :]
    cosine = np.ones((SEQ, LANES), np.float32)
    sine = np.zeros((SEQ, LANES), np.float32)
    for start in range(0, LANES, HEAD_DIM):
        cosine[:, start : start + half] = np.cos(angles)
        cosine[:, start + half : start + ROT] = np.cos(angles)
        sine[:, start : start + half] = -np.sin(angles)
        sine[:, start + half : start + ROT] = np.sin(angles)
    return cosine, sine


def rotate(values, cosine, sine):
    half = ROT // 2
    lane = lax.broadcasted_iota(jnp.int32, values.shape, 1)
    partner = jnp.where(
        lane % HEAD_DIM < half,
        pltpu.roll(values, LANES - half, 1),
        pltpu.roll(values, half, 1),
    )
    return values * cosine + partner * sine


def head_only(values, head):
    lane = lax.broadcasted_iota(jnp.int32, values.shape, 1)
    return jnp.where(lane // HEAD_DIM == head, values, jnp.zeros_like(values))


def rows_at(step, size):
    return pl.ds(pl.multiple_of(step * size, size), size)


def remote(src, dst, send_sem, recv_sem, **device):
    return pltpu.make_async_remote_copy(
        src_ref=src,
        dst_ref=dst,
        send_sem=send_sem,
        recv_sem=recv_sem,
        device_id=device,
        device_id_type=MESH,
    )


class Refs:
    pass


def step_kernel(nt_dev, nd, *refs):
    names = (
        "tok", "cot", "gain", "bias", "wqkv_h", "bqkv", "wout_h", "bout", "win_h", "bin",
        "wdown_h", "bdown", "cos_h", "sin_h", "ox", "og", "ogain", "obias", "obqkv", "obout",
        "obin", "obdown", "oq", "oo", "oi", "od", "wqkv", "wout", "win", "wdown", "cosine",
        "sine", "x", "g", "xt", "ct", "h0", "h1", "qm", "kv", "kt", "vt", "ob", "ot", "top",
        "lse", "u", "act", "mu", "rs", "part", "psend", "ra", "rb", "sa", "sb", "r2a", "r2b",
        "agbuf", "dz", "do", "dom", "delta", "dqt", "dkvo", "dkvi", "own", "dqkv", "du", "dact",
        "binacc", "dh0", "dh1", "ge", "gl", "r1e", "r1l", "r2e", "r2l", "s3e", "s3l", "r3e",
        "r3l", "k3e", "k3l", "ln", "other", "ln1", "other1", "ln2", "other2", "lnsum", "ln3",
        "lnall", "lnacc", "lsem", "kvs", "kvr", "dks", "dkr", "ars", "arr", "g1s", "g1r", "g2s",
        "g2r", "g3s", "g3r", "s1s", "s1r", "s2s", "s2r", "s3s", "s3r", "s4s", "s4r",
    )
    assert len(names) == len(refs)
    v = Refs()
    v.__dict__.update(zip(names, refs))
    rows, depth = v.x.shape
    group = SEQ // rows
    nx = nd // group
    chunk = rows // nt_dev
    grow = depth // nd
    width = v.wout.shape[1]
    ff = v.win.shape[2]

    me_t = lax.axis_index("tensor")
    me_d = lax.axis_index("dp")
    rank = lax.rem(me_d, group)
    core = lax.rem(me_d, 2)
    zlo = lax.rem(me_d // 2, 2)
    xc = me_d // group
    ny = nt_dev // 2
    hd = depth // 2
    yy = me_t // 2
    zh = lax.rem(me_t, 2)
    other_zh = me_t + 1 - 2 * zh
    other_core = me_d + 1 - 2 * core
    other_z = me_d + 2 - 4 * zlo

    barrier = pltpu.get_barrier_semaphore()
    for k in range(1, nt_dev):
        pl.semaphore_signal(
            barrier, inc=1, device_id={"tensor": lax.rem(me_t + k, nt_dev)}, device_id_type=MESH
        )
    for k in range(1, nd):
        pl.semaphore_signal(
            barrier, inc=1, device_id={"dp": lax.rem(me_d + k, nd)}, device_id_type=MESH
        )

    parts = [slice(i * rows // TP, (i + 1) * rows // TP) for i in range(TP)]

    def load(src, dst, index):
        copy = pltpu.make_async_copy(src, dst, v.lsem.at[index])
        copy.start()
        return copy

    load_tok = [load(v.tok.at[at], v.xt.at[at], 16 + i) for i, at in enumerate(parts)]
    load_cos = load(v.cos_h.at[rows_at(rank, rows)], v.cosine, 1)
    load_sin = load(v.sin_h.at[rows_at(rank, rows)], v.sine, 2)
    load_qkv = []
    load_rest = []
    for l in range(LAYERS):
        load_qkv.append(
            [
                load(
                    v.wqkv_h.at[l, c],
                    v.wqkv.at[l, :, pl.ds(c * width, width)],
                    4 + 6 * l + c,
                )
                for c in range(3)
            ]
        )
        load_rest.append(
            [
                load(v.win_h.at[l], v.win.at[l], 4 + 6 * l + 3),
                load(v.wdown_h.at[l], v.wdown.at[l], 4 + 6 * l + 4),
                load(v.wout_h.at[l], v.wout.at[l], 4 + 6 * l + 5),
            ]
        )
    load_cot = load(v.cot, v.ct, 3)

    def norm_rows(l, at, x):
        mean = jnp.mean(x, axis=-1, keepdims=True)
        center = x - mean
        spread = jnp.mean(center * center, axis=-1, keepdims=True)
        r = lax.rsqrt(spread + EPS)
        xhat = center * r
        v.mu[l, at, :] = mean
        v.rs[l, at, :] = r
        v.h0[l, at, :] = (xhat * v.gain[l, 0:1, :] + v.bias[l, 0:1, :]).astype(BF16)
        v.h1[l, at, :] = (xhat * v.gain[l, 1:2, :] + v.bias[l, 1:2, :]).astype(BF16)

    def stream_rows(l, at):
        if l == 0:
            return v.xt[at, :].astype(F32)
        return v.x[at, :]

    def at_y(k):
        return lax.rem(yy + k, ny)

    def copy_of(s, src, dst, sem, to):
        return remote(src, dst, v.ars.at[s, sem], v.arr.at[s, sem], tensor=to)

    def a1(s, k):
        to = at_y(k)
        return copy_of(
            s, v.psend.at[s, 0, pl.ds(2 * to, 2)], v.ra.at[s, k - 1], k - 1, 2 * to + zh
        )

    def b1(s, m):
        to = at_y(m)
        return copy_of(
            s, v.psend.at[s, 1, 2 * to + 1 - zh], v.rb.at[s, to], ny - 2 + m, other_zh
        )

    def a2(s):
        return copy_of(s, v.sa.at[s], v.r2a.at[s], 2 * ny - 1, other_zh)

    def b2(s, k):
        return copy_of(
            s, v.sb.at[s, k - 1], v.r2b.at[s, k - 1], 2 * ny - 1 + k, 2 * at_y(k) + zh
        )

    def rs_pair(s, m):
        b1(s, m).start()

        @pl.when(m < ny)
        def _():
            a1(s, m).start()

    def rs_forward(s):
        for m in range(1, ny):
            b1(s, m).wait_recv()
            to = at_y(m)
            v.sb[s, m - 1] = (
                v.psend[s, 1, 2 * to + zh].astype(F32) + v.rb[s, to].astype(F32)
            ).astype(BF16)
            b2(s, m).start()
        for k in range(1, ny):
            a1(s, k).wait_recv()
        total = v.psend[s, 0, other_zh].astype(F32)
        for k in range(1, ny):
            total = total + v.ra[s, k - 1, 1 - zh].astype(F32)
        v.sa[s] = total.astype(BF16)
        a2(s).start()
        b1(s, ny).wait_recv()

    def rs_finish(s):
        a2(s).wait()
        for k in range(1, ny):
            b2(s, k).wait()
            a1(s, k).wait_send()
        for m in range(1, ny + 1):
            b1(s, m).wait_send()

    def rs_sum(s, at):
        first = v.psend[s, 0, me_t, at, :].astype(F32) + v.r2a[s, at, :].astype(F32)
        second = v.psend[s, 1, me_t, at, :].astype(F32) + v.rb[s, yy, at, :].astype(F32)
        for k in range(1, ny):
            first = first + v.ra[s, k - 1, zh, at, :].astype(F32)
            second = second + v.r2b[s, k - 1, at, :].astype(F32)
        return jnp.concatenate([first, second], axis=1)

    def ag_copy(s, half, chunk_at, sem, to):
        block = v.agbuf.at[s, :, chunk_at] if s == 1 else v.agbuf.at[s, half, chunk_at]
        return copy_of(s, block, block, sem, to)

    ag0 = 3 * ny - 1
    near_first = sorted(range(1, ny), key=lambda k: min(k, ny - k))

    def gz(s):
        return ag_copy(s, 0, me_t, ag0, other_zh)

    def gy(s, k):
        return ag_copy(s, 0, me_t, ag0 + k, 2 * at_y(k) + zh)

    def fy(s, k):
        return ag_copy(s, 0, other_zh, ag0 + ny - 1 + k, 2 * at_y(k) + zh)

    def by(s, k):
        return ag_copy(s, 1, me_t, ag0 + 2 * ny - 2 + k, 2 * at_y(k) + zh)

    def bz(s, m):
        return ag_copy(s, 1, 2 * at_y(m) + zh, ag0 + 3 * ny - 2 + m, other_zh)

    def place(step):
        return ((step + 1) // 2 * (2 * (step % 2) - 1) + ny) % ny

    def arrived(s, half, chunk_at, sem):
        ag_copy(s, half, chunk_at, sem, other_zh).wait_recv()

    def ag_put(s, at, value):
        v.agbuf[s, 0, me_t, at, :] = value[:, :hd].astype(BF16)
        v.agbuf[s, 1, me_t, at, :] = value[:, hd:].astype(BF16)

    def ag_start(s):
        gz(s).start()
        if s == 0:
            for k in near_first:
                by(s, k).start()
            bz(s, 0).start()
        for k in near_first:
            gy(s, k).start()

    def ag_forward(s):
        arrived(s, 0, other_zh, ag0)
        for k in near_first:
            fy(s, k).start()
        if s == 0:
            for k in near_first:
                arrived(s, 1, 2 * at_y(ny - k) + zh, ag0 + 2 * ny - 2 + k)
                bz(s, ny - k).start()

    def ag_pairs(s, first, last, use, after):
        def one(step, carry):
            m = place(step)
            pair = at_y(m)

            @pl.when(m > 0)
            def _():
                arrived(s, 0, 2 * pair + zh, ag0 + ny - m)
                arrived(s, 0, 2 * pair + 1 - zh, ag0 + 2 * ny - 1 - m)

            if s == 0:
                arrived(s, 1, 2 * pair + 1 - zh, ag0 + 3 * ny - 2 + m)
            for i in range(2):
                src = 2 * pair + i
                for j in range(chunk // ST):
                    at = slice(j * ST, (j + 1) * ST)
                    use(
                        pl.ds(pl.multiple_of(src * chunk + j * ST, ST), ST),
                        jnp.concatenate(
                            [v.agbuf[s, 0, src, at, :], v.agbuf[s, 1, src, at, :]], axis=1
                        ).astype(F32),
                    )
            after(rows_at(pair, 2 * chunk))
            return carry

        lax.fori_loop(first, last, one, 0)

    def ag_sent(s):
        gz(s).wait_send()
        for k in range(1, ny):
            gy(s, k).wait_send()
            fy(s, k).wait_send()
        if s == 0:
            bz(s, 0).wait_send()
            for k in range(1, ny):
                by(s, k).wait_send()
                bz(s, k).wait_send()

    def kv_copy(l, step):
        slot, to = [(rank, other_core), (rank, other_z), (rank - 2, other_core)][step]
        block = v.kv.at[l, slot]
        return remote(block, block, v.kvs.at[l, step], v.kvr.at[l, step], dp=to)

    def kv_in(l, step):
        slot = [rank - 1, rank - 2, rank - 1 - 2 * core][step]
        block = v.kv.at[l, slot]
        return remote(block, block, v.kvs.at[l, step], v.kvr.at[l, step], dp=other_core)

    def dkv_copy(l, step, i):
        at = slice(i * KT, (i + 1) * KT)
        return remote(
            v.dkvo.at[l, step, at],
            v.dkvi.at[l, step, at],
            v.dks.at[l, step, i],
            v.dkr.at[l, step, i],
            dp=other_z if step == 1 else other_core,
        )

    def transpose_block(l, b):
        block = v.kv[l, b].astype(F32)
        v.kt[l, b] = block[:, :width].T.astype(BF16)
        v.vt[l, b] = block[:, width:].T.astype(BF16)

    def qkv_rows(l, at, size):
        mixed = nn(v.h0[l, at, :], v.wqkv[l])
        cosine, sine = v.cosine[at, :], v.sine[at, :]
        q = rotate(mixed[:, :width] + v.bqkv[0, l : l + 1, :], cosine, sine).astype(BF16)
        k = rotate(mixed[:, width : 2 * width] + v.bqkv[1, l : l + 1, :], cosine, sine)
        val = mixed[:, 2 * width :] + v.bqkv[2, l : l + 1, :]
        scaled = (q.astype(F32) * 0.125).astype(BF16)
        v.qm[l, 0, at, :] = head_only(scaled, 0)
        v.qm[l, 1, at, :] = head_only(scaled, 1)
        v.kv[l, rank, at, :width] = k.astype(BF16)
        v.kv[l, rank, at, width:] = val.astype(BF16)

    def kv_send(l):
        @pl.when(zlo == 0)
        def _():
            kv_copy(l, 1).start()

        @pl.when(core == 0)
        def _():
            kv_copy(l, 0).start()

    def kv_near(l):
        transpose_block(l, rank)

        @pl.when(core == 1)
        def _():
            kv_in(l, 0).wait_recv()
            transpose_block(l, rank - 1)

    def kv_far(l):
        @pl.when(zlo == 1)
        def _():
            kv_in(l, 1).wait_recv()
            kv_copy(l, 2).start()
            transpose_block(l, rank - 2)
            kv_in(l, 2).wait_recv()
            transpose_block(l, rank - 1 - 2 * core)

    def feed_forward(l, at, size):
        v.u[l, at, :] = nn(v.h1[l, at, :], v.win[l]) + v.bin[l : l + 1, :]

        def activate(i, carry):
            now = pl.ds(pl.multiple_of(at.start + i * ST, ST), ST)
            u = v.u[l, now, :]
            inner = 0.5 * (1.0 + lax.erf(u * np.float32(0.5**0.5)))
            v.act[l, now, :] = (u * inner).astype(BF16)
            v.u[l, now, :] = inner + u * jnp.exp(-0.5 * u * u) * np.float32((2.0 * np.pi) ** -0.5)
            return carry

        lax.fori_loop(0, size // ST, activate, 0)
        v.part[at, :] = nn(v.act[l, at, :], v.wdown[l])

    def attention(l, s, part):
        for qt in range(rows // QT):
            q_at = slice(qt * QT, (qt + 1) * QT)
            head_rows = [slice(h * HEAD_DIM, (h + 1) * HEAD_DIM) for h in range(2)]

            def block(b, carry, masked):
                keys = v.kv[l, b, :, :width]
                scores = [nt(keys, v.qm[l, h, q_at, :]) for h in range(2)]
                result = []
                for h in range(2):
                    top, total, out = carry[h]
                    sc = scores[h]
                    if masked:
                        key = lax.broadcasted_iota(jnp.int32, sc.shape, 0)
                        query = lax.broadcasted_iota(jnp.int32, sc.shape, 1) + qt * QT
                        sc = jnp.where(key <= query, sc, -1e30)
                    new = jnp.maximum(top, jnp.max(sc, axis=0, keepdims=True))
                    p = jnp.exp(sc - new)
                    fade = jnp.exp(top - new)
                    total = total * fade + jnp.sum(p, axis=0, keepdims=True)
                    out = out * fade + nn(v.vt[l, b, head_rows[h], :], p.astype(BF16))
                    result.append((new, total, out))
                return tuple(result)

            start = (
                jnp.full((1, QT), -1e30, F32),
                jnp.zeros((1, QT), F32),
                jnp.zeros((HEAD_DIM, QT), F32),
            )
            if part == 0:
                carry = block(rank, (start, start), True)
                carry = lax.fori_loop(
                    rank - core, rank, functools.partial(block, masked=False), carry
                )
                for h in range(2):
                    v.top[h : h + 1, q_at] = carry[h][0]
                    v.lse[l, h : h + 1, q_at] = carry[h][1]
                    v.ot[l, head_rows[h], q_at] = carry[h][2]
                continue
            carry = tuple(
                (
                    v.top[h : h + 1, q_at],
                    v.lse[l, h : h + 1, q_at],
                    v.ot[l, head_rows[h], q_at],
                )
                for h in range(2)
            )
            carry = lax.fori_loop(0, 2 * zlo, functools.partial(block, masked=False), carry)
            for h in range(2):
                top, total, out = carry[h]
                v.ot[l, head_rows[h], q_at] = out / total
                v.lse[l, h : h + 1, q_at] = top + jnp.log(total)
            v.ob[l, q_at, :] = v.ot[l, :, q_at].T.astype(BF16)
            both = nn(v.ob[l, q_at, :], v.wout[l]) + v.part[q_at, :]
            both = both.astype(BF16)
            first = qt * QT // chunk
            for half in range(2):
                v.psend[s, half, first : first + QT // chunk] = both[
                    :, half * hd : (half + 1) * hd
                ].reshape(QT // chunk, chunk, hd)
            for pair in range(first // 2, (first + QT // chunk) // 2):
                rs_pair(s, lax.rem(pair - yy - 1 + 2 * ny, ny) + 1)

    def branch_reduce(s):
        rs_finish(s)
        for i in range(chunk // 16):
            at = slice(i * 16, (i + 1) * 16)
            ag_put(s, at, rs_sum(s, at))
        ag_start(s)

    grads = {0: (v.ge, v.r1e, v.r2e, v.s3e, v.r3e, v.k3e), 1: (v.gl, v.r1l, v.r2l, v.s3l, v.r3l, v.k3l)}

    def core_copy(l, p):
        g, r1 = grads[p][:2]
        return remote(
            g.at[l, 1 - core], r1.at[l], v.g1s.at[l, p], v.g1r.at[l, p], dp=other_core
        )

    def x_copy(l, p, k):
        r1, r2 = grads[p][1:3]
        to = lax.rem(xc + k, nx)
        return remote(
            r1.at[l, pl.ds(2 * to, 2)],
            r2.at[l, k - 1],
            v.g2s.at[l, p, k - 1],
            v.g2r.at[l, p, k - 1],
            dp=to * group + zlo * 2 + core,
        )

    def z_copy(l, p):
        return remote(
            grads[p][3].at[l], grads[p][4].at[l], v.g3s.at[l, p], v.g3r.at[l, p], dp=other_z
        )

    def grad_core(l, p):
        core_copy(l, p).start()

    def grad_x(l, p):
        core_copy(l, p).wait()
        g, r1 = grads[p][:2]

        def one(i, carry):
            for j in range(grow // 16):
                at = slice(j * 16, (j + 1) * 16)
                r1[l, i, at, :] = (
                    r1[l, i, at, :].astype(F32) + g[l, core, i, at, :].astype(F32)
                ).astype(BF16)
            return carry

        lax.fori_loop(0, nd // 2, one, 0)
        for k in range(1, nx):
            x_copy(l, p, k).start()

    def grad_z(l, p):
        _, r1, r2, s3, r3, k3 = grads[p]
        for k in range(1, nx):
            x_copy(l, p, k).wait()

        def total(z, at):
            value = r1[l, 2 * xc + z, at, :].astype(F32)
            for k in range(1, nx):
                value = value + r2[l, k - 1, z, at, :].astype(F32)
            return value

        for j in range(grow // 16):
            at = slice(j * 16, (j + 1) * 16)
            s3[l, at, :] = total(1 - zlo, at).astype(BF16)
        z_copy(l, p).start()
        for j in range(grow // 16):
            at = slice(j * 16, (j + 1) * 16)
            k3[l, at, :] = total(zlo, at)

    def grad_end(l, p):
        z_copy(l, p).wait()
        _, _, _, _, r3, k3 = grads[p]
        for j in range(grow // 16):
            at = slice(j * 16, (j + 1) * 16)
            total = k3[l, at, :] + r3[l, at, :].astype(F32)
            if p == 0:
                v.oo[l, at, :] = total[:, :width]
                v.od[l, at, :] = total[:, width : width + ff]
                v.oi[l, at, :] = total[:, width + ff :]
            else:
                for c in range(3):
                    v.oq[l, c, at, :] = total[:, c * width : (c + 1) * width]

    def start_gradient(l, at, gradient):
        v.dz[at, :] = gradient.astype(BF16)

    def attention_back(l, first, second):
        do = v.do[...]
        product = do.astype(F32).T * v.ot[l]
        v.delta[0:1, :] = jnp.sum(product[:HEAD_DIM], axis=0, keepdims=True)
        v.delta[1:2, :] = jnp.sum(product[HEAD_DIM:], axis=0, keepdims=True)
        v.dqt[...] = jnp.zeros_like(v.dqt)

        def piece(b, i, masked):
            at = slice(i * KT, (i + 1) * KT)
            keys = v.kv[l, b, at, :width]
            values = v.kv[l, b, at, width:]
            dk = jnp.zeros((KT, width), F32)
            dv = jnp.zeros((KT, width), F32)
            for h in range(2):
                head_rows = slice(h * HEAD_DIM, (h + 1) * HEAD_DIM)
                sc = nt(keys, v.qm[l, h])
                if masked:
                    key = lax.broadcasted_iota(jnp.int32, sc.shape, 0) + i * KT
                    query = lax.broadcasted_iota(jnp.int32, sc.shape, 1)
                    sc = jnp.where(key <= query, sc, -1e30)
                p = jnp.exp(sc - v.lse[l, h : h + 1, :])
                dp = nt(values, v.dom[h])
                ds = (p * (dp - v.delta[h : h + 1, :])).astype(BF16)
                dv = dv + nn(p.astype(BF16), v.dom[h])
                dk = dk + nn(ds, v.qm[l, h])
                v.dqt[head_rows, :] += nn(v.kt[l, b, head_rows, at], ds)
            return dk, dv

        def far(b, slot, received):
            for i in range(rows // KT):
                dk, dv = piece(b, i, False)
                at = slice(i * KT, (i + 1) * KT)
                if received:
                    dkv_copy(l, 0, i).wait_recv()
                    dk = dk + v.dkvi[l, 0, at, :width].astype(F32)
                    dv = dv + v.dkvi[l, 0, at, width:].astype(F32)
                v.dkvo[l, slot, at, :width] = dk.astype(BF16)
                v.dkvo[l, slot, at, width:] = dv.astype(BF16)
                dkv_copy(l, slot, i).start()

        @pl.when(zlo == 1)
        def _():
            far(1 - core, 0, False)
            first()
            far(core, 1, True)

        @pl.when(core == 1)
        def _():
            far(rank - 1, 2, False)

        @pl.when(rank == group - 1)
        def _():
            second()

        for i in range(rows // KT):
            dk, dv = piece(rank, i, True)
            at = slice(i * KT, (i + 1) * KT)
            v.own[at, :width] = dk
            v.own[at, width:] = dv

    def do_rows(l, at):
        do = nt(v.dz[at, :], v.wout[l]).astype(BF16)
        v.do[at, :] = do
        v.dom[0, at, :] = head_only(do, 0)
        v.dom[1, at, :] = head_only(do, 1)

    def dact_rows(l, at):
        v.dact[at, :] = nt(v.dz[at, :], v.wdown[l])

    def back_rows(l, at, size):
        def slope(i, acc):
            now = pl.ds(pl.multiple_of(at.start + i * ST, ST), ST)
            du = (v.dact[now, :] * v.u[l, now, :]).astype(BF16)
            v.du[now, :] = du
            return acc + jnp.sum(du.astype(F32).reshape(ST // 8, 8, ff), axis=0)

        v.binacc[l] += lax.fori_loop(0, size // ST, slope, jnp.zeros((8, ff), F32))
        v.dh1[at, :] = nt(v.du[at, :], v.win[l])

    def early_grads(l):
        def one(i, carry):
            at = rows_at(i, 2 * grow)
            dzt = v.dz[:, at].astype(F32).T.astype(BF16)
            ht = v.h1[l, :, at].astype(F32).T.astype(BF16)
            wo = nn(dzt, v.ob[l]).astype(BF16)
            wd = nn(dzt, v.act[l]).astype(BF16)
            wi = nn(ht, v.du[...]).astype(BF16)
            for c in range(2):
                part = slice(c * grow, (c + 1) * grow)
                v.ge[l, c, i, :, :width] = wo[part]
                v.ge[l, c, i, :, width : width + ff] = wd[part]
                v.ge[l, c, i, :, width + ff :] = wi[part]
            return carry

        lax.fori_loop(0, depth // (2 * grow), one, 0)

    def late_grads(l):
        def one(i, carry):
            at = rows_at(i, 2 * grow)
            ht = v.h0[l, :, at].astype(F32).T.astype(BF16)
            wq = nn(ht, v.dqkv[...]).astype(BF16)
            for c in range(2):
                v.gl[l, c, i] = wq[c * grow : (c + 1) * grow]
            return carry

        lax.fori_loop(0, depth // (2 * grow), one, 0)

    def qkv_back(l):
        @pl.when(zlo == 0)
        def _():
            grad_x(l, 0)

        for step, here in ((2, core == 0), (1, zlo == 0)):

            @pl.when(here)
            def _():
                for i in range(rows // KT):
                    dkv_copy(l, step, i).wait_recv()
                v.own[...] += v.dkvi[l, step].astype(F32)

        cosine, sine = v.cosine[...], -v.sine[...]
        v.dqkv[:, :width] = rotate(v.dqt[...].T * 0.125, cosine, sine).astype(BF16)
        v.dqkv[:, width : 2 * width] = rotate(v.own[:, :width], cosine, sine).astype(BF16)
        v.dqkv[:, 2 * width : 3 * width] = v.own[:, width:].astype(BF16)
        v.other[4 * l + 3 : 4 * l + 4, : 3 * width] = jnp.sum(
            v.dqkv[...].astype(F32), axis=0, keepdims=True
        )

        def one(i, carry):
            at = rows_at(i, MT)
            v.dh0[at, :] = nt(v.dqkv[at, :], v.wqkv[l])
            return carry

        lax.fori_loop(0, rows // MT, one, 0)

        def send(m, carry):
            pair = at_y(m)
            for i in range(2 * chunk // ST):
                at = pl.ds(pl.multiple_of(pair * 2 * chunk + i * ST, ST), ST)
                both = v.dh0[at, :] * v.gain[l, 0:1, :] + v.dh1[at, :] * v.gain[l, 1:2, :]
                both = both.astype(BF16)
                part = slice(i * ST % chunk, i * ST % chunk + ST)
                for half in range(2):
                    v.psend[0, half, 2 * pair + i * ST // chunk, part, :] = both[
                        :, half * hd : (half + 1) * hd
                    ]
            rs_pair(0, m)
            return carry

        lax.fori_loop(1, ny + 1, send, 0)

    def norm_grads(l):
        v.lnacc[...] = jnp.zeros_like(v.lnacc)

        def fold(value):
            return jnp.sum(value.reshape(2, 8, depth), axis=0)

        def one(i, carry):
            at = rows_at(i, 16)
            xhat = (stream_rows(l, at) - v.mu[l, at, :]) * v.rs[l, at, :]
            first, second = v.dh0[at, :], v.dh1[at, :]
            v.lnacc[0] += fold(first * xhat)
            v.lnacc[1] += fold(second * xhat)
            v.lnacc[2] += fold(first)
            v.lnacc[3] += fold(second)
            v.lnacc[4] += fold(v.dz[at, :].astype(F32))
            return carry

        lax.fori_loop(0, rows // 16, one, 0)
        for i in range(4):
            v.ln[4 * l + i : 4 * l + i + 1, :] = jnp.sum(v.lnacc[i], axis=0, keepdims=True)
        column = jnp.sum(v.lnacc[4], axis=0, keepdims=True)
        v.other[4 * l : 4 * l + 1, :] = column[:, :ff]
        v.other[4 * l + 1 : 4 * l + 2, :] = column[:, ff:]
        v.other[4 * l + 2 : 4 * l + 3, :] = jnp.sum(v.binacc[l], axis=0, keepdims=True)

    def stream_reduce(l):
        rs_finish(0)
        for i in range(chunk // 16):
            at = pl.ds(pl.multiple_of(me_t * chunk + i * 16, 16), 16)
            gd = rs_sum(0, slice(i * 16, (i + 1) * 16))
            r = v.rs[l, at, :]
            xhat = (stream_rows(l, at) - v.mu[l, at, :]) * r
            mean = jnp.mean(gd, axis=-1, keepdims=True)
            along = jnp.mean(gd * xhat, axis=-1, keepdims=True)
            dx = r * (gd - mean - xhat * along)
            ag_put(0, slice(i * 16, (i + 1) * 16), dx)
        ag_start(0)

    def small_core(i):
        mine, theirs = [(v.ln, v.ln1), (v.other, v.other1)][i]
        return remote(mine, theirs, v.s1s.at[i], v.s1r.at[i], dp=other_core)

    def small_dp(k, i):
        to = lax.rem(me_d + 2 * k, nd)
        mine, theirs = [(v.lnsum, v.ln3), (v.other, v.other2)][i]
        return remote(mine, theirs.at[k - 1], v.s3s.at[i, k - 1], v.s3r.at[i, k - 1], dp=to)

    def small_scatter(k):
        to = lax.rem(me_t + k, nt_dev)
        columns = pl.ds(pl.multiple_of(to * LANES, LANES), LANES)
        return remote(
            v.ln.at[:, columns], v.ln2.at[k - 1], v.s2s.at[k - 1], v.s2r.at[k - 1], tensor=to
        )

    def small_gather(k):
        to = lax.rem(me_t + k, nt_dev)
        block = v.lnall.at[me_t]
        return remote(block, block, v.s4s.at[k - 1], v.s4r.at[me_t], tensor=to)

    def small_start():
        for i in range(2):
            small_core(i).start()

    def small_second():
        for i in range(2):
            small_core(i).wait()
        v.ln[...] += v.ln1[...]
        v.other[...] += v.other1[...]
        for k in range(1, nt_dev):
            small_scatter(k).start()
        for k in range(1, nd // 2):
            small_dp(k, 1).start()

    def small_third():
        mine = pl.ds(pl.multiple_of(me_t * LANES, LANES), LANES)
        total = v.ln[:, mine]
        for k in range(1, nt_dev):
            small_scatter(k).wait()
            total = total + v.ln2[k - 1]
        v.lnsum[...] = total
        for k in range(1, nd // 2):
            small_dp(k, 0).start()

    def small_fourth():
        total = v.lnsum[...]
        for k in range(1, nd // 2):
            small_dp(k, 0).wait()
            total = total + v.ln3[k - 1]
        v.lnall[me_t] = total
        for k in range(1, nt_dev):
            small_gather(k).start()
        total = v.other[...]
        for k in range(1, nd // 2):
            small_dp(k, 1).wait()
            total = total + v.other2[k - 1]
        for l in range(LAYERS):
            for half in range(2):
                at = slice(half * ff, (half + 1) * ff)
                row = total[4 * l + half : 4 * l + half + 1, :]
                v.obout[l : l + 1, at] = row
                v.obdown[l : l + 1, at] = row
            v.obin[l : l + 1, :] = total[4 * l + 2 : 4 * l + 3, :]
            for c in range(3):
                at = slice(c * width, (c + 1) * width)
                v.obqkv[c, l : l + 1, :] = total[4 * l + 3 : 4 * l + 4, at]

    def small_end():
        for k in range(1, nt_dev):
            src = lax.rem(me_t + k, nt_dev)
            block = v.lnall.at[src]
            remote(block, block, v.s4s.at[k - 1], v.s4r.at[src], tensor=src).wait()
        for j in range(nt_dev):
            at = slice(j * LANES, (j + 1) * LANES)
            block = v.lnall[j]
            for l in range(LAYERS):
                v.ogain[l, :, at] = block[4 * l : 4 * l + 2, :]
                v.obias[l, :, at] = block[4 * l + 2 : 4 * l + 4, :]

    def nothing(at):
        pass

    def first_norm(i, carry):
        at = rows_at(i, ST)
        norm_rows(0, at, v.xt[at, :].astype(F32))
        return carry

    with jax.named_scope("norm0"):
        for i in range(TP):
            load_tok[i].wait()
            lax.fori_loop(i * rows // TP // ST, (i + 1) * rows // TP // ST, first_norm, 0, unroll=2)
    with jax.named_scope("qkv0"):
        for c in load_qkv[0]:
            c.wait()
        load_cos.wait()
        load_sin.wait()

        def first_qkv(i, carry):
            qkv_rows(0, rows_at(i, MT), MT)
            return carry

        lax.fori_loop(0, rows // MT, first_qkv, 0)
    with jax.named_scope("barrier"):
        pl.semaphore_wait(barrier, nt_dev - 1 + nd - 1)
    kv_send(0)
    v.ln[...] = jnp.zeros_like(v.ln)
    v.other[...] = jnp.zeros_like(v.other)
    v.binacc[...] = jnp.zeros_like(v.binacc)
    with jax.named_scope("ffn0"):
        for c in load_rest[0]:
            c.wait()

        def first_ffn(i, carry):
            feed_forward(0, rows_at(i, MT), MT)
            return carry

        lax.fori_loop(0, rows // MT, first_ffn, 0)
    with jax.named_scope("near0"):
        kv_near(0)
        attention(0, 0, 0)
    def first_gradients(z):
        @pl.when(zlo == z)
        def _():
            load_cot.wait()
            for c in load_rest[1]:
                c.wait()

            def copy_rows(i, carry):
                at = rows_at(i, ST)
                v.dz[at, :] = v.ct[at, :]
                v.g[at, :] = v.ct[at, :].astype(F32)
                return carry

            def rows_back(i, carry):
                at = rows_at(i, MT)
                do_rows(1, at)
                dact_rows(1, at)
                return carry

            lax.fori_loop(0, rows // ST, copy_rows, 0)
            lax.fori_loop(0, rows // MT, rows_back, 0)

    with jax.named_scope("dz1"):
        first_gradients(1)
    with jax.named_scope("kv0"):
        kv_far(0)
    with jax.named_scope("attn0"):
        attention(0, 0, 1)
    with jax.named_scope("dz1b"):
        first_gradients(0)
    with jax.named_scope("forward0"):
        rs_forward(0)
    with jax.named_scope("reduce0"):
        branch_reduce(0)

    def next_stream(at, z):
        x = v.xt[at, :].astype(F32) + (z + (v.bout[0:1, :] + v.bdown[0:1, :]))
        v.x[at, :] = x
        norm_rows(1, at, x)

    def next_qkv(at):
        qkv_rows(1, at, 2 * chunk)

    def next_ffn(at):
        feed_forward(1, at, 2 * chunk)
        back_rows(1, at, 2 * chunk)

    def next_both(at):
        next_qkv(at)
        next_ffn(at)

    with jax.named_scope("gather0"):
        for c in load_qkv[1]:
            c.wait()
        ag_forward(0)
        ag_pairs(0, 0, ny - 1, next_stream, next_both)
        ag_pairs(0, ny - 1, ny, next_stream, next_qkv)
        kv_send(1)
        ag_sent(0)
    with jax.named_scope("ffn1"):
        next_ffn(rows_at(at_y(place(ny - 1)), 2 * chunk))
    with jax.named_scope("near1"):
        kv_near(1)
        attention(1, 1, 0)
    with jax.named_scope("kv1"):
        kv_far(1)
    with jax.named_scope("attn1"):
        attention(1, 1, 1)

    with jax.named_scope("attn_grad1"):
        attention_back(1, lambda: None, lambda: rs_forward(1))

        @pl.when(rank != group - 1)
        def _():
            rs_forward(1)


    def forward_at(z):
        @pl.when(zlo == z)
        def _():
            rs_forward(0)

    def late_x(l):
        @pl.when(zlo == 1)
        def _():
            grad_x(l, 0)

    def early(l, z):
        @pl.when(zlo == z)
        def _():
            early_grads(l)
            grad_core(l, 0)

    with jax.named_scope("early1"):
        early(1, 0)
    with jax.named_scope("qkv_grad1"):
        qkv_back(1)
    with jax.named_scope("early1b"):
        early(1, 1)
    with jax.named_scope("norm_grad1"):
        norm_grads(1)
    with jax.named_scope("forward"):
        forward_at(1)
    with jax.named_scope("gx10"):
        late_x(1)
    with jax.named_scope("late1"):
        late_grads(1)
        grad_core(1, 1)
    with jax.named_scope("forward"):
        forward_at(0)
    with jax.named_scope("gx11"):
        grad_x(1, 1)
    with jax.named_scope("stream_reduce1"):
        stream_reduce(1)

    def next_gradient(at, dx):
        gradient = v.g[at, :] + dx
        v.g[at, :] = gradient
        v.dz[at, :] = gradient.astype(BF16)

    def next_do(at):
        do_rows(0, at)

    def next_slope(at):
        dact_rows(0, at)
        back_rows(0, at, 2 * chunk)

    def next_back(at):
        next_do(at)
        next_slope(at)

    with jax.named_scope("gather2"):
        ag_forward(0)
        ag_pairs(0, 0, ny // 2, next_gradient, next_back)
    with jax.named_scope("reduce1"):
        branch_reduce(1)
    with jax.named_scope("gather2b"):
        ag_pairs(0, ny // 2, ny - 1, next_gradient, next_back)
        ag_pairs(0, ny - 1, ny, next_gradient, next_do)
        ag_sent(0)
    with jax.named_scope("attn_grad0"):
        attention_back(0, lambda: ag_forward(1), lambda: None)
    with jax.named_scope("slope0"):
        next_slope(rows_at(at_y(place(ny - 1)), 2 * chunk))
    with jax.named_scope("forward1b"):

        @pl.when(zlo == 0)
        def _():
            ag_forward(1)

    with jax.named_scope("early0"):
        early(0, 0)
    with jax.named_scope("qkv_grad0"):
        qkv_back(0)
    with jax.named_scope("early0b"):
        early(0, 1)
    with jax.named_scope("norm_grad0"):
        norm_grads(0)
        small_start()
    with jax.named_scope("gx00"):
        late_x(0)
    with jax.named_scope("small_second"):
        small_second()
    with jax.named_scope("forward"):
        forward_at(1)
    with jax.named_scope("late0"):
        late_grads(0)
        grad_core(0, 1)
    with jax.named_scope("forward"):
        forward_at(0)
    with jax.named_scope("small_third"):
        small_third()
    with jax.named_scope("gx01"):
        grad_x(0, 1)

    def last_stream(at, z):
        v.x[at, :] = v.x[at, :] + (z + (v.bout[1:2, :] + v.bdown[1:2, :]))

    store_x = pltpu.make_async_copy(v.x, v.ox, v.lsem.at[0])
    store_g = pltpu.make_async_copy(v.g, v.og, v.lsem.at[1])
    with jax.named_scope("stream_reduce0"):
        stream_reduce(0)
    with jax.named_scope("forward0c"):
        ag_forward(0)
    with jax.named_scope("gz1"):
        grad_z(1, 0)
        grad_z(1, 1)
    with jax.named_scope("gather1"):
        ag_pairs(1, 0, ny, last_stream, nothing)
        ag_sent(1)
        store_x.start()

    def last_gradient(at, dx):
        v.g[at, :] = v.g[at, :] + dx

    with jax.named_scope("gather3"):
        ag_pairs(0, 0, ny // 2, last_gradient, nothing)
    with jax.named_scope("small_fourth"):
        small_fourth()
    with jax.named_scope("gz00"):
        grad_z(0, 0)
    with jax.named_scope("gather3a"):
        ag_pairs(0, ny // 2, ny - 1, last_gradient, nothing)
    with jax.named_scope("gz01"):
        grad_z(0, 1)
    with jax.named_scope("gather3b"):
        ag_pairs(0, ny - 1, ny, last_gradient, nothing)
        store_g.start()
        ag_sent(0)
    with jax.named_scope("gend1"):
        grad_end(1, 0)
        grad_end(1, 1)
    with jax.named_scope("small_end"):
        small_end()
    with jax.named_scope("gend0"):
        grad_end(0, 0)
        grad_end(0, 1)
        store_x.wait()
        store_g.wait()
    for l in range(LAYERS):
        for step, here in ((0, core == 0), (1, zlo == 0), (2, zlo == 1)):

            @pl.when(here)
            def _():
                kv_copy(l, step).wait_send()

        for step, here in ((0, zlo == 1), (1, zlo == 1), (2, core == 1)):

            @pl.when(here)
            def _():
                for i in range(rows // KT):
                    dkv_copy(l, step, i).wait_send()


def store_kernel(count, *refs):
    given, kept = refs[:count], refs[count:]
    for i in range(2):
        kept[i][...] = given[i][...]

    @pl.when(pl.program_id(0) == 0)
    def _():
        for i in range(2, count):
            kept[i][...] = given[i][...]


def on_device(nt_dev, nd, *args):
    tokens, cotangent, ln_gain, ln_bias, w_qkv, b_qkv, w_out, b_out, w_in, b_in, w_down, b_down = args
    rows, depth = tokens.shape
    width = w_out.shape[1]
    ff = w_in.shape[2]
    group = SEQ // rows
    chunk = rows // nt_dev
    grow = depth // nd
    half = nd // 2
    nx = nd // group
    early = width + 2 * ff
    late = 3 * width
    cosine, sine = rope_constants()
    vm = pltpu.VMEM
    dma = pltpu.SemaphoreType.DMA
    two = LAYERS
    scratch = [
        vm((two, depth, 3 * width), BF16),
        vm((two, width, depth), BF16),
        vm((two, depth, ff), BF16),
        vm((two, ff, depth), BF16),
        vm((rows, LANES), F32),
        vm((rows, LANES), F32),
        vm((rows, depth), F32),
        vm((rows, depth), F32),
        vm((rows, depth), BF16),
        vm((rows, depth), BF16),
        vm((two, rows, depth), BF16),
        vm((two, rows, depth), BF16),
        vm((two, 2, rows, width), BF16),
        vm((two, group, rows, 2 * width), BF16),
        vm((two, group, width, rows), BF16),
        vm((two, group, width, rows), BF16),
        vm((two, rows, width), BF16),
        vm((two, width, rows), F32),
        vm((8, rows), F32),
        vm((two, 8, rows), F32),
        vm((two, rows, ff), F32),
        vm((two, rows, ff), BF16),
        vm((two, rows, 1), F32),
        vm((two, rows, 1), F32),
        vm((rows, depth), F32),
        vm((2, 2, nt_dev, chunk, depth // 2), BF16),
        vm((2, nt_dev // 2 - 1, 2, chunk, depth // 2), BF16),
        vm((2, nt_dev // 2, chunk, depth // 2), BF16),
        vm((2, chunk, depth // 2), BF16),
        vm((2, nt_dev // 2 - 1, chunk, depth // 2), BF16),
        vm((2, chunk, depth // 2), BF16),
        vm((2, nt_dev // 2 - 1, chunk, depth // 2), BF16),
        vm((2, 2, nt_dev, chunk, depth // 2), BF16),
        vm((rows, depth), BF16),
        vm((rows, width), BF16),
        vm((2, rows, width), BF16),
        vm((8, rows), F32),
        vm((width, rows), F32),
        vm((two, 3, rows, 2 * width), BF16),
        vm((two, 3, rows, 2 * width), BF16),
        vm((rows, 2 * width), F32),
        vm((rows, 3 * width), BF16),
        vm((rows, ff), BF16),
        vm((rows, ff), F32),
        vm((two, 8, ff), F32),
        vm((rows, depth), F32),
        vm((rows, depth), F32),
        vm((two, 2, half, grow, early), BF16),
        vm((two, 2, half, grow, late), BF16),
        vm((two, half, grow, early), BF16),
        vm((two, half, grow, late), BF16),
        vm((two, nx - 1, 2, grow, early), BF16),
        vm((two, nx - 1, 2, grow, late), BF16),
        vm((two, grow, early), BF16),
        vm((two, grow, late), BF16),
        vm((two, grow, early), BF16),
        vm((two, grow, late), BF16),
        vm((two, grow, early), F32),
        vm((two, grow, late), F32),
        vm((8, depth), F32),
        vm((8, ff), F32),
        vm((8, depth), F32),
        vm((8, ff), F32),
        vm((nt_dev - 1, 8, LANES), F32),
        vm((half - 1, 8, ff), F32),
        vm((8, LANES), F32),
        vm((half - 1, 8, LANES), F32),
        vm((nt_dev, 8, LANES), F32),
        vm((5, 8, depth), F32),
        dma((16 + TP,)),
        dma((two, 3)),
        dma((two, 3)),
        dma((two, 3, rows // KT)),
        dma((two, 3, rows // KT)),
        dma((2, 7 * (nt_dev // 2) - 3)),
        dma((2, 7 * (nt_dev // 2) - 3)),
        dma((two, 2)),
        dma((two, 2)),
        dma((two, 2, nx - 1)),
        dma((two, 2, nx - 1)),
        dma((two, 2)),
        dma((two, 2)),
        dma((2,)),
        dma((2,)),
        dma((nt_dev - 1,)),
        dma((nt_dev - 1,)),
        dma((2, half - 1)),
        dma((2, half - 1)),
        dma((nt_dev - 1,)),
        dma((nt_dev,)),
    ]
    here = pl.BlockSpec(memory_space=pltpu.VMEM)
    away = pl.BlockSpec(memory_space=pl.ANY)
    shapes = [
        (rows, depth),
        (rows, depth),
        (two, 2, depth),
        (two, 2, depth),
        (3, two, width),
        (two, depth),
        (two, ff),
        (two, depth),
        (two, 3, grow, width),
        (two, grow, width),
        (two, grow, ff),
        (two, grow, ff),
    ]
    out = pl.pallas_call(
        functools.partial(step_kernel, nt_dev, nd),
        out_shape=[jax.ShapeDtypeStruct(s, F32) for s in shapes],
        in_specs=[away, away, here, here, away, here, away, here, away, here, away, here, away, away],
        out_specs=[away] * 2 + [here] * (len(shapes) - 2),
        scratch_shapes=scratch,
        compiler_params=pltpu.CompilerParams(
            collective_id=0, has_side_effects=True, vmem_limit_bytes=64 * 1024 * 1024 - 65536
        ),
    )(
        tokens,
        cotangent,
        ln_gain,
        ln_bias,
        w_qkv.transpose(0, 2, 1, 3),
        b_qkv.transpose(1, 0, 2),
        w_out,
        b_out,
        w_in,
        b_in,
        w_down,
        b_down,
        jnp.asarray(cosine),
        jnp.asarray(sine),
    )
    out = pl.pallas_call(
        functools.partial(store_kernel, len(shapes)),
        out_shape=[jax.ShapeDtypeStruct(s, F32) for s in shapes],
        grid=(PARTS,),
        in_specs=[pl.BlockSpec((rows // PARTS, depth), lambda i: (i, 0))] * 2
        + [here] * (len(shapes) - 2),
        out_specs=[pl.BlockSpec((rows // PARTS, depth), lambda i: (i, 0))] * 2
        + [here] * (len(shapes) - 2),
    )(*out)
    x, g, gain, bias, bqkv, bout, b_in_g, bdown, wq, wo, wi, wd = out
    return (
        x,
        g,
        gain,
        bias,
        wq.transpose(0, 2, 1, 3),
        bqkv.transpose(1, 0, 2),
        wo.transpose(0, 2, 1),
        bout,
        wi,
        b_in_g,
        wd.transpose(0, 2, 1),
        bdown,
    )


def solution(mesh):
    return jax.shard_map(
        functools.partial(on_device, mesh.shape["tensor"], mesh.shape["dp"]),
        mesh=mesh,
        in_specs=(
            P("dp", None),
            P("dp", None),
            P(),
            P(),
            P(None, None, None, "tensor"),
            P(None, None, "tensor"),
            P(None, "tensor", None),
            P(),
            P(None, None, "tensor"),
            P(None, "tensor"),
            P(None, "tensor", None),
            P(),
        ),
        out_specs=(
            P("dp", None),
            P("dp", None),
            P(),
            P(),
            P(None, "dp", None, "tensor"),
            P(None, None, "tensor"),
            P(None, "tensor", "dp"),
            P(),
            P(None, "dp", "tensor"),
            P(None, "tensor"),
            P(None, "tensor", "dp"),
            P(),
        ),
        check_vma=False,
    )
```

```python
import functools

import jax
import jax.numpy as jnp
import numpy as np
from jax import lax
from jax.experimental import pallas as pl
from jax.experimental.pallas import tpu as pltpu
from jax.sharding import PartitionSpec as P

HEAD_DIM = 64
ROT = 16
SEQ = 2048
LAYERS = 2
EPS = 1e-05
F32 = jnp.float32
BF16 = jnp.bfloat16
MESH = pl.DeviceIdType.MESH
LANES = 128
QT = 256
KT = 256
MT = 256
ST = 32
TP = 4
PARTS = 2


def nn(a, b):
    return jnp.dot(a, b, preferred_element_type=F32)


def nt(a, b):
    return lax.dot_general(a, b, (((1,), (1,)), ((), ())), preferred_element_type=F32)


def rope_constants():
    half = ROT // 2
    exponent = np.arange(0, ROT, 2).astype(np.float32) / np.float32(ROT)
    inverse = (np.float32(1.0) / np.float32(10000.0) ** exponent).astype(np.float32)
    angles = np.arange(SEQ).astype(np.float32)[:, None] * inverse[None, :]
    cosine = np.ones((SEQ, LANES), np.float32)
    sine = np.zeros((SEQ, LANES), np.float32)
    for start in range(0, LANES, HEAD_DIM):
        cosine[:, start : start + half] = np.cos(angles)
        cosine[:, start + half : start + ROT] = np.cos(angles)
        sine[:, start : start + half] = -np.sin(angles)
        sine[:, start + half : start + ROT] = np.sin(angles)
    return cosine, sine


def rotate(values, cosine, sine):
    half = ROT // 2
    lane = lax.broadcasted_iota(jnp.int32, values.shape, 1)
    partner = jnp.where(
        lane % HEAD_DIM < half,
        pltpu.roll(values, LANES - half, 1),
        pltpu.roll(values, half, 1),
    )
    return values * cosine + partner * sine


def head_only(values, head):
    lane = lax.broadcasted_iota(jnp.int32, values.shape, 1)
    return jnp.where(lane // HEAD_DIM == head, values, jnp.zeros_like(values))


def rows_at(step, size):
    return pl.ds(pl.multiple_of(step * size, size), size)


def remote(src, dst, send_sem, recv_sem, **device):
    return pltpu.make_async_remote_copy(
        src_ref=src,
        dst_ref=dst,
        send_sem=send_sem,
        recv_sem=recv_sem,
        device_id=device,
        device_id_type=MESH,
    )


class Refs:
    pass


def step_kernel(nt_dev, nd, *refs):
    names = (
        "tok", "cot", "gain", "bias", "wqkv_h", "bqkv", "wout_h", "bout", "win_h", "bin",
        "wdown_h", "bdown", "cos_h", "sin_h", "ox", "og", "ogain", "obias", "obqkv", "obout",
        "obin", "obdown", "oq", "oo", "oi", "od", "wqkv", "wout", "win", "wdown", "cosine",
        "sine", "x", "g", "xt", "ct", "h0", "h1", "qm", "kv", "kt", "vt", "ob", "ot", "top",
        "lse", "u", "act", "mu", "rs", "part", "psend", "ra", "rb", "sa", "sb", "r2a", "r2b",
        "agbuf", "dz", "do", "dom", "delta", "dqt", "dkvo", "dkvi", "own", "dqkv", "du", "dact",
        "binacc", "dh0", "dh1", "ge", "gl", "r1e", "r1l", "r2e", "r2l", "s3e", "s3l", "r3e",
        "r3l", "k3e", "k3l", "ln", "other", "ln1", "other1", "ln2", "other2", "lnsum", "ln3",
        "lnall", "lnacc", "lsem", "kvs", "kvr", "dks", "dkr", "ars", "arr", "g1s", "g1r", "g2s",
        "g2r", "g3s", "g3r", "s1s", "s1r", "s2s", "s2r", "s3s", "s3r", "s4s", "s4r",
    )
    assert len(names) == len(refs)
    v = Refs()
    v.__dict__.update(zip(names, refs))
    rows, depth = v.x.shape
    group = SEQ // rows
    nx = nd // group
    chunk = rows // nt_dev
    grow = depth // nd
    width = v.wout.shape[1]
    ff = v.win.shape[2]

    me_t = lax.axis_index("tensor")
    me_d = lax.axis_index("dp")
    rank = lax.rem(me_d, group)
    core = lax.rem(me_d, 2)
    zlo = lax.rem(me_d // 2, 2)
    xc = me_d // group
    ny = nt_dev // 2
    hd = depth // 2
    yy = me_t // 2
    zh = lax.rem(me_t, 2)
    other_zh = me_t + 1 - 2 * zh
    other_core = me_d + 1 - 2 * core
    other_z = me_d + 2 - 4 * zlo

    barrier = pltpu.get_barrier_semaphore()
    for k in range(1, nt_dev):
        pl.semaphore_signal(
            barrier, inc=1, device_id={"tensor": lax.rem(me_t + k, nt_dev)}, device_id_type=MESH
        )
    for k in range(1, nd):
        pl.semaphore_signal(
            barrier, inc=1, device_id={"dp": lax.rem(me_d + k, nd)}, device_id_type=MESH
        )

    parts = [slice(i * rows // TP, (i + 1) * rows // TP) for i in range(TP)]

    def load(src, dst, index):
        copy = pltpu.make_async_copy(src, dst, v.lsem.at[index])
        copy.start()
        return copy

    load_tok = [load(v.tok.at[at], v.xt.at[at], 16 + i) for i, at in enumerate(parts)]
    load_cos = load(v.cos_h.at[rows_at(rank, rows)], v.cosine, 1)
    load_sin = load(v.sin_h.at[rows_at(rank, rows)], v.sine, 2)
    load_qkv = []
    load_rest = []
    for l in range(LAYERS):
        load_qkv.append(
            [
                load(
                    v.wqkv_h.at[l, c],
                    v.wqkv.at[l, :, pl.ds(c * width, width)],
                    4 + 6 * l + c,
                )
                for c in range(3)
            ]
        )
        load_rest.append(
            [
                load(v.win_h.at[l], v.win.at[l], 4 + 6 * l + 3),
                load(v.wdown_h.at[l], v.wdown.at[l], 4 + 6 * l + 4),
                load(v.wout_h.at[l], v.wout.at[l], 4 + 6 * l + 5),
            ]
        )
    load_cot = load(v.cot, v.ct, 3)

    def norm_rows(l, at, x):
        mean = jnp.mean(x, axis=-1, keepdims=True)
        center = x - mean
        spread = jnp.mean(center * center, axis=-1, keepdims=True)
        r = lax.rsqrt(spread + EPS)
        xhat = center * r
        v.mu[l, at, :] = mean
        v.rs[l, at, :] = r
        v.h0[l, at, :] = (xhat * v.gain[l, 0:1, :] + v.bias[l, 0:1, :]).astype(BF16)
        v.h1[l, at, :] = (xhat * v.gain[l, 1:2, :] + v.bias[l, 1:2, :]).astype(BF16)

    def stream_rows(l, at):
        if l == 0:
            return v.xt[at, :].astype(F32)
        return v.x[at, :]

    def at_y(k):
        return lax.rem(yy + k, ny)

    def copy_of(s, src, dst, sem, to):
        return remote(src, dst, v.ars.at[s, sem], v.arr.at[s, sem], tensor=to)

    def a1(s, k):
        to = at_y(k)
        return copy_of(
            s, v.psend.at[s, 0, pl.ds(2 * to, 2)], v.ra.at[s, k - 1], k - 1, 2 * to + zh
        )

    def b1(s, m):
        to = at_y(m)
        return copy_of(
            s, v.psend.at[s, 1, 2 * to + 1 - zh], v.rb.at[s, to], ny - 2 + m, other_zh
        )

    def a2(s):
        return copy_of(s, v.sa.at[s], v.r2a.at[s], 2 * ny - 1, other_zh)

    def b2(s, k):
        return copy_of(
            s, v.sb.at[s, k - 1], v.r2b.at[s, k - 1], 2 * ny - 1 + k, 2 * at_y(k) + zh
        )

    def rs_pair(s, m):
        b1(s, m).start()

        @pl.when(m < ny)
        def _():
            a1(s, m).start()

    def rs_forward(s):
        for m in range(1, ny):
            b1(s, m).wait_recv()
            to = at_y(m)
            v.sb[s, m - 1] = (
                v.psend[s, 1, 2 * to + zh].astype(F32) + v.rb[s, to].astype(F32)
            ).astype(BF16)
            b2(s, m).start()
        for k in range(1, ny):
            a1(s, k).wait_recv()
        total = v.psend[s, 0, other_zh].astype(F32)
        for k in range(1, ny):
            total = total + v.ra[s, k - 1, 1 - zh].astype(F32)
        v.sa[s] = total.astype(BF16)
        a2(s).start()
        b1(s, ny).wait_recv()

    def rs_finish(s):
        a2(s).wait()
        for k in range(1, ny):
            b2(s, k).wait()
            a1(s, k).wait_send()
        for m in range(1, ny + 1):
            b1(s, m).wait_send()

    def rs_sum(s, at):
        first = v.psend[s, 0, me_t, at, :].astype(F32) + v.r2a[s, at, :].astype(F32)
        second = v.psend[s, 1, me_t, at, :].astype(F32) + v.rb[s, yy, at, :].astype(F32)
        for k in range(1, ny):
            first = first + v.ra[s, k - 1, zh, at, :].astype(F32)
            second = second + v.r2b[s, k - 1, at, :].astype(F32)
        return jnp.concatenate([first, second], axis=1)

    def ag_copy(s, half, chunk_at, sem, to):
        block = v.agbuf.at[s, :, chunk_at] if s == 1 else v.agbuf.at[s, half, chunk_at]
        return copy_of(s, block, block, sem, to)

    ag0 = 3 * ny - 1
    near_first = sorted(range(1, ny), key=lambda k: min(k, ny - k))

    def gz(s):
        return ag_copy(s, 0, me_t, ag0, other_zh)

    def gy(s, k):
        return ag_copy(s, 0, me_t, ag0 + k, 2 * at_y(k) + zh)

    def fy(s, k):
        return ag_copy(s, 0, other_zh, ag0 + ny - 1 + k, 2 * at_y(k) + zh)

    def by(s, k):
        return ag_copy(s, 1, me_t, ag0 + 2 * ny - 2 + k, 2 * at_y(k) + zh)

    def bz(s, m):
        return ag_copy(s, 1, 2 * at_y(m) + zh, ag0 + 3 * ny - 2 + m, other_zh)

    def place(step):
        return ((step + 1) // 2 * (2 * (step % 2) - 1) + ny) % ny

    def arrived(s, half, chunk_at, sem):
        ag_copy(s, half, chunk_at, sem, other_zh).wait_recv()

    def ag_put(s, at, value):
        v.agbuf[s, 0, me_t, at, :] = value[:, :hd].astype(BF16)
        v.agbuf[s, 1, me_t, at, :] = value[:, hd:].astype(BF16)

    def ag_start(s):
        gz(s).start()
        if s == 0:
            for k in near_first:
                by(s, k).start()
            bz(s, 0).start()
        for k in near_first:
            gy(s, k).start()

    def ag_forward(s):
        arrived(s, 0, other_zh, ag0)
        for k in near_first:
            fy(s, k).start()
        if s == 0:
            for k in near_first:
                arrived(s, 1, 2 * at_y(ny - k) + zh, ag0 + 2 * ny - 2 + k)
                bz(s, ny - k).start()

    def ag_pairs(s, first, last, use, after):
        def one(step, carry):
            m = place(step)
            pair = at_y(m)

            @pl.when(m > 0)
            def _():
                arrived(s, 0, 2 * pair + zh, ag0 + ny - m)
                arrived(s, 0, 2 * pair + 1 - zh, ag0 + 2 * ny - 1 - m)

            if s == 0:
                arrived(s, 1, 2 * pair + 1 - zh, ag0 + 3 * ny - 2 + m)
            for i in range(2):
                src = 2 * pair + i
                for j in range(chunk // ST):
                    at = slice(j * ST, (j + 1) * ST)
                    use(
                        pl.ds(pl.multiple_of(src * chunk + j * ST, ST), ST),
                        jnp.concatenate(
                            [v.agbuf[s, 0, src, at, :], v.agbuf[s, 1, src, at, :]], axis=1
                        ).astype(F32),
                    )
            after(rows_at(pair, 2 * chunk))
            return carry

        lax.fori_loop(first, last, one, 0)

    def ag_sent(s):
        gz(s).wait_send()
        for k in range(1, ny):
            gy(s, k).wait_send()
            fy(s, k).wait_send()
        if s == 0:
            bz(s, 0).wait_send()
            for k in range(1, ny):
                by(s, k).wait_send()
                bz(s, k).wait_send()

    def kv_copy(l, step):
        slot, to = [(rank, other_core), (rank, other_z), (rank - 2, other_core)][step]
        block = v.kv.at[l, slot]
        return remote(block, block, v.kvs.at[l, step], v.kvr.at[l, step], dp=to)

    def kv_in(l, step):
        slot = [rank - 1, rank - 2, rank - 1 - 2 * core][step]
        block = v.kv.at[l, slot]
        return remote(block, block, v.kvs.at[l, step], v.kvr.at[l, step], dp=other_core)

    def dkv_copy(l, step, i):
        at = slice(i * KT, (i + 1) * KT)
        return remote(
            v.dkvo.at[l, step, at],
            v.dkvi.at[l, step, at],
            v.dks.at[l, step, i],
            v.dkr.at[l, step, i],
            dp=other_z if step == 1 else other_core,
        )

    def transpose_block(l, b):
        block = v.kv[l, b].astype(F32)
        v.kt[l, b] = block[:, :width].T.astype(BF16)
        v.vt[l, b] = block[:, width:].T.astype(BF16)

    def qkv_rows(l, at, size):
        mixed = nn(v.h0[l, at, :], v.wqkv[l])
        cosine, sine = v.cosine[at, :], v.sine[at, :]
        q = rotate(mixed[:, :width] + v.bqkv[0, l : l + 1, :], cosine, sine).astype(BF16)
        k = rotate(mixed[:, width : 2 * width] + v.bqkv[1, l : l + 1, :], cosine, sine)
        val = mixed[:, 2 * width :] + v.bqkv[2, l : l + 1, :]
        scaled = (q.astype(F32) * 0.125).astype(BF16)
        v.qm[l, 0, at, :] = head_only(scaled, 0)
        v.qm[l, 1, at, :] = head_only(scaled, 1)
        v.kv[l, rank, at, :width] = k.astype(BF16)
        v.kv[l, rank, at, width:] = val.astype(BF16)

    def kv_send(l):
        @pl.when(zlo == 0)
        def _():
            kv_copy(l, 1).start()

        @pl.when(core == 0)
        def _():
            kv_copy(l, 0).start()

    def kv_near(l):
        transpose_block(l, rank)

        @pl.when(core == 1)
        def _():
            kv_in(l, 0).wait_recv()
            transpose_block(l, rank - 1)

    def kv_far(l):
        @pl.when(zlo == 1)
        def _():
            kv_in(l, 1).wait_recv()
            kv_copy(l, 2).start()
            transpose_block(l, rank - 2)
            kv_in(l, 2).wait_recv()
            transpose_block(l, rank - 1 - 2 * core)

    def feed_forward(l, at, size):
        v.u[l, at, :] = nn(v.h1[l, at, :], v.win[l]) + v.bin[l : l + 1, :]

        def activate(i, carry):
            now = pl.ds(pl.multiple_of(at.start + i * ST, ST), ST)
            u = v.u[l, now, :]
            inner = 0.5 * (1.0 + lax.erf(u * np.float32(0.5**0.5)))
            v.act[l, now, :] = (u * inner).astype(BF16)
            v.u[l, now, :] = inner + u * jnp.exp(-0.5 * u * u) * np.float32((2.0 * np.pi) ** -0.5)
            return carry

        lax.fori_loop(0, size // ST, activate, 0)
        v.part[at, :] = nn(v.act[l, at, :], v.wdown[l])

    def attention(l, s, part):
        for qt in range(rows // QT):
            q_at = slice(qt * QT, (qt + 1) * QT)
            head_rows = [slice(h * HEAD_DIM, (h + 1) * HEAD_DIM) for h in range(2)]

            def block(b, carry, masked):
                keys = v.kv[l, b, :, :width]
                scores = [nt(keys, v.qm[l, h, q_at, :]) for h in range(2)]
                result = []
                for h in range(2):
                    top, total, out = carry[h]
                    sc = scores[h]
                    if masked:
                        key = lax.broadcasted_iota(jnp.int32, sc.shape, 0)
                        query = lax.broadcasted_iota(jnp.int32, sc.shape, 1) + qt * QT
                        sc = jnp.where(key <= query, sc, -1e30)
                    new = jnp.maximum(top, jnp.max(sc, axis=0, keepdims=True))
                    p = jnp.exp(sc - new)
                    fade = jnp.exp(top - new)
                    total = total * fade + jnp.sum(p, axis=0, keepdims=True)
                    out = out * fade + nn(v.vt[l, b, head_rows[h], :], p.astype(BF16))
                    result.append((new, total, out))
                return tuple(result)

            start = (
                jnp.full((1, QT), -1e30, F32),
                jnp.zeros((1, QT), F32),
                jnp.zeros((HEAD_DIM, QT), F32),
            )
            if part == 0:
                carry = block(rank, (start, start), True)
                carry = lax.fori_loop(
                    rank - core, rank, functools.partial(block, masked=False), carry
                )
                for h in range(2):
                    v.top[h : h + 1, q_at] = carry[h][0]
                    v.lse[l, h : h + 1, q_at] = carry[h][1]
                    v.ot[l, head_rows[h], q_at] = carry[h][2]
                continue
            carry = tuple(
                (
                    v.top[h : h + 1, q_at],
                    v.lse[l, h : h + 1, q_at],
                    v.ot[l, head_rows[h], q_at],
                )
                for h in range(2)
            )
            carry = lax.fori_loop(0, 2 * zlo, functools.partial(block, masked=False), carry)
            for h in range(2):
                top, total, out = carry[h]
                v.ot[l, head_rows[h], q_at] = out / total
                v.lse[l, h : h + 1, q_at] = top + jnp.log(total)
            v.ob[l, q_at, :] = v.ot[l, :, q_at].T.astype(BF16)
            both = nn(v.ob[l, q_at, :], v.wout[l]) + v.part[q_at, :]
            both = both.astype(BF16)
            first = qt * QT // chunk
            for half in range(2):
                v.psend[s, half, first : first + QT // chunk] = both[
                    :, half * hd : (half + 1) * hd
                ].reshape(QT // chunk, chunk, hd)
            for pair in range(first // 2, (first + QT // chunk) // 2):
                rs_pair(s, lax.rem(pair - yy - 1 + 2 * ny, ny) + 1)

    def branch_reduce(s):
        rs_finish(s)
        for i in range(chunk // 16):
            at = slice(i * 16, (i + 1) * 16)
            ag_put(s, at, rs_sum(s, at))
        ag_start(s)

    grads = {0: (v.ge, v.r1e, v.r2e, v.s3e, v.r3e, v.k3e), 1: (v.gl, v.r1l, v.r2l, v.s3l, v.r3l, v.k3l)}

    def core_copy(l, p):
        g, r1 = grads[p][:2]
        return remote(
            g.at[l, 1 - core], r1.at[l], v.g1s.at[l, p], v.g1r.at[l, p], dp=other_core
        )

    def x_copy(l, p, k):
        r1, r2 = grads[p][1:3]
        to = lax.rem(xc + k, nx)
        return remote(
            r1.at[l, pl.ds(2 * to, 2)],
            r2.at[l, k - 1],
            v.g2s.at[l, p, k - 1],
            v.g2r.at[l, p, k - 1],
            dp=to * group + zlo * 2 + core,
        )

    def z_copy(l, p):
        return remote(
            grads[p][3].at[l], grads[p][4].at[l], v.g3s.at[l, p], v.g3r.at[l, p], dp=other_z
        )

    def grad_core(l, p):
        core_copy(l, p).start()

    def grad_x(l, p):
        core_copy(l, p).wait()
        g, r1 = grads[p][:2]

        def one(i, carry):
            for j in range(grow // 16):
                at = slice(j * 16, (j + 1) * 16)
                r1[l, i, at, :] = (
                    r1[l, i, at, :].astype(F32) + g[l, core, i, at, :].astype(F32)
                ).astype(BF16)
            return carry

        lax.fori_loop(0, nd // 2, one, 0)
        for k in range(1, nx):
            x_copy(l, p, k).start()

    def grad_z(l, p):
        _, r1, r2, s3, r3, k3 = grads[p]
        for k in range(1, nx):
            x_copy(l, p, k).wait()

        def total(z, at):
            value = r1[l, 2 * xc + z, at, :].astype(F32)
            for k in range(1, nx):
                value = value + r2[l, k - 1, z, at, :].astype(F32)
            return value

        for j in range(grow // 16):
            at = slice(j * 16, (j + 1) * 16)
            s3[l, at, :] = total(1 - zlo, at).astype(BF16)
        z_copy(l, p).start()
        for j in range(grow // 16):
            at = slice(j * 16, (j + 1) * 16)
            k3[l, at, :] = total(zlo, at)

    def grad_end(l, p):
        z_copy(l, p).wait()
        _, _, _, _, r3, k3 = grads[p]
        for j in range(grow // 16):
            at = slice(j * 16, (j + 1) * 16)
            total = k3[l, at, :] + r3[l, at, :].astype(F32)
            if p == 0:
                v.oo[l, at, :] = total[:, :width]
                v.od[l, at, :] = total[:, width : width + ff]
                v.oi[l, at, :] = total[:, width + ff :]
            else:
                for c in range(3):
                    v.oq[l, c, at, :] = total[:, c * width : (c + 1) * width]

    def start_gradient(l, at, gradient):
        v.dz[at, :] = gradient.astype(BF16)

    def attention_back(l, first, second):
        do = v.do[...]
        product = do.astype(F32).T * v.ot[l]
        v.delta[0:1, :] = jnp.sum(product[:HEAD_DIM], axis=0, keepdims=True)
        v.delta[1:2, :] = jnp.sum(product[HEAD_DIM:], axis=0, keepdims=True)
        v.dqt[...] = jnp.zeros_like(v.dqt)

        def piece(b, i, masked):
            at = slice(i * KT, (i + 1) * KT)
            keys = v.kv[l, b, at, :width]
            values = v.kv[l, b, at, width:]
            dk = jnp.zeros((KT, width), F32)
            dv = jnp.zeros((KT, width), F32)
            for h in range(2):
                head_rows = slice(h * HEAD_DIM, (h + 1) * HEAD_DIM)
                sc = nt(keys, v.qm[l, h])
                if masked:
                    key = lax.broadcasted_iota(jnp.int32, sc.shape, 0) + i * KT
                    query = lax.broadcasted_iota(jnp.int32, sc.shape, 1)
                    sc = jnp.where(key <= query, sc, -1e30)
                p = jnp.exp(sc - v.lse[l, h : h + 1, :])
                dp = nt(values, v.dom[h])
                ds = (p * (dp - v.delta[h : h + 1, :])).astype(BF16)
                dv = dv + nn(p.astype(BF16), v.dom[h])
                dk = dk + nn(ds, v.qm[l, h])
                v.dqt[head_rows, :] += nn(v.kt[l, b, head_rows, at], ds)
            return dk, dv

        def far(b, slot, received):
            for i in range(rows // KT):
                dk, dv = piece(b, i, False)
                at = slice(i * KT, (i + 1) * KT)
                if received:
                    dkv_copy(l, 0, i).wait_recv()
                    dk = dk + v.dkvi[l, 0, at, :width].astype(F32)
                    dv = dv + v.dkvi[l, 0, at, width:].astype(F32)
                v.dkvo[l, slot, at, :width] = dk.astype(BF16)
                v.dkvo[l, slot, at, width:] = dv.astype(BF16)
                dkv_copy(l, slot, i).start()

        @pl.when(zlo == 1)
        def _():
            far(1 - core, 0, False)
            first()
            far(core, 1, True)

        @pl.when(core == 1)
        def _():
            far(rank - 1, 2, False)

        @pl.when(rank == group - 1)
        def _():
            second()

        for i in range(rows // KT):
            dk, dv = piece(rank, i, True)
            at = slice(i * KT, (i + 1) * KT)
            v.own[at, :width] = dk
            v.own[at, width:] = dv

    def do_rows(l, at):
        do = nt(v.dz[at, :], v.wout[l]).astype(BF16)
        v.do[at, :] = do
        v.dom[0, at, :] = head_only(do, 0)
        v.dom[1, at, :] = head_only(do, 1)

    def dact_rows(l, at):
        v.dact[at, :] = nt(v.dz[at, :], v.wdown[l])

    def back_rows(l, at, size):
        def slope(i, acc):
            now = pl.ds(pl.multiple_of(at.start + i * ST, ST), ST)
            du = (v.dact[now, :] * v.u[l, now, :]).astype(BF16)
            v.du[now, :] = du
            return acc + jnp.sum(du.astype(F32).reshape(ST // 8, 8, ff), axis=0)

        v.binacc[l] += lax.fori_loop(0, size // ST, slope, jnp.zeros((8, ff), F32))
        v.dh1[at, :] = nt(v.du[at, :], v.win[l])

    def early_grads(l):
        def one(i, carry):
            at = rows_at(i, 2 * grow)
            dzt = v.dz[:, at].astype(F32).T.astype(BF16)
            ht = v.h1[l, :, at].astype(F32).T.astype(BF16)
            wo = nn(dzt, v.ob[l]).astype(BF16)
            wd = nn(dzt, v.act[l]).astype(BF16)
            wi = nn(ht, v.du[...]).astype(BF16)
            for c in range(2):
                part = slice(c * grow, (c + 1) * grow)
                v.ge[l, c, i, :, :width] = wo[part]
                v.ge[l, c, i, :, width : width + ff] = wd[part]
                v.ge[l, c, i, :, width + ff :] = wi[part]
            return carry

        lax.fori_loop(0, depth // (2 * grow), one, 0)

    def late_grads(l):
        def one(i, carry):
            at = rows_at(i, 2 * grow)
            ht = v.h0[l, :, at].astype(F32).T.astype(BF16)
            wq = nn(ht, v.dqkv[...]).astype(BF16)
            for c in range(2):
                v.gl[l, c, i] = wq[c * grow : (c + 1) * grow]
            return carry

        lax.fori_loop(0, depth // (2 * grow), one, 0)

    def qkv_back(l):
        @pl.when(zlo == 0)
        def _():
            grad_x(l, 0)

        for step, here in ((2, core == 0), (1, zlo == 0)):

            @pl.when(here)
            def _():
                for i in range(rows // KT):
                    dkv_copy(l, step, i).wait_recv()
                v.own[...] += v.dkvi[l, step].astype(F32)

        cosine, sine = v.cosine[...], -v.sine[...]
        v.dqkv[:, :width] = rotate(v.dqt[...].T * 0.125, cosine, sine).astype(BF16)
        v.dqkv[:, width : 2 * width] = rotate(v.own[:, :width], cosine, sine).astype(BF16)
        v.dqkv[:, 2 * width : 3 * width] = v.own[:, width:].astype(BF16)
        v.other[4 * l + 3 : 4 * l + 4, : 3 * width] = jnp.sum(
            v.dqkv[...].astype(F32), axis=0, keepdims=True
        )

        def one(i, carry):
            at = rows_at(i, MT)
            v.dh0[at, :] = nt(v.dqkv[at, :], v.wqkv[l])
            return carry

        lax.fori_loop(0, rows // MT, one, 0)

        def send(m, carry):
            pair = at_y(m)
            for i in range(2 * chunk // ST):
                at = pl.ds(pl.multiple_of(pair * 2 * chunk + i * ST, ST), ST)
                both = v.dh0[at, :] * v.gain[l, 0:1, :] + v.dh1[at, :] * v.gain[l, 1:2, :]
                both = both.astype(BF16)
                part = slice(i * ST % chunk, i * ST % chunk + ST)
                for half in range(2):
                    v.psend[0, half, 2 * pair + i * ST // chunk, part, :] = both[
                        :, half * hd : (half + 1) * hd
                    ]
            rs_pair(0, m)
            return carry

        lax.fori_loop(1, ny + 1, send, 0)

    def norm_grads(l):
        v.lnacc[...] = jnp.zeros_like(v.lnacc)

        def fold(value):
            return jnp.sum(value.reshape(2, 8, depth), axis=0)

        def one(i, carry):
            at = rows_at(i, 16)
            xhat = (stream_rows(l, at) - v.mu[l, at, :]) * v.rs[l, at, :]
            first, second = v.dh0[at, :], v.dh1[at, :]
            v.lnacc[0] += fold(first * xhat)
            v.lnacc[1] += fold(second * xhat)
            v.lnacc[2] += fold(first)
            v.lnacc[3] += fold(second)
            v.lnacc[4] += fold(v.dz[at, :].astype(F32))
            return carry

        lax.fori_loop(0, rows // 16, one, 0)
        for i in range(4):
            v.ln[4 * l + i : 4 * l + i + 1, :] = jnp.sum(v.lnacc[i], axis=0, keepdims=True)
        column = jnp.sum(v.lnacc[4], axis=0, keepdims=True)
        v.other[4 * l : 4 * l + 1, :] = column[:, :ff]
        v.other[4 * l + 1 : 4 * l + 2, :] = column[:, ff:]
        v.other[4 * l + 2 : 4 * l + 3, :] = jnp.sum(v.binacc[l], axis=0, keepdims=True)

    def stream_reduce(l):
        rs_finish(0)
        for i in range(chunk // 16):
            at = pl.ds(pl.multiple_of(me_t * chunk + i * 16, 16), 16)
            gd = rs_sum(0, slice(i * 16, (i + 1) * 16))
            r = v.rs[l, at, :]
            xhat = (stream_rows(l, at) - v.mu[l, at, :]) * r
            mean = jnp.mean(gd, axis=-1, keepdims=True)
            along = jnp.mean(gd * xhat, axis=-1, keepdims=True)
            dx = r * (gd - mean - xhat * along)
            ag_put(0, slice(i * 16, (i + 1) * 16), dx)
        ag_start(0)

    def small_core(i):
        mine, theirs = [(v.ln, v.ln1), (v.other, v.other1)][i]
        return remote(mine, theirs, v.s1s.at[i], v.s1r.at[i], dp=other_core)

    def small_dp(k, i):
        to = lax.rem(me_d + 2 * k, nd)
        mine, theirs = [(v.lnsum, v.ln3), (v.other, v.other2)][i]
        return remote(mine, theirs.at[k - 1], v.s3s.at[i, k - 1], v.s3r.at[i, k - 1], dp=to)

    def small_scatter(k):
        to = lax.rem(me_t + k, nt_dev)
        columns = pl.ds(pl.multiple_of(to * LANES, LANES), LANES)
        return remote(
            v.ln.at[:, columns], v.ln2.at[k - 1], v.s2s.at[k - 1], v.s2r.at[k - 1], tensor=to
        )

    def small_gather(k):
        to = lax.rem(me_t + k, nt_dev)
        block = v.lnall.at[me_t]
        return remote(block, block, v.s4s.at[k - 1], v.s4r.at[me_t], tensor=to)

    def small_start():
        for i in range(2):
            small_core(i).start()

    def small_second():
        for i in range(2):
            small_core(i).wait()
        v.ln[...] += v.ln1[...]
        v.other[...] += v.other1[...]
        for k in range(1, nt_dev):
            small_scatter(k).start()
        for k in range(1, nd // 2):
            small_dp(k, 1).start()

    def small_third():
        mine = pl.ds(pl.multiple_of(me_t * LANES, LANES), LANES)
        total = v.ln[:, mine]
        for k in range(1, nt_dev):
            small_scatter(k).wait()
            total = total + v.ln2[k - 1]
        v.lnsum[...] = total
        for k in range(1, nd // 2):
            small_dp(k, 0).start()

    def small_fourth():
        total = v.lnsum[...]
        for k in range(1, nd // 2):
            small_dp(k, 0).wait()
            total = total + v.ln3[k - 1]
        v.lnall[me_t] = total
        for k in range(1, nt_dev):
            small_gather(k).start()
        total = v.other[...]
        for k in range(1, nd // 2):
            small_dp(k, 1).wait()
            total = total + v.other2[k - 1]
        for l in range(LAYERS):
            for half in range(2):
                at = slice(half * ff, (half + 1) * ff)
                row = total[4 * l + half : 4 * l + half + 1, :]
                v.obout[l : l + 1, at] = row
                v.obdown[l : l + 1, at] = row
            v.obin[l : l + 1, :] = total[4 * l + 2 : 4 * l + 3, :]
            for c in range(3):
                at = slice(c * width, (c + 1) * width)
                v.obqkv[c, l : l + 1, :] = total[4 * l + 3 : 4 * l + 4, at]

    def small_end():
        for k in range(1, nt_dev):
            src = lax.rem(me_t + k, nt_dev)
            block = v.lnall.at[src]
            remote(block, block, v.s4s.at[k - 1], v.s4r.at[src], tensor=src).wait()
        for j in range(nt_dev):
            at = slice(j * LANES, (j + 1) * LANES)
            block = v.lnall[j]
            for l in range(LAYERS):
                v.ogain[l, :, at] = block[4 * l : 4 * l + 2, :]
                v.obias[l, :, at] = block[4 * l + 2 : 4 * l + 4, :]

    def nothing(at):
        pass

    def first_norm(i, carry):
        at = rows_at(i, ST)
        norm_rows(0, at, v.xt[at, :].astype(F32))
        return carry

    with jax.named_scope("norm0"):
        for i in range(TP):
            load_tok[i].wait()
            lax.fori_loop(i * rows // TP // ST, (i + 1) * rows // TP // ST, first_norm, 0, unroll=2)
    with jax.named_scope("qkv0"):
        for c in load_qkv[0]:
            c.wait()
        load_cos.wait()
        load_sin.wait()

        def first_qkv(i, carry):
            qkv_rows(0, rows_at(i, MT), MT)
            return carry

        lax.fori_loop(0, rows // MT, first_qkv, 0)
    with jax.named_scope("barrier"):
        pl.semaphore_wait(barrier, nt_dev - 1 + nd - 1)
    kv_send(0)
    v.ln[...] = jnp.zeros_like(v.ln)
    v.other[...] = jnp.zeros_like(v.other)
    v.binacc[...] = jnp.zeros_like(v.binacc)
    with jax.named_scope("ffn0"):
        for c in load_rest[0]:
            c.wait()

        def first_ffn(i, carry):
            feed_forward(0, rows_at(i, MT), MT)
            return carry

        lax.fori_loop(0, rows // MT, first_ffn, 0)
    with jax.named_scope("near0"):
        kv_near(0)
        attention(0, 0, 0)
    def first_gradients(z):
        @pl.when(zlo == z)
        def _():
            load_cot.wait()
            for c in load_rest[1]:
                c.wait()

            def copy_rows(i, carry):
                at = rows_at(i, ST)
                v.dz[at, :] = v.ct[at, :]
                v.g[at, :] = v.ct[at, :].astype(F32)
                return carry

            def rows_back(i, carry):
                at = rows_at(i, MT)
                do_rows(1, at)
                dact_rows(1, at)
                return carry

            lax.fori_loop(0, rows // ST, copy_rows, 0)
            lax.fori_loop(0, rows // MT, rows_back, 0)

    with jax.named_scope("dz1"):
        first_gradients(1)
    with jax.named_scope("kv0"):
        kv_far(0)
    with jax.named_scope("attn0"):
        attention(0, 0, 1)
    with jax.named_scope("dz1b"):
        first_gradients(0)
    with jax.named_scope("forward0"):
        rs_forward(0)
    with jax.named_scope("reduce0"):
        branch_reduce(0)

    def next_stream(at, z):
        x = v.xt[at, :].astype(F32) + (z + (v.bout[0:1, :] + v.bdown[0:1, :]))
        v.x[at, :] = x
        norm_rows(1, at, x)

    def next_qkv(at):
        qkv_rows(1, at, 2 * chunk)

    def next_ffn(at):
        feed_forward(1, at, 2 * chunk)
        back_rows(1, at, 2 * chunk)

    def next_both(at):
        next_qkv(at)
        next_ffn(at)

    with jax.named_scope("gather0"):
        for c in load_qkv[1]:
            c.wait()
        ag_forward(0)
        ag_pairs(0, 0, ny // 2, next_stream, next_both)
        ag_pairs(0, ny // 2, ny, next_stream, next_qkv)
        kv_send(1)
        ag_sent(0)
    with jax.named_scope("ffn1"):
        for k in range(ny // 2, ny):
            next_ffn(rows_at(at_y(place(k)), 2 * chunk))
    with jax.named_scope("near1"):
        kv_near(1)
        attention(1, 1, 0)
    with jax.named_scope("kv1"):
        kv_far(1)
    with jax.named_scope("attn1"):
        attention(1, 1, 1)

    with jax.named_scope("attn_grad1"):
        attention_back(1, lambda: None, lambda: rs_forward(1))

        @pl.when(rank != group - 1)
        def _():
            rs_forward(1)


    def forward_at(z):
        @pl.when(zlo == z)
        def _():
            rs_forward(0)

    def late_x(l):
        @pl.when(zlo == 1)
        def _():
            grad_x(l, 0)

    def early(l, z):
        @pl.when(zlo == z)
        def _():
            early_grads(l)
            grad_core(l, 0)

    with jax.named_scope("early1"):
        early(1, 0)
    with jax.named_scope("qkv_grad1"):
        qkv_back(1)
    with jax.named_scope("early1b"):
        early(1, 1)
    with jax.named_scope("norm_grad1"):
        norm_grads(1)
    with jax.named_scope("forward"):
        forward_at(1)
    with jax.named_scope("gx10"):
        late_x(1)
    with jax.named_scope("late1"):
        late_grads(1)
        grad_core(1, 1)
    with jax.named_scope("forward"):
        forward_at(0)
    with jax.named_scope("gx11"):
        grad_x(1, 1)
    with jax.named_scope("stream_reduce1"):
        stream_reduce(1)

    def next_gradient(at, dx):
        gradient = v.g[at, :] + dx
        v.g[at, :] = gradient
        v.dz[at, :] = gradient.astype(BF16)

    def next_do(at):
        do_rows(0, at)

    def next_slope(at):
        dact_rows(0, at)
        back_rows(0, at, 2 * chunk)

    def next_back(at):
        next_do(at)
        next_slope(at)

    with jax.named_scope("gather2"):
        ag_forward(0)
        ag_pairs(0, 0, ny // 2, next_gradient, next_back)
    with jax.named_scope("reduce1"):
        branch_reduce(1)
    with jax.named_scope("gather2b"):
        ag_pairs(0, ny // 2, ny, next_gradient, next_do)
        ag_sent(0)
    with jax.named_scope("attn_grad0"):
        attention_back(0, lambda: ag_forward(1), lambda: None)
    with jax.named_scope("slope0"):
        for k in range(ny // 2, ny):
            next_slope(rows_at(at_y(place(k)), 2 * chunk))
    with jax.named_scope("forward1b"):

        @pl.when(zlo == 0)
        def _():
            ag_forward(1)

    with jax.named_scope("early0"):
        early(0, 0)
    with jax.named_scope("qkv_grad0"):
        qkv_back(0)
    with jax.named_scope("early0b"):
        early(0, 1)
    with jax.named_scope("norm_grad0"):
        norm_grads(0)
        small_start()
    with jax.named_scope("gx00"):
        late_x(0)
    with jax.named_scope("small_second"):
        small_second()
    with jax.named_scope("forward"):
        forward_at(1)
    with jax.named_scope("late0"):
        late_grads(0)
        grad_core(0, 1)
    with jax.named_scope("forward"):
        forward_at(0)
    with jax.named_scope("small_third"):
        small_third()
    with jax.named_scope("gx01"):
        grad_x(0, 1)

    def last_stream(at, z):
        v.x[at, :] = v.x[at, :] + (z + (v.bout[1:2, :] + v.bdown[1:2, :]))

    store_x = pltpu.make_async_copy(v.x, v.ox, v.lsem.at[0])
    store_g = pltpu.make_async_copy(v.g, v.og, v.lsem.at[1])
    with jax.named_scope("stream_reduce0"):
        stream_reduce(0)
    with jax.named_scope("forward0c"):
        ag_forward(0)
    with jax.named_scope("gz1"):
        grad_z(1, 0)
        grad_z(1, 1)
    with jax.named_scope("gather1"):
        ag_pairs(1, 0, ny, last_stream, nothing)
        ag_sent(1)
        store_x.start()

    def last_gradient(at, dx):
        v.g[at, :] = v.g[at, :] + dx

    with jax.named_scope("gather3"):
        ag_pairs(0, 0, ny // 2, last_gradient, nothing)
    with jax.named_scope("small_fourth"):
        small_fourth()
    with jax.named_scope("gz00"):
        grad_z(0, 0)
    with jax.named_scope("gather3a"):
        ag_pairs(0, ny // 2, ny - 1, last_gradient, nothing)
    with jax.named_scope("gz01"):
        grad_z(0, 1)
    with jax.named_scope("gather3b"):
        ag_pairs(0, ny - 1, ny, last_gradient, nothing)
        store_g.start()
        ag_sent(0)
    with jax.named_scope("gend1"):
        grad_end(1, 0)
        grad_end(1, 1)
    with jax.named_scope("small_end"):
        small_end()
    with jax.named_scope("gend0"):
        grad_end(0, 0)
        grad_end(0, 1)
        store_x.wait()
        store_g.wait()
    for l in range(LAYERS):
        for step, here in ((0, core == 0), (1, zlo == 0), (2, zlo == 1)):

            @pl.when(here)
            def _():
                kv_copy(l, step).wait_send()

        for step, here in ((0, zlo == 1), (1, zlo == 1), (2, core == 1)):

            @pl.when(here)
            def _():
                for i in range(rows // KT):
                    dkv_copy(l, step, i).wait_send()


def store_kernel(count, *refs):
    given, kept = refs[:count], refs[count:]
    for i in range(2):
        kept[i][...] = given[i][...]

    @pl.when(pl.program_id(0) == 0)
    def _():
        for i in range(2, count):
            kept[i][...] = given[i][...]


def on_device(nt_dev, nd, *args):
    tokens, cotangent, ln_gain, ln_bias, w_qkv, b_qkv, w_out, b_out, w_in, b_in, w_down, b_down = args
    rows, depth = tokens.shape
    width = w_out.shape[1]
    ff = w_in.shape[2]
    group = SEQ // rows
    chunk = rows // nt_dev
    grow = depth // nd
    half = nd // 2
    nx = nd // group
    early = width + 2 * ff
    late = 3 * width
    cosine, sine = rope_constants()
    vm = pltpu.VMEM
    dma = pltpu.SemaphoreType.DMA
    two = LAYERS
    scratch = [
        vm((two, depth, 3 * width), BF16),
        vm((two, width, depth), BF16),
        vm((two, depth, ff), BF16),
        vm((two, ff, depth), BF16),
        vm((rows, LANES), F32),
        vm((rows, LANES), F32),
        vm((rows, depth), F32),
        vm((rows, depth), F32),
        vm((rows, depth), BF16),
        vm((rows, depth), BF16),
        vm((two, rows, depth), BF16),
        vm((two, rows, depth), BF16),
        vm((two, 2, rows, width), BF16),
        vm((two, group, rows, 2 * width), BF16),
        vm((two, group, width, rows), BF16),
        vm((two, group, width, rows), BF16),
        vm((two, rows, width), BF16),
        vm((two, width, rows), F32),
        vm((8, rows), F32),
        vm((two, 8, rows), F32),
        vm((two, rows, ff), F32),
        vm((two, rows, ff), BF16),
        vm((two, rows, 1), F32),
        vm((two, rows, 1), F32),
        vm((rows, depth), F32),
        vm((2, 2, nt_dev, chunk, depth // 2), BF16),
        vm((2, nt_dev // 2 - 1, 2, chunk, depth // 2), BF16),
        vm((2, nt_dev // 2, chunk, depth // 2), BF16),
        vm((2, chunk, depth // 2), BF16),
        vm((2, nt_dev // 2 - 1, chunk, depth // 2), BF16),
        vm((2, chunk, depth // 2), BF16),
        vm((2, nt_dev // 2 - 1, chunk, depth // 2), BF16),
        vm((2, 2, nt_dev, chunk, depth // 2), BF16),
        vm((rows, depth), BF16),
        vm((rows, width), BF16),
        vm((2, rows, width), BF16),
        vm((8, rows), F32),
        vm((width, rows), F32),
        vm((two, 3, rows, 2 * width), BF16),
        vm((two, 3, rows, 2 * width), BF16),
        vm((rows, 2 * width), F32),
        vm((rows, 3 * width), BF16),
        vm((rows, ff), BF16),
        vm((rows, ff), F32),
        vm((two, 8, ff), F32),
        vm((rows, depth), F32),
        vm((rows, depth), F32),
        vm((two, 2, half, grow, early), BF16),
        vm((two, 2, half, grow, late), BF16),
        vm((two, half, grow, early), BF16),
        vm((two, half, grow, late), BF16),
        vm((two, nx - 1, 2, grow, early), BF16),
        vm((two, nx - 1, 2, grow, late), BF16),
        vm((two, grow, early), BF16),
        vm((two, grow, late), BF16),
        vm((two, grow, early), BF16),
        vm((two, grow, late), BF16),
        vm((two, grow, early), F32),
        vm((two, grow, late), F32),
        vm((8, depth), F32),
        vm((8, ff), F32),
        vm((8, depth), F32),
        vm((8, ff), F32),
        vm((nt_dev - 1, 8, LANES), F32),
        vm((half - 1, 8, ff), F32),
        vm((8, LANES), F32),
        vm((half - 1, 8, LANES), F32),
        vm((nt_dev, 8, LANES), F32),
        vm((5, 8, depth), F32),
        dma((16 + TP,)),
        dma((two, 3)),
        dma((two, 3)),
        dma((two, 3, rows // KT)),
        dma((two, 3, rows // KT)),
        dma((2, 7 * (nt_dev // 2) - 3)),
        dma((2, 7 * (nt_dev // 2) - 3)),
        dma((two, 2)),
        dma((two, 2)),
        dma((two, 2, nx - 1)),
        dma((two, 2, nx - 1)),
        dma((two, 2)),
        dma((two, 2)),
        dma((2,)),
        dma((2,)),
        dma((nt_dev - 1,)),
        dma((nt_dev - 1,)),
        dma((2, half - 1)),
        dma((2, half - 1)),
        dma((nt_dev - 1,)),
        dma((nt_dev,)),
    ]
    here = pl.BlockSpec(memory_space=pltpu.VMEM)
    away = pl.BlockSpec(memory_space=pl.ANY)
    shapes = [
        (rows, depth),
        (rows, depth),
        (two, 2, depth),
        (two, 2, depth),
        (3, two, width),
        (two, depth),
        (two, ff),
        (two, depth),
        (two, 3, grow, width),
        (two, grow, width),
        (two, grow, ff),
        (two, grow, ff),
    ]
    out = pl.pallas_call(
        functools.partial(step_kernel, nt_dev, nd),
        out_shape=[jax.ShapeDtypeStruct(s, F32) for s in shapes],
        in_specs=[away, away, here, here, away, here, away, here, away, here, away, here, away, away],
        out_specs=[away] * 2 + [here] * (len(shapes) - 2),
        scratch_shapes=scratch,
        compiler_params=pltpu.CompilerParams(
            collective_id=0, has_side_effects=True, vmem_limit_bytes=64 * 1024 * 1024 - 65536
        ),
    )(
        tokens,
        cotangent,
        ln_gain,
        ln_bias,
        w_qkv.transpose(0, 2, 1, 3),
        b_qkv.transpose(1, 0, 2),
        w_out,
        b_out,
        w_in,
        b_in,
        w_down,
        b_down,
        jnp.asarray(cosine),
        jnp.asarray(sine),
    )
    out = pl.pallas_call(
        functools.partial(store_kernel, len(shapes)),
        out_shape=[jax.ShapeDtypeStruct(s, F32) for s in shapes],
        grid=(PARTS,),
        in_specs=[pl.BlockSpec((rows // PARTS, depth), lambda i: (i, 0))] * 2
        + [here] * (len(shapes) - 2),
        out_specs=[pl.BlockSpec((rows // PARTS, depth), lambda i: (i, 0))] * 2
        + [here] * (len(shapes) - 2),
    )(*out)
    x, g, gain, bias, bqkv, bout, b_in_g, bdown, wq, wo, wi, wd = out
    return (
        x,
        g,
        gain,
        bias,
        wq.transpose(0, 2, 1, 3),
        bqkv.transpose(1, 0, 2),
        wo.transpose(0, 2, 1),
        bout,
        wi,
        b_in_g,
        wd.transpose(0, 2, 1),
        bdown,
    )


def solution(mesh):
    return jax.shard_map(
        functools.partial(on_device, mesh.shape["tensor"], mesh.shape["dp"]),
        mesh=mesh,
        in_specs=(
            P("dp", None),
            P("dp", None),
            P(),
            P(),
            P(None, None, None, "tensor"),
            P(None, None, "tensor"),
            P(None, "tensor", None),
            P(),
            P(None, None, "tensor"),
            P(None, "tensor"),
            P(None, "tensor", None),
            P(),
        ),
        out_specs=(
            P("dp", None),
            P("dp", None),
            P(),
            P(),
            P(None, "dp", None, "tensor"),
            P(None, None, "tensor"),
            P(None, "tensor", "dp"),
            P(),
            P(None, "dp", "tensor"),
            P(None, "tensor"),
            P(None, "tensor", "dp"),
            P(),
        ),
        check_vma=False,
    )
```
